32 devices in a mesh: cand: 16 (over z, y, core), img: 2 (over x).
Axes of the slice: x: 2, y: 2, z: 4, core: 2. Of those that a mesh axis runs over, the one named last changes fastest.
Arguments:
- first_maps: float32 [2, 256, 344], P('img', 'cand'), may hold values from -6 to 6
- layer_of: int32 [16], P('cand'), may hold values from 0 to 1, as said below
- expand_half: int32 [16], P('cand'), may hold values from 1 to 2
- radius: int32 [16], P('cand'), may hold values from 1 to 2
- teach_up: bfloat16 [2, 344, 2064], replicated, may hold values from -0.3125 to 0.3125
- teach_dw: float32 [2, 25, 2064], replicated, may hold values from -1.25 to 1.25
- teach_down: bfloat16 [2, 344, 2064], replicated, may hold values from -0.125 to 0.125
- cand_up: bfloat16 [16, 344, 2064], P('cand'), may hold values from -0.3125 to 0.3125
- cand_dw: float32 [16, 25, 2064], P('cand'), may hold values from -1.25 to 1.25
- cand_down: bfloat16 [16, 344, 2064], P('cand'), may hold values from -0.125 to 0.125
Outputs:
- grad_up: float32 [16, 344, 2064], P('cand', None, 'img')
- grad_dw: float32 [16, 25, 2064], P('cand', None, 'img')
- grad_down: float32 [16, 344, 2064], P('cand', None, 'img')
The draws below stay inside these ranges and needn't reach their ends.
Inputs may be any that keep to these rules, and one draw needn't show every extreme that they name: `layer_of`: both layers have at least one candidate.
All inputs are finite; a program needn't handle non-finite values.
Results may differ from the reference program's by a relative error of at most 0.014.
Values may be sent and summed in bfloat16 or wider, within the bound.
No kernel may reach another device: no remote copies, remote signals or barrier semaphores. Data moves between devices by JAX's collectives and lax.ppermute only.
A program may use at most 192 MiB of HBM per device.

```python
import jax
import jax.numpy as jnp
from jax import lax

C = 344
HID = 2064
H = 16
CELLS = 256
IMG_DEV = 1
IMAGES = 2
CANDIDATES = 16
N_IMG = 2


def draw_layer_of(key, part):
    first_key, second_key = jax.random.split(jax.random.fold_in(key, 17))
    count = jax.random.randint(first_key, (), CANDIDATES // 4, CANDIDATES - CANDIDATES // 4 + 1)
    order = jax.random.permutation(second_key, CANDIDATES)
    return (order >= count).astype(jnp.int32)


def with_ends(values, own_key, smallest, largest):
    place = [jax.random.randint(jax.random.fold_in(own_key, axis), (), 0, length) for axis, length in enumerate(values.shape)]
    main_axis = values.shape.index(max(values.shape))
    neighbour = place[:main_axis] + [(place[main_axis] + 1) % values.shape[main_axis]] + place[main_axis + 1:]
    return values.at[tuple(place)].set(smallest).at[tuple(neighbour)].set(largest)


def block_scale(rng, shape, shards, low, largest):
    loudness = 1.0
    for position, shards_of in shards:
        heights = jax.random.uniform(jax.random.fold_in(jax.random.fold_in(rng, 6), position), (shards_of,), jnp.float32, low / len(shards), largest / len(shards))
        loudness = loudness * jnp.repeat(jnp.exp(heights), shape[position] // shards_of).reshape((-1,) + (1,) * (len(shape) - 1 - position))
    return loudness


def noise(rng, shape, deviation, bound, shards=(), kind=jnp.bfloat16):
    values = deviation * jax.random.normal(rng, shape, jnp.float32)
    if shards:
        values = values * block_scale(rng, shape, shards, -0.22, 0.18)
    return jnp.clip(values, -bound, bound).astype(kind)


def setup_inputs(seed: int = 0) -> dict:
    keys = jax.random.split(jax.random.key(seed), 11)
    return {
        "first_maps": noise(keys[0], (IMAGES, CELLS, C), 1.0, 6.0, ((0, 2), (1, 16)), jnp.float32),
        "layer_of": draw_layer_of(jax.random.fold_in(keys[10], 71), 0),
        "expand_half": with_ends(jax.random.randint(keys[2], (CANDIDATES,), 1, 3), jax.random.fold_in(keys[2], 1), 1, 2).astype(jnp.int32),
        "radius": with_ends(jax.random.randint(keys[3], (CANDIDATES,), 1, 3), jax.random.fold_in(keys[3], 1), 1, 2).astype(jnp.int32),
        "teach_up": noise(keys[4], (2, C, HID), C ** -0.5, 0.3125),
        "teach_dw": noise(keys[5], (2, 25, HID), 25 ** -0.5, 1.25, (), jnp.float32),
        "teach_down": noise(keys[6], (2, C, HID), HID ** -0.5, 0.125),
        "cand_up": noise(keys[7], (CANDIDATES, C, HID), C ** -0.5, 0.3125, ((0, 16),)),
        "cand_dw": noise(keys[8], (CANDIDATES, 25, HID), 25 ** -0.5, 1.25, ((0, 16),), jnp.float32),
        "cand_down": noise(keys[9], (CANDIDATES, C, HID), HID ** -0.5, 0.125, ((0, 16),)),
    }


def apply_block(map_in, w_up, w_dw, w_down, unit_mask, tap_mask):
    batch_size = map_in.shape[0]
    flat_rows = map_in.reshape(-1, map_in.shape[2]).astype(jnp.bfloat16)
    preact = jnp.dot(flat_rows, w_up, preferred_element_type=jnp.float32)
    expanded = jax.nn.silu(preact) * unit_mask
    grid_maps = expanded.reshape(batch_size, H, H, expanded.shape[1])
    padded = jnp.pad(grid_maps, ((0, 0), (2, 2), (2, 2), (0, 0)))
    tap_weights = w_dw * tap_mask[:, None]
    accumulated = jnp.zeros_like(grid_maps)
    for tap_row in range(5):
        for tap_col in range(5):
            accumulated = accumulated + tap_weights[tap_row * 5 + tap_col] * padded[:, tap_row:tap_row + H, tap_col:tap_col + H, :]
    activated = jax.nn.silu(accumulated).reshape(-1, grid_maps.shape[3]).astype(jnp.bfloat16)
    branch = lax.dot_general(activated, w_down, (((1,), (1,)), ((), ())), preferred_element_type=jnp.float32)
    return map_in + branch.reshape(map_in.shape)

def make_masks(half_count, kernel_radius):
    unit_index = lax.broadcasted_iota(jnp.int32, (HID,), 0)
    unit_mask = (unit_index < half_count * (HID // 2)).astype(jnp.float32)
    tap_index = lax.broadcasted_iota(jnp.int32, (25,), 0)
    shift_row = tap_index // 5 - 2
    shift_col = tap_index % 5 - 2
    tap_mask = (jnp.maximum(jnp.abs(shift_row), jnp.abs(shift_col)) <= kernel_radius).astype(jnp.float32)
    return (unit_mask, tap_mask)

def candidate_grads(inputs, target, w_up, w_dw, w_down, unit_mask, tap_mask, images):

    def squared_loss(up_wide, depth_weights, down_wide):
        result = apply_block(inputs, up_wide.astype(jnp.bfloat16), depth_weights, down_wide.astype(jnp.bfloat16), unit_mask, tap_mask)
        error_map = result - target
        return 0.5 * jnp.sum(error_map * error_map) / images
    return jax.grad(squared_loss, argnums=(0, 1, 2))(w_up.astype(jnp.float32), w_dw, w_down.astype(jnp.float32))

def reference(first_maps, layer_of, expand_half, radius, teach_up, teach_dw, teach_down, cand_up, cand_dw, cand_down):
    full_units = jnp.ones((HID,), jnp.float32)
    all_taps = jnp.ones((25,), jnp.float32)
    maps_one = apply_block(first_maps, teach_up[0], teach_dw[0], teach_down[0], full_units, all_taps)
    maps_two = apply_block(maps_one, teach_up[1], teach_dw[1], teach_down[1], full_units, all_taps)

    def one_candidate(cand_index):
        layer_here = layer_of[cand_index]
        inputs = jnp.where(layer_here == 0, first_maps, maps_one)
        target = jnp.where(layer_here == 0, maps_one, maps_two)
        unit_mask, tap_mask = make_masks(expand_half[cand_index], radius[cand_index])

        def one_shard(running, shard_index):
            start = (shard_index * IMG_DEV).astype(jnp.int32)
            part_in = lax.dynamic_slice_in_dim(inputs, start, IMG_DEV, 0)
            part_target = lax.dynamic_slice_in_dim(target, start, IMG_DEV, 0)
            gradients = candidate_grads(part_in, part_target, cand_up[cand_index], cand_dw[cand_index], cand_down[cand_index], unit_mask, tap_mask, IMAGES)
            rounded = tuple((lax.optimization_barrier(piece.astype(jnp.bfloat16)).astype(jnp.float32) for piece in gradients))
            return (tuple((acc + piece for acc, piece in zip(running, rounded))), 0)
        zero_grads = (jnp.zeros((C, HID), jnp.float32), jnp.zeros((25, HID), jnp.float32), jnp.zeros((C, HID), jnp.float32))
        totals, unused = lax.scan(one_shard, zero_grads, jnp.arange(N_IMG, dtype=jnp.int32))
        return totals
    grad_up, grad_dw, grad_down = lax.map(one_candidate, jnp.arange(CANDIDATES, dtype=jnp.int32))
    return (grad_up, grad_dw, grad_down)
```

```python
import functools

import jax
import jax.numpy as jnp
import ml_dtypes
import numpy as np
from jax import lax
from jax.experimental import pallas as pl
from jax.experimental.pallas import tpu as pltpu
from jax.sharding import PartitionSpec as P

F32 = jnp.float32
BF16 = jnp.bfloat16
LANES = 128
TILE = 256


def round_up(value, step):
    return -(-value // step) * step


def dft_matrices(side, taps):
    width = int(round(taps**0.5))
    reach = width // 2
    period = side + reach
    kept = []
    for u in range(period):
        for v in range(period):
            if (u, v) <= ((-u) % period, (-v) % period):
                kept.append((u, v))
    freqs = np.array(kept)
    count = len(kept)
    rows = round_up(count, 8)
    mirrored = ((-freqs) % period == freqs).all(axis=1)
    weight = np.where(mirrored, 1.0, 2.0) / period**2
    cell = np.stack(np.meshgrid(np.arange(side), np.arange(side), indexing="ij"), -1).reshape(-1, 2)
    tap = np.stack(np.meshgrid(np.arange(width), np.arange(width), indexing="ij"), -1).reshape(-1, 2) - reach
    cell_angle = 2 * np.pi * ((freqs @ cell.T) % period) / period
    tap_angle = 2 * np.pi * ((freqs @ tap.T) % period) / period
    tap_rows = round_up(taps, 16)

    analysis = np.zeros((2 * rows, side * side))
    analysis[:count] = np.cos(cell_angle)
    analysis[rows : rows + count] = -np.sin(cell_angle)
    synthesis = np.zeros((side * side, 2 * rows))
    synthesis[:, :count] = (weight[:, None] * np.cos(cell_angle)).T
    synthesis[:, rows : rows + count] = -(weight[:, None] * np.sin(cell_angle)).T
    spectrum = np.zeros((2 * rows, tap_rows))
    spectrum[:count, :taps] = np.cos(tap_angle)
    spectrum[rows : rows + count, :taps] = np.sin(tap_angle)
    gather = np.zeros((tap_rows, 2 * rows))
    gather[:taps, :count] = (weight[:, None] * np.cos(tap_angle)).T
    gather[:taps, rows : rows + count] = -(weight[:, None] * np.sin(tap_angle)).T

    coarse = spectrum.astype(ml_dtypes.bfloat16).astype(np.float64)
    fine = spectrum - coarse
    spectrum = np.concatenate([coarse, coarse, fine], axis=1)
    return rows, [jnp.asarray(m.astype(ml_dtypes.bfloat16)) for m in (analysis, synthesis, spectrum, gather)]


def dot(a, b):
    return jnp.dot(a, b, preferred_element_type=F32)


def dot_nt(a, b):
    return lax.dot_general(a, b, (((1,), (1,)), ((), ())), preferred_element_type=F32)


def grads_kernel(
    dims,
    layer_ref,
    half_ref,
    radius_ref,
    part_ref,
    x_ref,
    analysis_ref,
    synthesis_ref,
    spectrum_ref,
    gather_ref,
    teach_up,
    teach_dw,
    teach_down,
    cand_up,
    cand_dw,
    cand_down,
    grad_up,
    grad_dw,
    grad_down,
    up_buf,
    dw_buf,
    down_buf,
    up_tail,
    dw_pad,
    down_pad,
    act,
    spec,
    slope_e,
    slope_k,
    x_now,
    x_turned,
    err_now,
    err_turned,
    target,
    wide_up,
    wide_dw,
    wide_down,
    sems,
):
    maps, cells, channels, hid, taps, rows, parts, scale = dims
    main = hid // TILE * TILE
    tail = hid - main
    padded = round_up(hid, LANES)
    own = hid // parts
    window = wide_up.shape[1]

    def copies(slot):
        if slot < 2:
            sources = (teach_up.at[slot], teach_dw.at[slot], teach_down.at[slot])
        else:
            sources = (cand_up.at[0], cand_dw.at[0], cand_down.at[0])
        targets = (up_buf.at[slot], dw_buf.at[slot], down_buf.at[slot])
        return [
            pltpu.make_async_copy(src, dst, sems.at[slot, n])
            for n, (src, dst) in enumerate(zip(sources, targets))
        ]

    for slot in (0, 2):
        for copy in copies(slot):
            copy.start()

    @pl.when(layer_ref[0] != 0)
    def _():
        for copy in copies(1):
            copy.start()

    analysis = analysis_ref[...]
    synthesis = synthesis_ref[...]
    spectrum = spectrum_ref[...]
    dw_pad[...] = jnp.zeros_like(dw_pad)
    up_tail[...] = jnp.zeros_like(up_tail)
    down_pad[:, main:] = jnp.zeros((channels, padded - main), BF16)

    def tap_spectrum(cols):
        weights = dw_pad[:, cols]
        high = weights.astype(BF16)
        low = (weights - high.astype(F32)).astype(BF16)
        both = dot(spectrum, jnp.concatenate([high, low, high], axis=0))
        return both[:rows], both[rows:]

    def load(slot, mask_taps):
        for copy in copies(slot):
            copy.wait()
        weights = dw_buf[slot]
        if mask_taps:
            side = int(round(taps**0.5))
            index = lax.broadcasted_iota(jnp.int32, weights.shape, 0)
            row = sum((index >= side * n).astype(jnp.int32) for n in range(1, side))
            ring = jnp.maximum(jnp.abs(row - side // 2), jnp.abs(index - side * row - side // 2))
            unit = lax.broadcasted_iota(jnp.int32, weights.shape, 1)
            keep = (ring <= radius_ref[0]) & (unit < half_ref[0] * (hid // 2))
            weights = jnp.where(keep, weights, 0.0)
        dw_pad[:taps, :hid] = weights
        if tail:
            up_tail[:, :tail] = up_buf[slot, :, main:]
            down_pad[:, main:hid] = down_buf[slot, :, main:]

    def forward(slot, keep):
        def tile(cols, weights_up):
            pre = dot(x_now[...], weights_up)
            half = 0.5 * pre
            bend = jnp.tanh(half)
            units = (half + half * bend).astype(BF16)
            if keep:
                slope_e[:, cols] = 0.5 * ((1.0 + bend) + half * (1.0 - bend * bend))
            tap_re, tap_im = tap_spectrum(cols)
            for m in range(maps):
                here = slice(m * cells, (m + 1) * cells)
                both = dot(analysis, units[here])
                re, im = both[:rows], both[rows:]
                if keep:
                    spec[m, :, cols] = both
                mixed = jnp.concatenate([re * tap_re - im * tap_im, re * tap_im + im * tap_re], axis=0)
                mixed = dot(synthesis, mixed.astype(BF16))
                half_k = 0.5 * mixed
                bend_k = jnp.tanh(half_k)
                act[here, cols] = (half_k + half_k * bend_k).astype(BF16)
                if keep:
                    slope_k[here, cols] = 0.5 * ((1.0 + bend_k) + half_k * (1.0 - bend_k * bend_k))

        def step(n, _):
            cols = pl.ds(pl.multiple_of(n * TILE, TILE), TILE)
            tile(cols, up_buf[slot, :, cols])
            return 0

        lax.fori_loop(0, main // TILE, step, 0)
        if tail:
            tile(pl.ds(main, padded - main), up_tail[...])
        out = dot_nt(act[:, :main], down_buf[slot, :, :main])
        if tail:
            out += dot_nt(act[:, main:], down_pad[:, main:])
        return out

    x_now[...] = x_ref[...]
    load(0, False)
    target[...] = forward(0, False)

    @pl.when(layer_ref[0] != 0)
    def _():
        x_now[...] = (x_ref[...].astype(F32) + target[...]).astype(BF16)
        load(1, False)
        target[...] = forward(1, False)

    load(2, True)
    down_pad[:, :main] = down_buf[2, :, :main]
    err = (forward(2, True) - target[...]) * scale
    err_now[...] = err.astype(BF16)
    err_turned[...] = jnp.transpose(err).astype(BF16)
    x_turned[...] = jnp.transpose(x_now[...].astype(F32)).astype(BF16)

    start = part_ref[0] * own
    base = jnp.minimum(start // LANES * LANES, padded - window)

    def back(at, width):
        cols = pl.ds(pl.multiple_of(base + at, LANES), width)
        here = pl.ds(pl.multiple_of(at, LANES), width)
        grad_act = dot(err_now[...], down_pad[:, cols])
        grad_k = (grad_act * slope_k[:, cols]).astype(BF16)
        tap_re, tap_im = tap_spectrum(cols)
        sum_re = jnp.zeros((rows, width), F32)
        sum_im = jnp.zeros((rows, width), F32)
        grad_pre = []
        for m in range(maps):
            rows_here = slice(m * cells, (m + 1) * cells)
            both = dot(analysis, grad_k[rows_here])
            re, im = both[:rows], both[rows:]
            e_re, e_im = spec[m, :rows, cols], spec[m, rows:, cols]
            sum_re += re * e_re + im * e_im
            sum_im += re * e_im - im * e_re
            mixed = jnp.concatenate([re * tap_re + im * tap_im, im * tap_re - re * tap_im], axis=0)
            grad_e = dot(synthesis, mixed.astype(BF16))
            grad_pre.append((grad_e * slope_e[rows_here, cols]).astype(BF16))
        wide_up[:, here] = dot(x_turned[...], jnp.concatenate(grad_pre, axis=0))
        wide_down[:, here] = dot(err_turned[...], act[:, cols])
        sums = jnp.concatenate([sum_re, sum_im], axis=0).astype(BF16)
        wide_dw[:, here] = dot(gather_ref[...], sums)

    def back_step(n, _):
        back(n * TILE, TILE)
        return 0

    lax.fori_loop(0, window // TILE, back_step, 0)
    if window % TILE:
        back(window // TILE * TILE, window % TILE)

    offset = start - base
    turn = lax.rem(window - offset, window)
    grad_up[0] = pltpu.roll(wide_up[...], turn, 1)[:, :own]
    grad_down[0] = pltpu.roll(wide_down[...], turn, 1)[:, :own]
    rolled = pltpu.roll(wide_dw[...], turn, 1)[:taps, :own]
    side = int(round(taps**0.5))
    index = lax.broadcasted_iota(jnp.int32, rolled.shape, 0)
    row = sum((index >= side * n).astype(jnp.int32) for n in range(1, side))
    ring = jnp.maximum(jnp.abs(row - side // 2), jnp.abs(index - side * row - side // 2))
    unit = lax.broadcasted_iota(jnp.int32, rolled.shape, 1) + start
    keep = (ring <= radius_ref[0]) & (unit < half_ref[0] * (hid // 2))
    grad_dw[0] = jnp.where(keep, rolled, 0.0)


def local_grads(maps_in, layer, half, radius, part, parts, images, weights):
    maps, cells, channels = maps_in.shape
    taps, hid = weights[1].shape[1:]
    side = int(round(cells**0.5))
    rows, constants = dft_matrices(side, taps)
    padded = round_up(hid, LANES)
    own = hid // parts
    spare = max((p * own) % LANES for p in range(parts))
    window = min(round_up(own + spare, LANES), padded)
    count = maps * cells
    tap_rows = round_up(taps, 16)
    main = hid // TILE * TILE
    dims = (maps, cells, channels, hid, taps, rows, parts, 1.0 / images)
    smem = pl.BlockSpec(memory_space=pltpu.SMEM)
    vmem = pl.BlockSpec(memory_space=pltpu.VMEM)
    anywhere = pl.BlockSpec(memory_space=pl.ANY)
    return pl.pallas_call(
        functools.partial(grads_kernel, dims),
        out_shape=(
            jax.ShapeDtypeStruct((1, channels, own), F32),
            jax.ShapeDtypeStruct((1, taps, own), F32),
            jax.ShapeDtypeStruct((1, channels, own), F32),
        ),
        in_specs=[smem] * 4 + [vmem] * 5 + [anywhere] * 6,
        out_specs=(vmem, vmem, vmem),
        scratch_shapes=[
            pltpu.VMEM((3, channels, hid), BF16),
            pltpu.VMEM((3, taps, hid), F32),
            pltpu.VMEM((3, channels, hid), BF16),
            pltpu.VMEM((channels, max(padded - main, LANES)), BF16),
            pltpu.VMEM((tap_rows, padded), F32),
            pltpu.VMEM((channels, padded), BF16),
            pltpu.VMEM((count, padded), BF16),
            pltpu.VMEM((maps, 2 * rows, padded), F32),
            pltpu.VMEM((count, padded), F32),
            pltpu.VMEM((count, padded), F32),
            pltpu.VMEM((count, channels), BF16),
            pltpu.VMEM((channels, count), BF16),
            pltpu.VMEM((count, channels), BF16),
            pltpu.VMEM((channels, count), BF16),
            pltpu.VMEM((count, channels), F32),
            pltpu.VMEM((channels, window), F32),
            pltpu.VMEM((tap_rows, window), F32),
            pltpu.VMEM((channels, window), F32),
            pltpu.SemaphoreType.DMA((3, 3)),
        ],
        compiler_params=pltpu.CompilerParams(vmem_limit_bytes=60 * 2**20),
        cost_estimate=pl.CostEstimate(
            flops=20 * count * channels * hid, bytes_accessed=12 * channels * hid, transcendentals=6 * count * hid
        ),
    )(layer, half, radius, part, maps_in.reshape(count, channels), *constants, *weights)


def body(
    first_maps,
    layer_of,
    expand_half,
    radius,
    teach_up,
    teach_dw,
    teach_down,
    cand_up,
    cand_dw,
    cand_down,
):
    parts = lax.axis_size("img")
    part = lax.axis_index("img").reshape(1)
    whole = lax.all_gather(first_maps.astype(BF16), ("img", "cand"))
    batch, own_cells, channels = first_maps.shape
    whole = whole.reshape(parts, lax.axis_size("cand"), batch, own_cells, channels)
    whole = whole.transpose(0, 2, 1, 3, 4).reshape(parts * batch, -1, channels)
    images = whole.shape[0]
    weights = (teach_up, teach_dw, teach_down, cand_up, cand_dw, cand_down)
    group = 2 if images % 2 == 0 else 1
    total = None
    for first in range(0, images, group):
        grads = local_grads(
            whole[first : first + group], layer_of, expand_half, radius, part, parts, images, weights
        )
        total = grads if total is None else tuple(a + b for a, b in zip(total, grads))
    return total


def solution(mesh):
    placed = (
        P("img", "cand", None),
        P("cand"),
        P("cand"),
        P("cand"),
        P(),
        P(),
        P(),
        P("cand", None, None),
        P("cand", None, None),
        P("cand", None, None),
    )
    return jax.shard_map(
        body,
        mesh=mesh,
        in_specs=placed,
        out_specs=(P("cand", None, "img"), P("cand", None, "img"), P("cand", None, "img")),
        check_vma=False,
    )
```

```python
import functools

import jax
import jax.numpy as jnp
import ml_dtypes
import numpy as np
from jax import lax
from jax.experimental import pallas as pl
from jax.experimental.pallas import tpu as pltpu
from jax.sharding import PartitionSpec as P

F32 = jnp.float32
BF16 = jnp.bfloat16
LANES = 128
TILE = 256


def round_up(value, step):
    return -(-value // step) * step


def dft_matrices(side, taps):
    width = int(round(taps**0.5))
    reach = width // 2
    period = side + reach
    kept = []
    for u in range(period):
        for v in range(period):
            if (u, v) <= ((-u) % period, (-v) % period):
                kept.append((u, v))
    freqs = np.array(kept)
    count = len(kept)
    rows = round_up(count, 8)
    mirrored = ((-freqs) % period == freqs).all(axis=1)
    weight = np.where(mirrored, 1.0, 2.0) / period**2
    cell = np.stack(np.meshgrid(np.arange(side), np.arange(side), indexing="ij"), -1).reshape(-1, 2)
    half = len(cell) // 2
    cell = np.concatenate([cell[:half], cell[half:][::-1]]) - (side - 1) / 2
    tap = np.stack(np.meshgrid(np.arange(width), np.arange(width), indexing="ij"), -1).reshape(-1, 2) - reach
    cell_angle = 2 * np.pi * (freqs @ cell.T) / period
    tap_angle = 2 * np.pi * ((freqs @ tap.T) % period) / period
    tap_rows = round_up(taps, 16)

    analysis = np.zeros((2 * rows, side * side))
    analysis[:count] = np.cos(cell_angle)
    analysis[rows : rows + count] = -np.sin(cell_angle)
    even = np.zeros((half, rows))
    even[:, :count] = (weight[:, None] * np.cos(cell_angle)).T[:half]
    odd = np.zeros((half, rows))
    odd[:, :count] = -(weight[:, None] * np.sin(cell_angle)).T[:half]
    spectrum = np.zeros((2 * rows, tap_rows))
    spectrum[:count, :taps] = np.cos(tap_angle)
    spectrum[rows : rows + count, :taps] = np.sin(tap_angle)
    gather = np.zeros((tap_rows, 2 * rows))
    gather[:taps, :count] = (weight[:, None] * np.cos(tap_angle)).T
    gather[:taps, rows : rows + count] = -(weight[:, None] * np.sin(tap_angle)).T

    coarse = spectrum.astype(ml_dtypes.bfloat16).astype(np.float64)
    spectrum = np.concatenate([coarse, coarse, spectrum - coarse], axis=1)
    return rows, [jnp.asarray(m.astype(ml_dtypes.bfloat16)) for m in (analysis, even, odd, spectrum, gather)]


def dot(a, b):
    return jnp.dot(a, b, preferred_element_type=F32)


def dot_nt(a, b):
    return lax.dot_general(a, b, (((1,), (1,)), ((), ())), preferred_element_type=F32)


def grads_kernel(
    dims,
    offsets,
    layer_ref,
    half_ref,
    radius_ref,
    place_ref,
    *refs,
):
    x_refs, refs = refs[: len(offsets)], refs[len(offsets) :]
    (
    analysis_ref,
    even_ref,
    odd_ref,
    spectrum_ref,
    gather_ref,
    teach_up,
    teach_dw,
    teach_down,
    cand_up,
    cand_dw,
    cand_down,
    grad_up,
    grad_dw,
    grad_down,
    up_buf,
    dw_buf,
    cand_dw_buf,
    down_buf,
    up_tail,
    dw_pad,
    down_pad,
    act,
    spec,
    slope_e,
    slope_k,
    x_first,
    x_now,
    x_turned,
    err_now,
    err_turned,
    target,
    wide_up,
    wide_dw,
    wide_down,
    sems,
    ) = refs
    maps, cells, channels, hid, taps, rows, parts, scale = dims
    main = hid // TILE * TILE
    tail = hid - main
    padded = round_up(hid, LANES)
    own = hid // parts
    window = wide_up.shape[1]

    def copies(slot):
        if slot < 2:
            sources = (teach_up.at[slot], teach_dw, teach_down.at[slot])
            targets = (up_buf.at[slot], dw_buf, down_buf.at[slot])
        else:
            sources = (cand_up.at[0], cand_dw, cand_down.at[0])
            targets = (up_buf.at[slot], cand_dw_buf, down_buf.at[slot])
        if slot == 1:
            sources, targets = sources[::2], targets[::2]
        return [
            pltpu.make_async_copy(src, dst, sems.at[slot, n])
            for n, (src, dst) in enumerate(zip(sources, targets))
        ]

    for slot in (0, 2):
        for copy in copies(slot):
            copy.start()

    @pl.when(layer_ref[0] != 0)
    def _():
        for copy in copies(1):
            copy.start()

    analysis = analysis_ref[...]
    even, odd = even_ref[...], odd_ref[...]
    spectrum = spectrum_ref[...]
    dw_pad[...] = jnp.zeros_like(dw_pad)
    up_tail[...] = jnp.zeros_like(up_tail)
    down_pad[:, main:] = jnp.zeros((channels, padded - main), BF16)

    half_cells = cells // 2

    def synthesis(re, im):
        same, other = dot(even, re.astype(BF16)), dot(odd, im.astype(BF16))
        return jnp.concatenate([same + other, same - other], axis=0)

    def tap_spectrum(cols):
        weights = dw_pad[:, cols]
        high = weights.astype(BF16)
        low = (weights - high.astype(F32)).astype(BF16)
        both = dot(spectrum, jnp.concatenate([high, low, high], axis=0))
        return both[:rows], both[rows:]

    def load(slot, mask_taps):
        for copy in copies(slot):
            copy.wait()
        weights = cand_dw_buf[:, 0] if slot == 2 else dw_buf[:, slot]
        if mask_taps:
            side = int(round(taps**0.5))
            index = lax.broadcasted_iota(jnp.int32, weights.shape, 0)
            row = sum((index >= side * n).astype(jnp.int32) for n in range(1, side))
            ring = jnp.maximum(jnp.abs(row - side // 2), jnp.abs(index - side * row - side // 2))
            unit = lax.broadcasted_iota(jnp.int32, weights.shape, 1)
            keep = (ring <= radius_ref[0]) & (unit < half_ref[0] * (hid // 2))
            weights = jnp.where(keep, weights, 0.0)
        dw_pad[:taps, :hid] = weights
        if tail:
            up_tail[:, :tail] = up_buf[slot, :, main:]
            down_pad[:, main:hid] = down_buf[slot, :, main:]

    def forward(slot, keep):
        def tile(cols, weights_up):
            pre = dot(x_now[...], weights_up)
            half = 0.5 * pre
            bend = jnp.tanh(half)
            units = (half + half * bend).astype(BF16)
            if keep:
                slope_e[:, cols] = (0.5 * ((1.0 + bend) + half * (1.0 - bend * bend))).astype(BF16)
            tap_re, tap_im = tap_spectrum(cols)
            for m in range(maps):
                here = slice(m * cells, (m + 1) * cells)
                both = dot(analysis, units[here])
                re, im = both[:rows], both[rows:]
                if keep:
                    spec[m, :, cols] = both.astype(BF16)
                mixed = synthesis(re * tap_re - im * tap_im, re * tap_im + im * tap_re)
                half_k = 0.5 * mixed
                bend_k = jnp.tanh(half_k)
                act[here, cols] = (half_k + half_k * bend_k).astype(BF16)
                if keep:
                    slope_k[here, cols] = (0.5 * ((1.0 + bend_k) + half_k * (1.0 - bend_k * bend_k))).astype(BF16)

        def step(n, _):
            cols = pl.ds(pl.multiple_of(n * TILE, TILE), TILE)
            tile(cols, up_buf[slot, :, cols])
            return 0

        lax.fori_loop(0, main // TILE, step, 0)
        if tail:
            tile(pl.ds(main, padded - main), up_tail[...])
        out = dot_nt(act[:, :main], down_buf[slot, :, :main])
        if tail:
            out += dot_nt(act[:, main:], down_pad[:, main:])
        return out

    whole_turn = (
        lax.broadcasted_iota(jnp.int32, (half_cells, half_cells), 0)
        + lax.broadcasted_iota(jnp.int32, (half_cells, half_cells), 1)
    ) == half_cells - 1
    turn_half = whole_turn.astype(F32).astype(BF16)
    for x_ref, offset in zip(x_refs, offsets):
        if offset is None:
            x_first[...] = x_ref[...]
            continue
        block = x_ref.shape[1]
        for n, distance in enumerate(offset):
            source = place_ref[0] ^ distance
            source = (source & (parts - 1)) * (cells // block) + (source >> (parts.bit_length() - 1))
            at = pl.multiple_of(source * block, block)
            x_first[pl.ds(at, block), :] = x_ref[n]
    for m in range(maps):
        second = slice(m * cells + half_cells, (m + 1) * cells)
        x_first[second] = dot(turn_half, x_first[second]).astype(BF16)
    x_now[...] = x_first[...]
    load(0, False)
    target[...] = forward(0, False)

    @pl.when(layer_ref[0] != 0)
    def _():
        x_now[...] = (x_first[...].astype(F32) + target[...]).astype(BF16)
        load(1, False)
        target[...] = forward(1, False)

    load(2, True)
    down_pad[:, :main] = down_buf[2, :, :main]
    err = (forward(2, True) - target[...]) * scale
    err_now[...] = err.astype(BF16)
    err_turned[...] = jnp.transpose(err).astype(BF16)
    x_turned[...] = jnp.transpose(x_now[...].astype(F32)).astype(BF16)

    start = place_ref[1] * own
    base = jnp.minimum(start // LANES * LANES, padded - window)

    def back(at, width):
        cols = pl.ds(pl.multiple_of(base + at, LANES), width)
        here = pl.ds(pl.multiple_of(at, LANES), width)
        grad_act = dot(err_now[...], down_pad[:, cols])
        grad_k = (grad_act * slope_k[:, cols].astype(F32)).astype(BF16)
        tap_re, tap_im = tap_spectrum(cols)
        sum_re = jnp.zeros((rows, width), F32)
        sum_im = jnp.zeros((rows, width), F32)
        grad_pre = []
        for m in range(maps):
            rows_here = slice(m * cells, (m + 1) * cells)
            both = dot(analysis, grad_k[rows_here])
            re, im = both[:rows], both[rows:]
            kept = spec[m, :, cols].astype(F32)
            e_re, e_im = kept[:rows], kept[rows:]
            sum_re += re * e_re + im * e_im
            sum_im += re * e_im - im * e_re
            grad_e = synthesis(re * tap_re + im * tap_im, im * tap_re - re * tap_im)
            grad_pre.append((grad_e * slope_e[rows_here, cols].astype(F32)).astype(BF16))
        wide_up[:, here] = dot(x_turned[...], jnp.concatenate(grad_pre, axis=0))
        wide_down[:, here] = dot(err_turned[...], act[:, cols])
        sums = jnp.concatenate([sum_re, sum_im], axis=0).astype(BF16)
        wide_dw[:, here] = dot(gather_ref[...], sums)

    def back_step(n, _):
        back(n * TILE, TILE)
        return 0

    lax.fori_loop(0, window // TILE, back_step, 0)
    if window % TILE:
        back(window // TILE * TILE, window % TILE)

    offset = start - base
    turn = lax.rem(window - offset, window)
    grad_up[0] = pltpu.roll(wide_up[...], turn, 1)[:, :own]
    grad_down[0] = pltpu.roll(wide_down[...], turn, 1)[:, :own]
    rolled = pltpu.roll(wide_dw[...], turn, 1)[:taps, :own]
    side = int(round(taps**0.5))
    index = lax.broadcasted_iota(jnp.int32, rolled.shape, 0)
    row = sum((index >= side * n).astype(jnp.int32) for n in range(1, side))
    ring = jnp.maximum(jnp.abs(row - side // 2), jnp.abs(index - side * row - side // 2))
    unit = lax.broadcasted_iota(jnp.int32, rolled.shape, 1) + start
    keep = (ring <= radius_ref[0]) & (unit < half_ref[0] * (hid // 2))
    grad_dw[:, 0] = jnp.where(keep, rolled, 0.0)


def local_grads(pieces, offsets, maps, layer, half, radius, place, parts, images, weights):
    teach_up, teach_dw, teach_down, cand_up, cand_dw, cand_down = weights
    weights = (teach_up, teach_dw.transpose(1, 0, 2), teach_down, cand_up, cand_dw.transpose(1, 0, 2), cand_down)
    channels, hid = teach_up.shape[1:]
    taps = teach_dw.shape[1]
    count = sum(piece.size for piece in pieces) // channels
    cells = count // maps
    side = int(round(cells**0.5))
    rows, constants = dft_matrices(side, taps)
    padded = round_up(hid, LANES)
    own = hid // parts
    spare = max((p * own) % LANES for p in range(parts))
    window = min(round_up(own + spare, LANES), padded)
    tap_rows = round_up(taps, 16)
    main = hid // TILE * TILE
    dims = (maps, cells, channels, hid, taps, rows, parts, 1.0 / images)
    smem = pl.BlockSpec(memory_space=pltpu.SMEM)
    vmem = pl.BlockSpec(memory_space=pltpu.VMEM)
    anywhere = pl.BlockSpec(memory_space=pl.ANY)
    grad_up, grad_dw, grad_down = pl.pallas_call(
        functools.partial(grads_kernel, dims, offsets),
        out_shape=(
            jax.ShapeDtypeStruct((1, channels, own), F32),
            jax.ShapeDtypeStruct((taps, 1, own), F32),
            jax.ShapeDtypeStruct((1, channels, own), F32),
        ),
        in_specs=[smem] * 4 + [vmem] * (len(pieces) + 5) + [anywhere] * 6,
        out_specs=(vmem, vmem, vmem),
        scratch_shapes=[
            pltpu.VMEM((3, channels, hid), BF16),
            pltpu.VMEM(weights[1].shape, F32),
            pltpu.VMEM(weights[4].shape, F32),
            pltpu.VMEM((3, channels, hid), BF16),
            pltpu.VMEM((channels, max(padded - main, LANES)), BF16),
            pltpu.VMEM((tap_rows, padded), F32),
            pltpu.VMEM((channels, padded), BF16),
            pltpu.VMEM((count, padded), BF16),
            pltpu.VMEM((maps, 2 * rows, padded), BF16),
            pltpu.VMEM((count, padded), BF16),
            pltpu.VMEM((count, padded), BF16),
            pltpu.VMEM((count, channels), BF16),
            pltpu.VMEM((count, channels), BF16),
            pltpu.VMEM((channels, count), BF16),
            pltpu.VMEM((count, channels), BF16),
            pltpu.VMEM((channels, count), BF16),
            pltpu.VMEM((count, channels), F32),
            pltpu.VMEM((channels, window), F32),
            pltpu.VMEM((tap_rows, window), F32),
            pltpu.VMEM((channels, window), F32),
            pltpu.SemaphoreType.DMA((3, 3)),
        ],
        compiler_params=pltpu.CompilerParams(vmem_limit_bytes=60 * 2**20),
        cost_estimate=pl.CostEstimate(
            flops=20 * count * channels * hid, bytes_accessed=12 * channels * hid, transcendentals=6 * count * hid
        ),
    )(layer, half, radius, place, *pieces, *constants, *weights)
    return grad_up, grad_dw.transpose(1, 0, 2), grad_down


def exchange(block, masks, axes, devices):
    offset = [0]
    for mask in masks:
        distances = [d for d in range(1, devices) if d & ~mask == 0]
        parts = [block] + [
            lax.ppermute(block, axes, [(source, source ^ d) for source in range(devices)]) for d in distances
        ]
        pieces = [[o ^ d for o in offset] for d in [0] + distances]
        offset = sum(pieces, [])
        if mask != masks[-1]:
            block = jnp.concatenate(parts, axis=0)
    return parts, pieces


def body(
    first_maps,
    layer_of,
    expand_half,
    radius,
    teach_up,
    teach_dw,
    teach_down,
    cand_up,
    cand_dw,
    cand_down,
):
    parts = lax.axis_size("img")
    cands = lax.axis_size("cand")
    devices = parts * cands
    batch, own_cells, channels = first_maps.shape
    images = parts * batch
    part = lax.axis_index("img")
    place = jnp.stack([lax.axis_index("cand") * parts + part, part])
    weights = (teach_up, teach_dw, teach_down, cand_up, cand_dw, cand_down)
    scalars = (layer_of, expand_half, radius, place, parts, images, weights)
    mine = first_maps.astype(BF16)
    if batch == 1 and images == 2 and own_cells % 16 == 0 and devices & (devices - 1) == 0:
        low = min(2, cands) - 1
        low, near = low * parts, (parts - 1) | (low * parts * 2)
        masks = [(devices - 1) & ~near & ~low, near, low]
        pieces, offsets = exchange(mine, masks, ("cand", "img"), devices)
        return local_grads(pieces, offsets, images, *scalars)
    whole = lax.all_gather(mine, ("img", "cand")).reshape(parts, cands, batch, own_cells, channels)
    whole = whole.transpose(0, 2, 1, 3, 4).reshape(images, -1, channels)
    group = 2 if images % 2 == 0 else 1
    total = None
    for first in range(0, images, group):
        pieces = [whole[first : first + group].reshape(-1, channels)]
        grads = local_grads(pieces, [None], group, *scalars)
        total = grads if total is None else tuple(a + b for a, b in zip(total, grads))
    return total


def solution(mesh):
    placed = (
        P("img", "cand", None),
        P("cand"),
        P("cand"),
        P("cand"),
        P(),
        P(),
        P(),
        P("cand", None, None),
        P("cand", None, None),
        P("cand", None, None),
    )
    return jax.shard_map(
        body,
        mesh=mesh,
        in_specs=placed,
        out_specs=(P("cand", None, "img"), P("cand", None, "img"), P("cand", None, "img")),
        check_vma=False,
    )
```

```python
import functools

import jax
import jax.numpy as jnp
import ml_dtypes
import numpy as np
from jax import lax
from jax.experimental import pallas as pl
from jax.experimental.pallas import tpu as pltpu
from jax.sharding import PartitionSpec as P

F32 = jnp.float32
BF16 = jnp.bfloat16
LANES = 128
TILE = 512


def round_up(value, step):
    return -(-value // step) * step


def dft_matrices(side, taps):
    width = int(round(taps**0.5))
    reach = width // 2
    period = side + reach
    kept = []
    for u in range(period):
        for v in range(period):
            if (u, v) <= ((-u) % period, (-v) % period):
                kept.append((u, v))
    freqs = np.array(kept)
    count = len(kept)
    rows = round_up(count, 8)
    mirrored = ((-freqs) % period == freqs).all(axis=1)
    weight = np.where(mirrored, 1.0, 2.0) / period**2
    cell = np.stack(np.meshgrid(np.arange(side), np.arange(side), indexing="ij"), -1).reshape(-1, 2)
    half = len(cell) // 2
    cell = np.concatenate([cell[:half], cell[half:][::-1]]) - (side - 1) / 2
    tap = np.stack(np.meshgrid(np.arange(width), np.arange(width), indexing="ij"), -1).reshape(-1, 2) - reach
    cell_angle = 2 * np.pi * (freqs @ cell.T) / period
    tap_angle = 2 * np.pi * ((freqs @ tap.T) % period) / period
    tap_rows = round_up(taps, 16)

    analysis = np.zeros((2 * rows, side * side))
    analysis[:count] = np.cos(cell_angle)
    analysis[rows : rows + count] = -np.sin(cell_angle)
    even = np.zeros((half, rows))
    even[:, :count] = (weight[:, None] * np.cos(cell_angle)).T[:half]
    odd = np.zeros((half, rows))
    odd[:, :count] = -(weight[:, None] * np.sin(cell_angle)).T[:half]
    spectrum = np.zeros((2 * rows, tap_rows))
    spectrum[:count, :taps] = np.cos(tap_angle)
    spectrum[rows : rows + count, :taps] = np.sin(tap_angle)
    gather = np.zeros((tap_rows, 2 * rows))
    gather[:taps, :count] = (weight[:, None] * np.cos(tap_angle)).T
    gather[:taps, rows : rows + count] = -(weight[:, None] * np.sin(tap_angle)).T

    coarse = spectrum.astype(ml_dtypes.bfloat16).astype(np.float64)
    spectrum = np.concatenate([coarse, coarse, spectrum - coarse], axis=1)
    return rows, [jnp.asarray(m.astype(ml_dtypes.bfloat16)) for m in (analysis, even, odd, spectrum, gather)]


def dot(a, b):
    return jnp.dot(a, b, preferred_element_type=F32)


def dot_nt(a, b):
    return lax.dot_general(a, b, (((1,), (1,)), ((), ())), preferred_element_type=F32)


def grads_kernel(
    dims,
    offsets,
    layer_ref,
    half_ref,
    radius_ref,
    place_ref,
    *refs,
):
    x_refs, refs = refs[: len(offsets)], refs[len(offsets) :]
    (
    analysis_ref,
    even_ref,
    odd_ref,
    spectrum_ref,
    gather_ref,
    teach_up,
    teach_dw,
    teach_down,
    cand_up,
    cand_dw,
    cand_down,
    grad_up,
    grad_dw,
    grad_down,
    up_buf,
    dw_buf,
    cand_dw_buf,
    down_buf,
    up_tail,
    dw_pad,
    down_pad,
    act,
    spec,
    slope_e,
    slope_k,
    x_first,
    x_now,
    x_turned,
    err_now,
    err_turned,
    target,
    wide_up,
    wide_dw,
    wide_down,
    sems,
    ) = refs
    maps, cells, channels, hid, taps, rows, parts, scale = dims
    main = hid // TILE * TILE
    tail = hid - main
    padded = round_up(hid, LANES)
    own = hid // parts
    window = wide_up.shape[1]

    def copies(slot):
        if slot < 2:
            sources = (teach_up.at[slot], teach_dw, teach_down.at[slot])
            targets = (up_buf.at[slot], dw_buf, down_buf.at[slot])
        else:
            sources = (cand_up.at[0], cand_dw, cand_down.at[0])
            targets = (up_buf.at[slot], cand_dw_buf, down_buf.at[slot])
        if slot == 1:
            sources, targets = sources[::2], targets[::2]
        return [
            pltpu.make_async_copy(src, dst, sems.at[slot, n])
            for n, (src, dst) in enumerate(zip(sources, targets))
        ]

    for slot in (0, 2):
        for copy in copies(slot):
            copy.start()

    @pl.when(layer_ref[0] != 0)
    def _():
        for copy in copies(1):
            copy.start()

    analysis = analysis_ref[...]
    even, odd = even_ref[...], odd_ref[...]
    spectrum = spectrum_ref[...]
    dw_pad[...] = jnp.zeros_like(dw_pad)
    up_tail[...] = jnp.zeros_like(up_tail)
    down_pad[:, main:] = jnp.zeros((channels, padded - main), BF16)

    half_cells = cells // 2

    def synthesis(re, im):
        same, other = dot(even, re.astype(BF16)), dot(odd, im.astype(BF16))
        return jnp.concatenate([same + other, same - other], axis=0)

    def tap_spectrum(cols):
        weights = dw_pad[:, cols]
        high = weights.astype(BF16)
        low = (weights - high.astype(F32)).astype(BF16)
        both = dot(spectrum, jnp.concatenate([high, low, high], axis=0))
        return both[:rows], both[rows:]

    def load(slot, mask_taps):
        for copy in copies(slot):
            copy.wait()
        weights = cand_dw_buf[:, 0] if slot == 2 else dw_buf[:, slot]
        if mask_taps:
            side = int(round(taps**0.5))
            index = lax.broadcasted_iota(jnp.int32, weights.shape, 0)
            row = sum((index >= side * n).astype(jnp.int32) for n in range(1, side))
            ring = jnp.maximum(jnp.abs(row - side // 2), jnp.abs(index - side * row - side // 2))
            unit = lax.broadcasted_iota(jnp.int32, weights.shape, 1)
            keep = (ring <= radius_ref[0]) & (unit < half_ref[0] * (hid // 2))
            weights = jnp.where(keep, weights, 0.0)
        dw_pad[:taps, :hid] = weights
        if tail:
            up_tail[:, :tail] = up_buf[slot, :, main:]
            down_pad[:, main:hid] = down_buf[slot, :, main:]

    def forward(slot, keep):
        def tile(cols, weights_up):
            pre = dot(x_now[...], weights_up)
            half = 0.5 * pre
            bend = jnp.tanh(half)
            units = (half + half * bend).astype(BF16)
            if keep:
                slope_e[:, cols] = (0.5 * ((1.0 + bend) + half * (1.0 - bend * bend))).astype(BF16)
            tap_re, tap_im = tap_spectrum(cols)
            for m in range(maps):
                here = slice(m * cells, (m + 1) * cells)
                both = dot(analysis, units[here])
                re, im = both[:rows], both[rows:]
                if keep:
                    spec[m, :, cols] = both.astype(BF16)
                mixed = synthesis(re * tap_re - im * tap_im, re * tap_im + im * tap_re)
                half_k = 0.5 * mixed
                bend_k = jnp.tanh(half_k)
                act[here, cols] = (half_k + half_k * bend_k).astype(BF16)
                if keep:
                    slope_k[here, cols] = (0.5 * ((1.0 + bend_k) + half_k * (1.0 - bend_k * bend_k))).astype(BF16)

        def step(n, _):
            cols = pl.ds(pl.multiple_of(n * TILE, TILE), TILE)
            tile(cols, up_buf[slot, :, cols])
            return 0

        lax.fori_loop(0, main // TILE, step, 0)
        if tail:
            tile(pl.ds(main, padded - main), up_tail[...])
        out = dot_nt(act[:, :main], down_buf[slot, :, :main])
        if tail:
            out += dot_nt(act[:, main:], down_pad[:, main:])
        return out

    whole_turn = (
        lax.broadcasted_iota(jnp.int32, (half_cells, half_cells), 0)
        + lax.broadcasted_iota(jnp.int32, (half_cells, half_cells), 1)
    ) == half_cells - 1
    turn_half = whole_turn.astype(F32).astype(BF16)
    for x_ref, offset in zip(x_refs, offsets):
        if offset is None:
            x_first[...] = x_ref[...]
            continue
        block = x_ref.shape[1]
        for n, distance in enumerate(offset):
            source = place_ref[0] ^ distance
            source = (source & (parts - 1)) * (cells // block) + (source >> (parts.bit_length() - 1))
            at = pl.multiple_of(source * block, block)
            x_first[pl.ds(at, block), :] = x_ref[n]
    for m in range(maps):
        second = slice(m * cells + half_cells, (m + 1) * cells)
        x_first[second] = dot(turn_half, x_first[second]).astype(BF16)
    x_now[...] = x_first[...]
    load(0, False)
    target[...] = forward(0, False)

    @pl.when(layer_ref[0] != 0)
    def _():
        x_now[...] = (x_first[...].astype(F32) + target[...]).astype(BF16)
        load(1, False)
        target[...] = forward(1, False)

    load(2, True)
    down_pad[:, :main] = down_buf[2, :, :main]
    err = (forward(2, True) - target[...]) * scale
    err_now[...] = err.astype(BF16)
    err_turned[...] = jnp.transpose(err).astype(BF16)
    x_turned[...] = jnp.transpose(x_now[...].astype(F32)).astype(BF16)

    start = place_ref[1] * own
    base = jnp.minimum(start // LANES * LANES, padded - window)

    def back(at, width):
        cols = pl.ds(pl.multiple_of(base + at, LANES), width)
        here = pl.ds(pl.multiple_of(at, LANES), width)
        grad_act = dot(err_now[...], down_pad[:, cols])
        grad_k = (grad_act * slope_k[:, cols].astype(F32)).astype(BF16)
        tap_re, tap_im = tap_spectrum(cols)
        sum_re = jnp.zeros((rows, width), F32)
        sum_im = jnp.zeros((rows, width), F32)
        grad_pre = []
        for m in range(maps):
            rows_here = slice(m * cells, (m + 1) * cells)
            both = dot(analysis, grad_k[rows_here])
            re, im = both[:rows], both[rows:]
            kept = spec[m, :, cols].astype(F32)
            e_re, e_im = kept[:rows], kept[rows:]
            sum_re += re * e_re + im * e_im
            sum_im += re * e_im - im * e_re
            grad_e = synthesis(re * tap_re + im * tap_im, im * tap_re - re * tap_im)
            grad_pre.append((grad_e * slope_e[rows_here, cols].astype(F32)).astype(BF16))
        wide_up[:, here] = dot(x_turned[...], jnp.concatenate(grad_pre, axis=0))
        wide_down[:, here] = dot(err_turned[...], act[:, cols])
        sums = jnp.concatenate([sum_re, sum_im], axis=0).astype(BF16)
        wide_dw[:, here] = dot(gather_ref[...], sums)

    def back_step(n, _):
        back(n * TILE, TILE)
        return 0

    lax.fori_loop(0, window // TILE, back_step, 0)
    if window % TILE:
        back(window // TILE * TILE, window % TILE)

    offset = start - base
    turn = lax.rem(window - offset, window)
    grad_up[0] = pltpu.roll(wide_up[...], turn, 1)[:, :own]
    grad_down[0] = pltpu.roll(wide_down[...], turn, 1)[:, :own]
    rolled = pltpu.roll(wide_dw[...], turn, 1)[:taps, :own]
    side = int(round(taps**0.5))
    index = lax.broadcasted_iota(jnp.int32, rolled.shape, 0)
    row = sum((index >= side * n).astype(jnp.int32) for n in range(1, side))
    ring = jnp.maximum(jnp.abs(row - side // 2), jnp.abs(index - side * row - side // 2))
    unit = lax.broadcasted_iota(jnp.int32, rolled.shape, 1) + start
    keep = (ring <= radius_ref[0]) & (unit < half_ref[0] * (hid // 2))
    grad_dw[:, 0] = jnp.where(keep, rolled, 0.0)


def local_grads(pieces, offsets, maps, layer, half, radius, place, parts, images, weights):
    teach_up, teach_dw, teach_down, cand_up, cand_dw, cand_down = weights
    weights = (teach_up, teach_dw.transpose(1, 0, 2), teach_down, cand_up, cand_dw.transpose(1, 0, 2), cand_down)
    channels, hid = teach_up.shape[1:]
    taps = teach_dw.shape[1]
    count = sum(piece.size for piece in pieces) // channels
    cells = count // maps
    side = int(round(cells**0.5))
    rows, constants = dft_matrices(side, taps)
    padded = round_up(hid, LANES)
    own = hid // parts
    spare = max((p * own) % LANES for p in range(parts))
    window = min(round_up(own + spare, LANES), padded)
    tap_rows = round_up(taps, 16)
    main = hid // TILE * TILE
    dims = (maps, cells, channels, hid, taps, rows, parts, 1.0 / images)
    smem = pl.BlockSpec(memory_space=pltpu.SMEM)
    vmem = pl.BlockSpec(memory_space=pltpu.VMEM)
    anywhere = pl.BlockSpec(memory_space=pl.ANY)
    grad_up, grad_dw, grad_down = pl.pallas_call(
        functools.partial(grads_kernel, dims, offsets),
        out_shape=(
            jax.ShapeDtypeStruct((1, channels, own), F32),
            jax.ShapeDtypeStruct((taps, 1, own), F32),
            jax.ShapeDtypeStruct((1, channels, own), F32),
        ),
        in_specs=[smem] * 4 + [vmem] * (len(pieces) + 5) + [anywhere] * 6,
        out_specs=(vmem, vmem, vmem),
        scratch_shapes=[
            pltpu.VMEM((3, channels, hid), BF16),
            pltpu.VMEM(weights[1].shape, F32),
            pltpu.VMEM(weights[4].shape, F32),
            pltpu.VMEM((3, channels, hid), BF16),
            pltpu.VMEM((channels, max(padded - main, LANES)), BF16),
            pltpu.VMEM((tap_rows, padded), F32),
            pltpu.VMEM((channels, padded), BF16),
            pltpu.VMEM((count, padded), BF16),
            pltpu.VMEM((maps, 2 * rows, padded), BF16),
            pltpu.VMEM((count, padded), BF16),
            pltpu.VMEM((count, padded), BF16),
            pltpu.VMEM((count, channels), BF16),
            pltpu.VMEM((count, channels), BF16),
            pltpu.VMEM((channels, count), BF16),
            pltpu.VMEM((count, channels), BF16),
            pltpu.VMEM((channels, count), BF16),
            pltpu.VMEM((count, channels), F32),
            pltpu.VMEM((channels, window), F32),
            pltpu.VMEM((tap_rows, window), F32),
            pltpu.VMEM((channels, window), F32),
            pltpu.SemaphoreType.DMA((3, 3)),
        ],
        compiler_params=pltpu.CompilerParams(vmem_limit_bytes=60 * 2**20),
        cost_estimate=pl.CostEstimate(
            flops=20 * count * channels * hid, bytes_accessed=12 * channels * hid, transcendentals=6 * count * hid
        ),
    )(layer, half, radius, place, *pieces, *constants, *weights)
    return grad_up, grad_dw.transpose(1, 0, 2), grad_down


def exchange(block, masks, axes, devices):
    offset = [0]
    for mask in masks:
        distances = [d for d in range(1, devices) if d & ~mask == 0]
        parts = [block] + [
            lax.ppermute(block, axes, [(source, source ^ d) for source in range(devices)]) for d in distances
        ]
        pieces = [[o ^ d for o in offset] for d in [0] + distances]
        offset = sum(pieces, [])
        if mask != masks[-1]:
            block = jnp.concatenate(parts, axis=0)
    return parts, pieces


def body(
    first_maps,
    layer_of,
    expand_half,
    radius,
    teach_up,
    teach_dw,
    teach_down,
    cand_up,
    cand_dw,
    cand_down,
):
    parts = lax.axis_size("img")
    cands = lax.axis_size("cand")
    devices = parts * cands
    batch, own_cells, channels = first_maps.shape
    images = parts * batch
    part = lax.axis_index("img")
    place = jnp.stack([lax.axis_index("cand") * parts + part, part])
    weights = (teach_up, teach_dw, teach_down, cand_up, cand_dw, cand_down)
    scalars = (layer_of, expand_half, radius, place, parts, images, weights)
    mine = first_maps.astype(BF16)
    if batch == 1 and images == 2 and own_cells % 16 == 0 and devices & (devices - 1) == 0:
        low = min(2, cands) - 1
        low, near = low * parts, (parts - 1) | (low * parts * 2)
        masks = [(devices - 1) & ~near & ~low, near, low]
        pieces, offsets = exchange(mine, masks, ("cand", "img"), devices)
        return local_grads(pieces, offsets, images, *scalars)
    whole = lax.all_gather(mine, ("img", "cand")).reshape(parts, cands, batch, own_cells, channels)
    whole = whole.transpose(0, 2, 1, 3, 4).reshape(images, -1, channels)
    group = 2 if images % 2 == 0 else 1
    total = None
    for first in range(0, images, group):
        pieces = [whole[first : first + group].reshape(-1, channels)]
        grads = local_grads(pieces, [None], group, *scalars)
        total = grads if total is None else tuple(a + b for a, b in zip(total, grads))
    return total


def solution(mesh):
    placed = (
        P("img", "cand", None),
        P("cand"),
        P("cand"),
        P("cand"),
        P(),
        P(),
        P(),
        P("cand", None, None),
        P("cand", None, None),
        P("cand", None, None),
    )
    return jax.shard_map(
        body,
        mesh=mesh,
        in_specs=placed,
        out_specs=(P("cand", None, "img"), P("cand", None, "img"), P("cand", None, "img")),
        check_vma=False,
    )
```

```python
import functools

import jax
import jax.numpy as jnp
import ml_dtypes
import numpy as np
from jax import lax
from jax.experimental import pallas as pl
from jax.experimental.pallas import tpu as pltpu
from jax.sharding import PartitionSpec as P

F32 = jnp.float32
BF16 = jnp.bfloat16
LANES = 128
TILE = 1024


def round_up(value, step):
    return -(-value // step) * step


def dft_matrices(side, taps):
    width = int(round(taps**0.5))
    reach = width // 2
    period = side + reach
    kept = []
    for u in range(period):
        for v in range(period):
            if (u, v) <= ((-u) % period, (-v) % period):
                kept.append((u, v))
    freqs = np.array(kept)
    count = len(kept)
    rows = round_up(count, 8)
    mirrored = ((-freqs) % period == freqs).all(axis=1)
    weight = np.where(mirrored, 1.0, 2.0) / period**2
    cell = np.stack(np.meshgrid(np.arange(side), np.arange(side), indexing="ij"), -1).reshape(-1, 2)
    half = len(cell) // 2
    cell = np.concatenate([cell[:half], cell[half:][::-1]]) - (side - 1) / 2
    tap = np.stack(np.meshgrid(np.arange(width), np.arange(width), indexing="ij"), -1).reshape(-1, 2) - reach
    cell_angle = 2 * np.pi * (freqs @ cell.T) / period
    tap_angle = 2 * np.pi * ((freqs @ tap.T) % period) / period
    tap_rows = round_up(taps, 16)

    analysis = np.zeros((2 * rows, side * side))
    analysis[:count] = np.cos(cell_angle)
    analysis[rows : rows + count] = -np.sin(cell_angle)
    even = np.zeros((half, rows))
    even[:, :count] = (weight[:, None] * np.cos(cell_angle)).T[:half]
    odd = np.zeros((half, rows))
    odd[:, :count] = -(weight[:, None] * np.sin(cell_angle)).T[:half]
    spectrum = np.zeros((2 * rows, tap_rows))
    spectrum[:count, :taps] = np.cos(tap_angle)
    spectrum[rows : rows + count, :taps] = np.sin(tap_angle)
    gather = np.zeros((tap_rows, 2 * rows))
    gather[:taps, :count] = (weight[:, None] * np.cos(tap_angle)).T
    gather[:taps, rows : rows + count] = -(weight[:, None] * np.sin(tap_angle)).T

    coarse = spectrum.astype(ml_dtypes.bfloat16).astype(np.float64)
    spectrum = np.concatenate([coarse, coarse, spectrum - coarse], axis=1)
    return rows, [jnp.asarray(m.astype(ml_dtypes.bfloat16)) for m in (analysis, even, odd, spectrum, gather)]


def dot(a, b):
    return jnp.dot(a, b, preferred_element_type=F32)


def dot_nt(a, b):
    return lax.dot_general(a, b, (((1,), (1,)), ((), ())), preferred_element_type=F32)


def grads_kernel(
    dims,
    offsets,
    layer_ref,
    half_ref,
    radius_ref,
    place_ref,
    *refs,
):
    x_refs, refs = refs[: len(offsets)], refs[len(offsets) :]
    (
    analysis_ref,
    even_ref,
    odd_ref,
    spectrum_ref,
    gather_ref,
    teach_up,
    teach_dw,
    teach_down,
    cand_up,
    cand_dw,
    cand_down,
    grad_up,
    grad_dw,
    grad_down,
    up_buf,
    dw_buf,
    cand_dw_buf,
    down_buf,
    up_tail,
    dw_pad,
    down_pad,
    act,
    spec,
    slope_e,
    slope_k,
    x_first,
    x_now,
    x_turned,
    err_now,
    err_turned,
    target,
    wide_up,
    wide_dw,
    wide_down,
    sems,
    ) = refs
    maps, cells, channels, hid, taps, rows, parts, scale = dims
    main = hid // TILE * TILE
    tail = hid - main
    padded = round_up(hid, LANES)
    own = hid // parts
    window = wide_up.shape[1]

    def copies(slot):
        if slot < 2:
            sources = (teach_up.at[slot], teach_dw, teach_down.at[slot])
            targets = (up_buf.at[slot], dw_buf, down_buf.at[slot])
        else:
            sources = (cand_up.at[0], cand_dw, cand_down.at[0])
            targets = (up_buf.at[slot], cand_dw_buf, down_buf.at[slot])
        if slot == 1:
            sources, targets = sources[::2], targets[::2]
        return [
            pltpu.make_async_copy(src, dst, sems.at[slot, n])
            for n, (src, dst) in enumerate(zip(sources, targets))
        ]

    for slot in (0, 2):
        for copy in copies(slot):
            copy.start()

    @pl.when(layer_ref[0] != 0)
    def _():
        for copy in copies(1):
            copy.start()

    analysis = analysis_ref[...]
    even, odd = even_ref[...], odd_ref[...]
    spectrum = spectrum_ref[...]
    dw_pad[...] = jnp.zeros_like(dw_pad)
    up_tail[...] = jnp.zeros_like(up_tail)
    down_pad[:, main:] = jnp.zeros((channels, padded - main), BF16)

    half_cells = cells // 2

    def synthesis(re, im):
        same, other = dot(even, re.astype(BF16)), dot(odd, im.astype(BF16))
        return jnp.concatenate([same + other, same - other], axis=0)

    def tap_spectrum(cols):
        weights = dw_pad[:, cols]
        high = weights.astype(BF16)
        low = (weights - high.astype(F32)).astype(BF16)
        both = dot(spectrum, jnp.concatenate([high, low, high], axis=0))
        return both[:rows], both[rows:]

    def load(slot, mask_taps):
        for copy in copies(slot):
            copy.wait()
        weights = cand_dw_buf[:, 0] if slot == 2 else dw_buf[:, slot]
        if mask_taps:
            side = int(round(taps**0.5))
            index = lax.broadcasted_iota(jnp.int32, weights.shape, 0)
            row = sum((index >= side * n).astype(jnp.int32) for n in range(1, side))
            ring = jnp.maximum(jnp.abs(row - side // 2), jnp.abs(index - side * row - side // 2))
            unit = lax.broadcasted_iota(jnp.int32, weights.shape, 1)
            keep = (ring <= radius_ref[0]) & (unit < half_ref[0] * (hid // 2))
            weights = jnp.where(keep, weights, 0.0)
        dw_pad[:taps, :hid] = weights
        if tail:
            up_tail[:, :tail] = up_buf[slot, :, main:]
            down_pad[:, main:hid] = down_buf[slot, :, main:]

    def forward(slot, keep):
        def tile(cols, weights_up):
            pre = dot(x_now[...], weights_up)
            half = 0.5 * pre
            bend = jnp.tanh(half)
            units = (half + half * bend).astype(BF16)
            if keep:
                slope_e[:, cols] = (0.5 * ((1.0 + bend) + half * (1.0 - bend * bend))).astype(BF16)
            tap_re, tap_im = tap_spectrum(cols)
            for m in range(maps):
                here = slice(m * cells, (m + 1) * cells)
                both = dot(analysis, units[here])
                re, im = both[:rows], both[rows:]
                if keep:
                    spec[m, :, cols] = both.astype(BF16)
                mixed = synthesis(re * tap_re - im * tap_im, re * tap_im + im * tap_re)
                half_k = 0.5 * mixed
                bend_k = jnp.tanh(half_k)
                act[here, cols] = (half_k + half_k * bend_k).astype(BF16)
                if keep:
                    slope_k[here, cols] = (0.5 * ((1.0 + bend_k) + half_k * (1.0 - bend_k * bend_k))).astype(BF16)

        def step(n, _):
            cols = pl.ds(pl.multiple_of(n * TILE, TILE), TILE)
            tile(cols, up_buf[slot, :, cols])
            return 0

        lax.fori_loop(0, main // TILE, step, 0)
        if tail:
            tile(pl.ds(main, padded - main), up_tail[...])
        out = dot_nt(act[:, :main], down_buf[slot, :, :main])
        if tail:
            out += dot_nt(act[:, main:], down_pad[:, main:])
        return out

    whole_turn = (
        lax.broadcasted_iota(jnp.int32, (half_cells, half_cells), 0)
        + lax.broadcasted_iota(jnp.int32, (half_cells, half_cells), 1)
    ) == half_cells - 1
    turn_half = whole_turn.astype(F32).astype(BF16)
    for x_ref, offset in zip(x_refs, offsets):
        if offset is None:
            x_first[...] = x_ref[...]
            continue
        block = x_ref.shape[1]
        for n, distance in enumerate(offset):
            source = place_ref[0] ^ distance
            source = (source & (parts - 1)) * (cells // block) + (source >> (parts.bit_length() - 1))
            at = pl.multiple_of(source * block, block)
            x_first[pl.ds(at, block), :] = x_ref[n]
    for m in range(maps):
        second = slice(m * cells + half_cells, (m + 1) * cells)
        x_first[second] = dot(turn_half, x_first[second]).astype(BF16)
    x_now[...] = x_first[...]
    load(0, False)
    target[...] = forward(0, False)

    @pl.when(layer_ref[0] != 0)
    def _():
        x_now[...] = (x_first[...].astype(F32) + target[...]).astype(BF16)
        load(1, False)
        target[...] = forward(1, False)

    load(2, True)
    down_pad[:, :main] = down_buf[2, :, :main]
    err = (forward(2, True) - target[...]) * scale
    err_now[...] = err.astype(BF16)
    err_turned[...] = jnp.transpose(err).astype(BF16)
    x_turned[...] = jnp.transpose(x_now[...].astype(F32)).astype(BF16)

    start = place_ref[1] * own
    base = jnp.minimum(start // LANES * LANES, padded - window)

    def back(at, width):
        cols = pl.ds(pl.multiple_of(base + at, LANES), width)
        here = pl.ds(pl.multiple_of(at, LANES), width)
        grad_act = dot(err_now[...], down_pad[:, cols])
        grad_k = (grad_act * slope_k[:, cols].astype(F32)).astype(BF16)
        tap_re, tap_im = tap_spectrum(cols)
        sum_re = jnp.zeros((rows, width), F32)
        sum_im = jnp.zeros((rows, width), F32)
        grad_pre = []
        for m in range(maps):
            rows_here = slice(m * cells, (m + 1) * cells)
            both = dot(analysis, grad_k[rows_here])
            re, im = both[:rows], both[rows:]
            kept = spec[m, :, cols].astype(F32)
            e_re, e_im = kept[:rows], kept[rows:]
            sum_re += re * e_re + im * e_im
            sum_im += re * e_im - im * e_re
            grad_e = synthesis(re * tap_re + im * tap_im, im * tap_re - re * tap_im)
            grad_pre.append((grad_e * slope_e[rows_here, cols].astype(F32)).astype(BF16))
        wide_up[:, here] = dot(x_turned[...], jnp.concatenate(grad_pre, axis=0))
        wide_down[:, here] = dot(err_turned[...], act[:, cols])
        sums = jnp.concatenate([sum_re, sum_im], axis=0).astype(BF16)
        wide_dw[:, here] = dot(gather_ref[...], sums)

    def back_step(n, _):
        back(n * TILE, TILE)
        return 0

    lax.fori_loop(0, window // TILE, back_step, 0)
    if window % TILE:
        back(window // TILE * TILE, window % TILE)

    offset = start - base
    turn = lax.rem(window - offset, window)
    grad_up[0] = pltpu.roll(wide_up[...], turn, 1)[:, :own]
    grad_down[0] = pltpu.roll(wide_down[...], turn, 1)[:, :own]
    rolled = pltpu.roll(wide_dw[...], turn, 1)[:taps, :own]
    side = int(round(taps**0.5))
    index = lax.broadcasted_iota(jnp.int32, rolled.shape, 0)
    row = sum((index >= side * n).astype(jnp.int32) for n in range(1, side))
    ring = jnp.maximum(jnp.abs(row - side // 2), jnp.abs(index - side * row - side // 2))
    unit = lax.broadcasted_iota(jnp.int32, rolled.shape, 1) + start
    keep = (ring <= radius_ref[0]) & (unit < half_ref[0] * (hid // 2))
    grad_dw[:, 0] = jnp.where(keep, rolled, 0.0)


def local_grads(pieces, offsets, maps, layer, half, radius, place, parts, images, weights):
    teach_up, teach_dw, teach_down, cand_up, cand_dw, cand_down = weights
    weights = (teach_up, teach_dw.transpose(1, 0, 2), teach_down, cand_up, cand_dw.transpose(1, 0, 2), cand_down)
    channels, hid = teach_up.shape[1:]
    taps = teach_dw.shape[1]
    count = sum(piece.size for piece in pieces) // channels
    cells = count // maps
    side = int(round(cells**0.5))
    rows, constants = dft_matrices(side, taps)
    padded = round_up(hid, LANES)
    own = hid // parts
    spare = max((p * own) % LANES for p in range(parts))
    window = min(round_up(own + spare, LANES), padded)
    tap_rows = round_up(taps, 16)
    main = hid // TILE * TILE
    dims = (maps, cells, channels, hid, taps, rows, parts, 1.0 / images)
    smem = pl.BlockSpec(memory_space=pltpu.SMEM)
    vmem = pl.BlockSpec(memory_space=pltpu.VMEM)
    anywhere = pl.BlockSpec(memory_space=pl.ANY)
    grad_up, grad_dw, grad_down = pl.pallas_call(
        functools.partial(grads_kernel, dims, offsets),
        out_shape=(
            jax.ShapeDtypeStruct((1, channels, own), F32),
            jax.ShapeDtypeStruct((taps, 1, own), F32),
            jax.ShapeDtypeStruct((1, channels, own), F32),
        ),
        in_specs=[smem] * 4 + [vmem] * (len(pieces) + 5) + [anywhere] * 6,
        out_specs=(vmem, vmem, vmem),
        scratch_shapes=[
            pltpu.VMEM((3, channels, hid), BF16),
            pltpu.VMEM(weights[1].shape, F32),
            pltpu.VMEM(weights[4].shape, F32),
            pltpu.VMEM((3, channels, hid), BF16),
            pltpu.VMEM((channels, max(padded - main, LANES)), BF16),
            pltpu.VMEM((tap_rows, padded), F32),
            pltpu.VMEM((channels, padded), BF16),
            pltpu.VMEM((count, padded), BF16),
            pltpu.VMEM((maps, 2 * rows, padded), BF16),
            pltpu.VMEM((count, padded), BF16),
            pltpu.VMEM((count, padded), BF16),
            pltpu.VMEM((count, channels), BF16),
            pltpu.VMEM((count, channels), BF16),
            pltpu.VMEM((channels, count), BF16),
            pltpu.VMEM((count, channels), BF16),
            pltpu.VMEM((channels, count), BF16),
            pltpu.VMEM((count, channels), F32),
            pltpu.VMEM((channels, window), F32),
            pltpu.VMEM((tap_rows, window), F32),
            pltpu.VMEM((channels, window), F32),
            pltpu.SemaphoreType.DMA((3, 3)),
        ],
        compiler_params=pltpu.CompilerParams(vmem_limit_bytes=60 * 2**20),
        cost_estimate=pl.CostEstimate(
            flops=20 * count * channels * hid, bytes_accessed=12 * channels * hid, transcendentals=6 * count * hid
        ),
    )(layer, half, radius, place, *pieces, *constants, *weights)
    return grad_up, grad_dw.transpose(1, 0, 2), grad_down


def exchange(block, masks, axes, devices):
    offset = [0]
    for mask in masks:
        distances = [d for d in range(1, devices) if d & ~mask == 0]
        parts = [block] + [
            lax.ppermute(block, axes, [(source, source ^ d) for source in range(devices)]) for d in distances
        ]
        pieces = [[o ^ d for o in offset] for d in [0] + distances]
        offset = sum(pieces, [])
        if mask != masks[-1]:
            block = jnp.concatenate(parts, axis=0)
    return parts, pieces


def body(
    first_maps,
    layer_of,
    expand_half,
    radius,
    teach_up,
    teach_dw,
    teach_down,
    cand_up,
    cand_dw,
    cand_down,
):
    parts = lax.axis_size("img")
    cands = lax.axis_size("cand")
    devices = parts * cands
    batch, own_cells, channels = first_maps.shape
    images = parts * batch
    part = lax.axis_index("img")
    place = jnp.stack([lax.axis_index("cand") * parts + part, part])
    weights = (teach_up, teach_dw, teach_down, cand_up, cand_dw, cand_down)
    scalars = (layer_of, expand_half, radius, place, parts, images, weights)
    mine = first_maps.astype(BF16)
    if batch == 1 and images == 2 and own_cells % 16 == 0 and devices & (devices - 1) == 0:
        low = min(2, cands) - 1
        low, near = low * parts, (parts - 1) | (low * parts * 2)
        masks = [(devices - 1) & ~near & ~low, near, low]
        pieces, offsets = exchange(mine, masks, ("cand", "img"), devices)
        return local_grads(pieces, offsets, images, *scalars)
    whole = lax.all_gather(mine, ("img", "cand")).reshape(parts, cands, batch, own_cells, channels)
    whole = whole.transpose(0, 2, 1, 3, 4).reshape(images, -1, channels)
    group = 2 if images % 2 == 0 else 1
    total = None
    for first in range(0, images, group):
        pieces = [whole[first : first + group].reshape(-1, channels)]
        grads = local_grads(pieces, [None], group, *scalars)
        total = grads if total is None else tuple(a + b for a, b in zip(total, grads))
    return total


def solution(mesh):
    placed = (
        P("img", "cand", None),
        P("cand"),
        P("cand"),
        P("cand"),
        P(),
        P(),
        P(),
        P("cand", None, None),
        P("cand", None, None),
        P("cand", None, None),
    )
    return jax.shard_map(
        body,
        mesh=mesh,
        in_specs=placed,
        out_specs=(P("cand", None, "img"), P("cand", None, "img"), P("cand", None, "img")),
        check_vma=False,
    )
```

```python
import functools

import jax
import jax.numpy as jnp
import ml_dtypes
import numpy as np
from jax import lax
from jax.experimental import pallas as pl
from jax.experimental.pallas import tpu as pltpu
from jax.sharding import PartitionSpec as P

F32 = jnp.float32
BF16 = jnp.bfloat16
LANES = 128
UNIT = 512
BACK_UNIT = 384
DEPTH = 2
STAGGER = 5


def round_up(value, step):
    return -(-value // step) * step


def dft_matrices(side, taps):
    width = int(round(taps**0.5))
    reach = width // 2
    period = side + reach
    kept = []
    for u in range(period):
        for v in range(period):
            if (u, v) <= ((-u) % period, (-v) % period):
                kept.append((u, v))
    freqs = np.array(kept)
    count = len(kept)
    rows = round_up(count, 8)
    mirrored = ((-freqs) % period == freqs).all(axis=1)
    weight = np.where(mirrored, 1.0, 2.0) / period**2
    cell = np.stack(np.meshgrid(np.arange(side), np.arange(side), indexing="ij"), -1).reshape(-1, 2)
    half = len(cell) // 2
    cell = np.concatenate([cell[:half], cell[half:][::-1]]) - (side - 1) / 2
    tap = np.stack(np.meshgrid(np.arange(width), np.arange(width), indexing="ij"), -1).reshape(-1, 2) - reach
    cell_angle = 2 * np.pi * (freqs @ cell.T) / period
    tap_angle = 2 * np.pi * ((freqs @ tap.T) % period) / period
    tap_rows = round_up(taps, 16)

    analysis = np.zeros((2 * rows, side * side))
    analysis[:count] = np.cos(cell_angle)
    analysis[rows : rows + count] = -np.sin(cell_angle)
    even = np.zeros((half, rows))
    even[:, :count] = (weight[:, None] * np.cos(cell_angle)).T[:half]
    odd = np.zeros((half, rows))
    odd[:, :count] = -(weight[:, None] * np.sin(cell_angle)).T[:half]
    spectrum = np.zeros((2 * rows, tap_rows))
    spectrum[:count, :taps] = np.cos(tap_angle)
    spectrum[rows : rows + count, :taps] = np.sin(tap_angle)
    gather = np.zeros((tap_rows, 2 * rows))
    gather[:taps, :count] = (weight[:, None] * np.cos(tap_angle)).T
    gather[:taps, rows : rows + count] = -(weight[:, None] * np.sin(tap_angle)).T

    coarse = spectrum.astype(ml_dtypes.bfloat16).astype(np.float64)
    spectrum = np.concatenate([coarse, coarse, spectrum - coarse], axis=1)
    return rows, [jnp.asarray(m.astype(ml_dtypes.bfloat16)) for m in (analysis, even, odd, spectrum, gather)]


def dot(a, b):
    return jnp.dot(a, b, preferred_element_type=F32)


def dot_nt(a, b):
    return lax.dot_general(a, b, (((1,), (1,)), ((), ())), preferred_element_type=F32)


def interleave(units):
    waiting, running = list(units), []
    turn = 0
    while waiting or running:
        if waiting and len(running) < DEPTH and turn % STAGGER == 0:
            running.append(waiting.pop(0))
        turn += 1
        for unit in list(running):
            try:
                next(unit)
            except StopIteration:
                running.remove(unit)


def grads_kernel(
    dims,
    offsets,
    layer_ref,
    half_ref,
    radius_ref,
    place_ref,
    *refs,
):
    x_refs, refs = refs[: len(offsets)], refs[len(offsets) :]
    (
    analysis_ref,
    even_ref,
    odd_ref,
    spectrum_ref,
    gather_ref,
    teach_up,
    teach_dw,
    teach_down,
    cand_up,
    cand_dw,
    cand_down,
    grad_up,
    grad_dw,
    grad_down,
    up_buf,
    dw_buf,
    cand_dw_buf,
    down_buf,
    dw_pad,
    down_pad,
    act,
    spec,
    slope_e,
    slope_k,
    x_first,
    x_next,
    x_now,
    x_turned,
    err_now,
    err_turned,
    target,
    wide_up,
    wide_dw,
    wide_down,
    sems,
    ) = refs
    maps, cells, channels, hid, taps, rows, parts, scale = dims
    padded = round_up(hid, LANES)
    own = hid // parts
    window = wide_up.shape[1]

    def copies(slot):
        if slot < 2:
            sources = (teach_up.at[slot], teach_dw, teach_down.at[slot])
            targets = (up_buf.at[slot], dw_buf, down_buf.at[slot])
        else:
            sources = (cand_up.at[0], cand_dw, cand_down.at[0])
            targets = (up_buf.at[slot], cand_dw_buf, down_buf.at[slot])
        if slot == 1:
            sources, targets = sources[::2], targets[::2]
        return [
            pltpu.make_async_copy(src, dst, sems.at[slot, n])
            for n, (src, dst) in enumerate(zip(sources, targets))
        ]

    for slot in (0, 2, 1):
        for copy in copies(slot):
            copy.start()

    analysis = analysis_ref[...]
    even, odd = even_ref[...], odd_ref[...]
    spectrum = spectrum_ref[...]
    dw_pad[...] = jnp.zeros_like(dw_pad)

    half_cells = cells // 2

    def synthesis(re, im):
        same, other = dot(even, re.astype(BF16)), dot(odd, im.astype(BF16))
        return jnp.concatenate([same + other, same - other], axis=0)

    def tap_spectrum(slot, cols):
        weights = dw_pad[slot, :, cols]
        high = weights.astype(BF16)
        low = (weights - high.astype(F32)).astype(BF16)
        both = dot(spectrum, jnp.concatenate([high, low, high], axis=0))
        return both[:rows], both[rows:]

    def load(slot, mask_taps):
        for copy in copies(slot):
            copy.wait()
        weights = cand_dw_buf[:, 0] if slot == 2 else dw_buf[:, slot]
        if mask_taps:
            side = int(round(taps**0.5))
            index = lax.broadcasted_iota(jnp.int32, weights.shape, 0)
            row = sum((index >= side * n).astype(jnp.int32) for n in range(1, side))
            ring = jnp.maximum(jnp.abs(row - side // 2), jnp.abs(index - side * row - side // 2))
            unit = lax.broadcasted_iota(jnp.int32, weights.shape, 1)
            keep = (ring <= radius_ref[0]) & (unit < half_ref[0] * (hid // 2))
            weights = jnp.where(keep, weights, 0.0)
        dw_pad[slot, :taps, :hid] = weights

    def forward(slot, lhs, keep, lo, hi, results):
        cols = slice(lo, hi)
        pre = dot(lhs[...], up_buf[slot, :, cols])
        yield
        half = 0.5 * pre
        bend = jnp.tanh(half)
        units = (half + half * bend).astype(BF16)
        if keep:
            slope_e[:, cols] = (0.5 * ((1.0 + bend) + half * (1.0 - bend * bend))).astype(BF16)
        yield
        tap_re, tap_im = tap_spectrum(slot, cols)
        acts = []
        for m in range(maps):
            here = slice(m * cells, (m + 1) * cells)
            both = dot(analysis, units[here])
            yield
            re, im = both[:rows], both[rows:]
            if keep:
                spec[m, :, cols] = both.astype(BF16)
            mixed_re, mixed_im = re * tap_re - im * tap_im, re * tap_im + im * tap_re
            yield
            mixed = synthesis(mixed_re, mixed_im)
            yield
            half_k = 0.5 * mixed
            bend_k = jnp.tanh(half_k)
            acts.append((half_k + half_k * bend_k).astype(BF16))
            if keep:
                act[here, cols] = acts[-1]
                slope_k[here, cols] = (0.5 * ((1.0 + bend_k) + half_k * (1.0 - bend_k * bend_k))).astype(BF16)
        yield
        results.append(dot_nt(jnp.concatenate(acts, axis=0), down_buf[slot, :, cols]))

    bounds = list(range(0, max(hid - UNIT // 2, 1), UNIT)) + [hid]
    spans = list(zip(bounds, bounds[1:]))

    whole_turn = (
        lax.broadcasted_iota(jnp.int32, (half_cells, half_cells), 0)
        + lax.broadcasted_iota(jnp.int32, (half_cells, half_cells), 1)
    ) == half_cells - 1
    turn_half = whole_turn.astype(F32).astype(BF16)
    for x_ref, offset in zip(x_refs, offsets):
        if offset is None:
            x_first[...] = x_ref[...]
            continue
        block = x_ref.shape[1]
        for n, distance in enumerate(offset):
            source = place_ref[0] ^ distance
            source = (source & (parts - 1)) * (cells // block) + (source >> (parts.bit_length() - 1))
            at = pl.multiple_of(source * block, block)
            x_first[pl.ds(at, block), :] = x_ref[n]
    for m in range(maps):
        second = slice(m * cells + half_cells, (m + 1) * cells)
        x_first[second] = dot(turn_half, x_first[second]).astype(BF16)
    load(0, False)
    first = []
    interleave([forward(0, x_first, False, lo, hi, first) for lo, hi in spans])
    branch = sum(first)
    x_next[...] = (x_first[...].astype(F32) + branch).astype(BF16)
    x_now[...] = jnp.where(layer_ref[0] == 0, x_first[...], x_next[...])
    target[...] = branch
    load(2, True)
    load(1, False)
    second, third = [], []
    units = []
    for lo, hi in spans:
        units.append(forward(1, x_next, False, lo, hi, second))
        units.append(forward(2, x_now, True, lo, hi, third))
    interleave(units)
    down_pad[:, :hid] = down_buf[2]
    err = (sum(third) - jnp.where(layer_ref[0] == 0, target[...], sum(second))) * scale
    err_now[...] = err.astype(BF16)
    err_turned[...] = jnp.transpose(err).astype(BF16)
    x_turned[...] = jnp.transpose(x_now[...].astype(F32)).astype(BF16)

    start = place_ref[1] * own
    base = jnp.minimum(start // LANES * LANES, padded - window)

    def back(at, width):
        cols = pl.ds(pl.multiple_of(base + at, LANES), width)
        here = slice(at, at + width)
        grad_act = dot(err_now[...], down_pad[:, cols])
        wide_down[:, here] = dot(err_turned[...], act[:, cols])
        yield
        grad_k = (grad_act * slope_k[:, cols].astype(F32)).astype(BF16)
        yield
        tap_re, tap_im = tap_spectrum(2, cols)
        sum_re = sum_im = 0.0
        grad_pre = []
        for m in range(maps):
            rows_here = slice(m * cells, (m + 1) * cells)
            both = dot(analysis, grad_k[rows_here])
            yield
            re, im = both[:rows], both[rows:]
            kept = spec[m, :, cols].astype(F32)
            e_re, e_im = kept[:rows], kept[rows:]
            sum_re += re * e_re + im * e_im
            sum_im += re * e_im - im * e_re
            mixed_re, mixed_im = re * tap_re + im * tap_im, im * tap_re - re * tap_im
            yield
            grad_e = synthesis(mixed_re, mixed_im)
            yield
            grad_pre.append((grad_e * slope_e[rows_here, cols].astype(F32)).astype(BF16))
        yield
        wide_up[:, here] = dot(x_turned[...], jnp.concatenate(grad_pre, axis=0))
        sums = jnp.concatenate([sum_re, sum_im], axis=0).astype(BF16)
        wide_dw[:, here] = dot(gather_ref[...], sums)

    interleave([back(at, min(BACK_UNIT, window - at)) for at in range(0, window, BACK_UNIT)])

    offset = start - base
    turn = lax.rem(window - offset, window)
    grad_up[0] = pltpu.roll(wide_up[...], turn, 1)[:, :own]
    grad_down[0] = pltpu.roll(wide_down[...], turn, 1)[:, :own]
    rolled = pltpu.roll(wide_dw[...], turn, 1)[:taps, :own]
    side = int(round(taps**0.5))
    index = lax.broadcasted_iota(jnp.int32, rolled.shape, 0)
    row = sum((index >= side * n).astype(jnp.int32) for n in range(1, side))
    ring = jnp.maximum(jnp.abs(row - side // 2), jnp.abs(index - side * row - side // 2))
    unit = lax.broadcasted_iota(jnp.int32, rolled.shape, 1) + start
    keep = (ring <= radius_ref[0]) & (unit < half_ref[0] * (hid // 2))
    grad_dw[:, 0] = jnp.where(keep, rolled, 0.0)


def local_grads(pieces, offsets, maps, layer, half, radius, place, parts, images, weights):
    teach_up, teach_dw, teach_down, cand_up, cand_dw, cand_down = weights
    weights = (teach_up, teach_dw.transpose(1, 0, 2), teach_down, cand_up, cand_dw.transpose(1, 0, 2), cand_down)
    channels, hid = teach_up.shape[1:]
    taps = teach_dw.shape[1]
    count = sum(piece.size for piece in pieces) // channels
    cells = count // maps
    side = int(round(cells**0.5))
    rows, constants = dft_matrices(side, taps)
    padded = round_up(hid, LANES)
    own = hid // parts
    spare = max((p * own) % LANES for p in range(parts))
    window = min(round_up(own + spare, LANES), padded)
    tap_rows = round_up(taps, 16)
    dims = (maps, cells, channels, hid, taps, rows, parts, 1.0 / images)
    smem = pl.BlockSpec(memory_space=pltpu.SMEM)
    vmem = pl.BlockSpec(memory_space=pltpu.VMEM)
    anywhere = pl.BlockSpec(memory_space=pl.ANY)
    grad_up, grad_dw, grad_down = pl.pallas_call(
        functools.partial(grads_kernel, dims, offsets),
        out_shape=(
            jax.ShapeDtypeStruct((1, channels, own), F32),
            jax.ShapeDtypeStruct((taps, 1, own), F32),
            jax.ShapeDtypeStruct((1, channels, own), F32),
        ),
        in_specs=[smem] * 4 + [vmem] * (len(pieces) + 5) + [anywhere] * 6,
        out_specs=(vmem, vmem, vmem),
        scratch_shapes=[
            pltpu.VMEM((3, channels, hid), BF16),
            pltpu.VMEM(weights[1].shape, F32),
            pltpu.VMEM(weights[4].shape, F32),
            pltpu.VMEM((3, channels, hid), BF16),
            pltpu.VMEM((3, tap_rows, padded), F32),
            pltpu.VMEM((channels, padded), BF16),
            pltpu.VMEM((count, padded), BF16),
            pltpu.VMEM((maps, 2 * rows, padded), BF16),
            pltpu.VMEM((count, padded), BF16),
            pltpu.VMEM((count, padded), BF16),
            pltpu.VMEM((count, channels), BF16),
            pltpu.VMEM((count, channels), BF16),
            pltpu.VMEM((count, channels), BF16),
            pltpu.VMEM((channels, count), BF16),
            pltpu.VMEM((count, channels), BF16),
            pltpu.VMEM((channels, count), BF16),
            pltpu.VMEM((count, channels), F32),
            pltpu.VMEM((channels, window), F32),
            pltpu.VMEM((tap_rows, window), F32),
            pltpu.VMEM((channels, window), F32),
            pltpu.SemaphoreType.DMA((3, 3)),
        ],
        compiler_params=pltpu.CompilerParams(vmem_limit_bytes=60 * 2**20),
        cost_estimate=pl.CostEstimate(
            flops=20 * count * channels * hid, bytes_accessed=12 * channels * hid, transcendentals=6 * count * hid
        ),
    )(layer, half, radius, place, *pieces, *constants, *weights)
    return grad_up, grad_dw.transpose(1, 0, 2), grad_down


def exchange(block, masks, axes, devices):
    offset = [0]
    for mask in masks:
        distances = [d for d in range(1, devices) if d & ~mask == 0]
        parts = [block] + [
            lax.ppermute(block, axes, [(source, source ^ d) for source in range(devices)]) for d in distances
        ]
        pieces = [[o ^ d for o in offset] for d in [0] + distances]
        offset = sum(pieces, [])
        if mask != masks[-1]:
            block = jnp.concatenate(parts, axis=0)
    return parts, pieces


def body(
    first_maps,
    layer_of,
    expand_half,
    radius,
    teach_up,
    teach_dw,
    teach_down,
    cand_up,
    cand_dw,
    cand_down,
):
    parts = lax.axis_size("img")
    cands = lax.axis_size("cand")
    devices = parts * cands
    batch, own_cells, channels = first_maps.shape
    images = parts * batch
    part = lax.axis_index("img")
    place = jnp.stack([lax.axis_index("cand") * parts + part, part])
    weights = (teach_up, teach_dw, teach_down, cand_up, cand_dw, cand_down)
    scalars = (layer_of, expand_half, radius, place, parts, images, weights)
    mine = first_maps.astype(BF16)
    if batch == 1 and images == 2 and own_cells % 16 == 0 and devices & (devices - 1) == 0:
        low = min(2, cands) - 1
        low, near = low * parts, (parts - 1) | (low * parts * 2)
        masks = [(devices - 1) & ~near & ~low, near, low]
        pieces, offsets = exchange(mine, masks, ("cand", "img"), devices)
        return local_grads(pieces, offsets, images, *scalars)
    whole = lax.all_gather(mine, ("img", "cand")).reshape(parts, cands, batch, own_cells, channels)
    whole = whole.transpose(0, 2, 1, 3, 4).reshape(images, -1, channels)
    group = 2 if images % 2 == 0 else 1
    total = None
    for first in range(0, images, group):
        pieces = [whole[first : first + group].reshape(-1, channels)]
        grads = local_grads(pieces, [None], group, *scalars)
        total = grads if total is None else tuple(a + b for a, b in zip(total, grads))
    return total


def solution(mesh):
    placed = (
        P("img", "cand", None),
        P("cand"),
        P("cand"),
        P("cand"),
        P(),
        P(),
        P(),
        P("cand", None, None),
        P("cand", None, None),
        P("cand", None, None),
    )
    return jax.shard_map(
        body,
        mesh=mesh,
        in_specs=placed,
        out_specs=(P("cand", None, "img"), P("cand", None, "img"), P("cand", None, "img")),
        check_vma=False,
    )
```

```python
import functools
import itertools

import jax
import jax.numpy as jnp
import ml_dtypes
import numpy as np
from jax import lax
from jax.experimental import pallas as pl
from jax.experimental.pallas import tpu as pltpu
from jax.sharding import PartitionSpec as P

F32 = jnp.float32
BF16 = jnp.bfloat16
LANES = 128
UNIT = 512
BACK_UNIT = 384
DEPTH = 2
STAGGER = 5


def round_up(value, step):
    return -(-value // step) * step


def dft_matrices(side, taps):
    width = int(round(taps**0.5))
    reach = width // 2
    period = side + reach
    kept = []
    for u in range(period):
        for v in range(period):
            if (u, v) <= ((-u) % period, (-v) % period):
                kept.append((u, v))
    freqs = np.array(kept)
    count = len(kept)
    rows = round_up(count, 8)
    mirrored = ((-freqs) % period == freqs).all(axis=1)
    weight = np.where(mirrored, 1.0, 2.0) / period**2
    cell = np.stack(np.meshgrid(np.arange(side), np.arange(side), indexing="ij"), -1).reshape(-1, 2)
    half = len(cell) // 2
    cell = np.concatenate([cell[:half], cell[half:][::-1]]) - (side - 1) / 2
    tap = np.stack(np.meshgrid(np.arange(width), np.arange(width), indexing="ij"), -1).reshape(-1, 2) - reach
    cell_angle = 2 * np.pi * (freqs @ cell.T) / period
    tap_angle = 2 * np.pi * ((freqs @ tap.T) % period) / period
    tap_rows = round_up(taps, 16)

    analysis = np.zeros((2 * rows, side * side))
    analysis[:count] = np.cos(cell_angle)
    analysis[rows : rows + count] = -np.sin(cell_angle)
    even = np.zeros((half, rows))
    even[:, :count] = (weight[:, None] * np.cos(cell_angle)).T[:half]
    odd = np.zeros((half, rows))
    odd[:, :count] = -(weight[:, None] * np.sin(cell_angle)).T[:half]
    spectrum = np.zeros((2 * rows, tap_rows))
    spectrum[:count, :taps] = np.cos(tap_angle)
    spectrum[rows : rows + count, :taps] = np.sin(tap_angle)
    gather = np.zeros((tap_rows, 2 * rows))
    gather[:taps, :count] = (weight[:, None] * np.cos(tap_angle)).T
    gather[:taps, rows : rows + count] = -(weight[:, None] * np.sin(tap_angle)).T

    coarse = spectrum.astype(ml_dtypes.bfloat16).astype(np.float64)
    spectrum = np.concatenate([coarse, coarse, spectrum - coarse], axis=1)
    return rows, [jnp.asarray(m.astype(ml_dtypes.bfloat16)) for m in (analysis, even, odd, spectrum, gather)]


def dot(a, b):
    return jnp.dot(a, b, preferred_element_type=F32)


def dot_nt(a, b):
    return lax.dot_general(a, b, (((1,), (1,)), ((), ())), preferred_element_type=F32)


def interleave(units):
    waiting, running = list(units), []
    turn = 0
    while waiting or running:
        if waiting and len(running) < DEPTH and turn % STAGGER == 0:
            running.append(waiting.pop(0))
        turn += 1
        for unit in list(running):
            try:
                next(unit)
            except StopIteration:
                running.remove(unit)


def grads_kernel(
    dims,
    offsets,
    layer_ref,
    half_ref,
    radius_ref,
    place_ref,
    *refs,
):
    x_refs, refs = refs[: len(offsets)], refs[len(offsets) :]
    (
    analysis_ref,
    even_ref,
    odd_ref,
    spectrum_ref,
    gather_ref,
    teach_up,
    teach_dw,
    teach_down,
    cand_up,
    cand_dw,
    cand_down,
    grad_up,
    grad_dw,
    grad_down,
    up_buf,
    dw_buf,
    cand_dw_buf,
    down_buf,
    dw_pad,
    up_pad,
    down_pad,
    act,
    spec,
    slope_e,
    slope_k,
    x_first,
    x_next,
    x_now,
    x_turned,
    err_now,
    err_turned,
    target,
    wide_up,
    wide_dw,
    wide_down,
    sems,
    ) = refs
    maps, cells, channels, hid, taps, rows, parts, scale = dims
    padded = round_up(hid, LANES)
    own = hid // parts
    window = wide_up.shape[1]

    def copies(slot):
        if slot < 2:
            sources = (teach_up.at[slot], teach_dw, teach_down.at[slot])
            targets = (up_buf.at[slot], dw_buf, down_buf.at[slot])
        else:
            sources = (cand_up.at[0], cand_dw, cand_down.at[0])
            targets = (up_buf.at[slot], cand_dw_buf, down_buf.at[slot])
        if slot == 1:
            sources, targets = sources[::2], targets[::2]
        return [
            pltpu.make_async_copy(src, dst, sems.at[slot, n])
            for n, (src, dst) in enumerate(zip(sources, targets))
        ]

    for slot in (0, 2, 1):
        for copy in copies(slot):
            copy.start()

    analysis = analysis_ref[...]
    even, odd = even_ref[...], odd_ref[...]
    spectrum = spectrum_ref[...]
    dw_pad[...] = jnp.zeros_like(dw_pad)

    half_cells = cells // 2
    bases = [min(p * own // LANES * LANES, padded - window) for p in range(parts)]
    start = place_ref[1] * own
    base = jnp.minimum(start // LANES * LANES, padded - window)

    def synthesis(re, im):
        same, other = dot(even, re.astype(BF16)), dot(odd, im.astype(BF16))
        return jnp.concatenate([same + other, same - other], axis=0)

    def tap_spectrum(slot, cols):
        weights = dw_pad[slot, :, cols]
        high = weights.astype(BF16)
        low = (weights - high.astype(F32)).astype(BF16)
        both = dot(spectrum, jnp.concatenate([high, low, high], axis=0))
        return both[:rows], both[rows:]

    def load(slot, mask_taps):
        for copy in copies(slot):
            copy.wait()
        weights = cand_dw_buf[:, 0] if slot == 2 else dw_buf[:, slot]
        if mask_taps:
            side = int(round(taps**0.5))
            index = lax.broadcasted_iota(jnp.int32, weights.shape, 0)
            row = sum((index >= side * n).astype(jnp.int32) for n in range(1, side))
            ring = jnp.maximum(jnp.abs(row - side // 2), jnp.abs(index - side * row - side // 2))
            unit = lax.broadcasted_iota(jnp.int32, weights.shape, 1)
            keep = (ring <= radius_ref[0]) & (unit < half_ref[0] * (hid // 2))
            weights = jnp.where(keep, weights, 0.0)
        dw_pad[slot, :taps, :hid] = weights

    def forward(slot, lhs, up, down, cols, save, results):
        keep = save is not None
        pre = dot(lhs[...], up[:, cols])
        yield
        half = 0.5 * pre
        bend = jnp.tanh(half)
        more = 1.0 + bend
        wide = half * more
        units = wide.astype(BF16)
        if keep:
            slope_e[:, save] = (more + wide - wide * bend).astype(BF16)
        yield
        tap_re, tap_im = tap_spectrum(slot, cols)
        acts = []
        for m in range(maps):
            here = slice(m * cells, (m + 1) * cells)
            both = dot(analysis, units[here])
            yield
            re, im = both[:rows], both[rows:]
            if keep:
                spec[m, :, save] = both.astype(BF16)
            mixed_re, mixed_im = re * tap_re - im * tap_im, re * tap_im + im * tap_re
            yield
            mixed = synthesis(mixed_re, mixed_im)
            yield
            half_k = 0.5 * mixed
            bend_k = jnp.tanh(half_k)
            more_k = 1.0 + bend_k
            wide_k = half_k * more_k
            acts.append(wide_k.astype(BF16))
            if keep:
                act[here, save] = acts[-1]
                slope_k[here, save] = (more_k + wide_k - wide_k * bend_k).astype(BF16)
        yield
        results.append(dot_nt(jnp.concatenate(acts, axis=0), down[:, cols]))

    def teacher(slot, lhs, results):
        bounds = list(range(0, max(hid - UNIT // 2, 1), UNIT)) + [hid]
        return [
            forward(slot, lhs, up_buf.at[slot], down_buf.at[slot], slice(lo, hi), None, results)
            for lo, hi in zip(bounds, bounds[1:])
        ]

    def aligned(at, width):
        return pl.ds(pl.multiple_of(at, LANES), width)

    def candidate(lhs, results):
        units = []
        for at in range(0, window, BACK_UNIT):
            width = min(BACK_UNIT, window - at)
            cols = aligned(base + at, width)
            units.append(forward(2, lhs, up_pad, down_pad, cols, slice(at, at + width), results))
        step = max(w for w in (LANES, 2 * LANES, UNIT) if all(b % w == 0 for b in bases))
        for at in range(0, padded - window, step):
            cols = aligned(jnp.where(at < base, at, at + window), min(step, padded - window - at))
            units.append(forward(2, lhs, up_pad, down_pad, cols, None, results))
        return units

    whole_turn = (
        lax.broadcasted_iota(jnp.int32, (half_cells, half_cells), 0)
        + lax.broadcasted_iota(jnp.int32, (half_cells, half_cells), 1)
    ) == half_cells - 1
    turn_half = whole_turn.astype(F32).astype(BF16)
    for x_ref, offset in zip(x_refs, offsets):
        if offset is None:
            x_first[...] = x_ref[...]
            continue
        block = x_ref.shape[1]
        for n, (mask, distance) in enumerate(offset):
            source = (place_ref[0] & mask) ^ distance
            source = (source & (parts - 1)) * (cells // block) + (source >> (parts.bit_length() - 1))
            at = pl.multiple_of(source * block, block)
            x_first[pl.ds(at, block), :] = x_ref[n]
    for m in range(maps):
        second = slice(m * cells + half_cells, (m + 1) * cells)
        x_first[second] = dot(turn_half, x_first[second]).astype(BF16)
    load(0, False)
    first = []
    interleave(teacher(0, x_first, first))
    branch = sum(first)
    x_next[...] = (x_first[...].astype(F32) + branch).astype(BF16)
    x_now[...] = jnp.where(layer_ref[0] == 0, x_first[...], x_next[...])
    target[...] = branch
    load(2, True)
    load(1, False)
    for pad, buf in ((up_pad, up_buf), (down_pad, down_buf)):
        pad[:, hid // LANES * LANES :] = jnp.zeros((channels, padded - hid // LANES * LANES), BF16)
        pad[:, :hid] = buf[2]
    second, third = [], []
    units = [teacher(1, x_next, second), candidate(x_now, third)]
    interleave([unit for pair in itertools.zip_longest(*units) for unit in pair if unit is not None])
    err = (sum(third) - jnp.where(layer_ref[0] == 0, target[...], sum(second))) * scale
    err_now[...] = (0.5 * err).astype(BF16)
    err_turned[...] = jnp.transpose(err).astype(BF16)
    x_turned[...] = jnp.transpose(0.5 * x_now[...].astype(F32)).astype(BF16)

    def back(at, width):
        cols = aligned(base + at, width)
        here = slice(at, at + width)
        grad_act = dot(err_now[...], down_pad[:, cols])
        wide_down[:, here] = dot(err_turned[...], act[:, here])
        yield
        grad_k = (grad_act * slope_k[:, here].astype(F32)).astype(BF16)
        yield
        tap_re, tap_im = tap_spectrum(2, cols)
        sum_re = sum_im = 0.0
        grad_pre = []
        for m in range(maps):
            rows_here = slice(m * cells, (m + 1) * cells)
            both = dot(analysis, grad_k[rows_here])
            yield
            re, im = both[:rows], both[rows:]
            kept = spec[m, :, here].astype(F32)
            e_re, e_im = kept[:rows], kept[rows:]
            sum_re += re * e_re + im * e_im
            sum_im += re * e_im - im * e_re
            mixed_re, mixed_im = re * tap_re + im * tap_im, im * tap_re - re * tap_im
            yield
            grad_e = synthesis(mixed_re, mixed_im)
            yield
            grad_pre.append((grad_e * slope_e[rows_here, here].astype(F32)).astype(BF16))
        yield
        wide_up[:, here] = dot(x_turned[...], jnp.concatenate(grad_pre, axis=0))
        sums = jnp.concatenate([sum_re, sum_im], axis=0).astype(BF16)
        wide_dw[:, here] = dot(gather_ref[...], sums)

    interleave([back(at, min(BACK_UNIT, window - at)) for at in range(0, window, BACK_UNIT)])

    offset = start - base
    turn = lax.rem(window - offset, window)
    grad_up[0] = pltpu.roll(wide_up[...], turn, 1)[:, :own]
    grad_down[0] = pltpu.roll(wide_down[...], turn, 1)[:, :own]
    rolled = pltpu.roll(wide_dw[...], turn, 1)[:taps, :own]
    side = int(round(taps**0.5))
    index = lax.broadcasted_iota(jnp.int32, rolled.shape, 0)
    row = sum((index >= side * n).astype(jnp.int32) for n in range(1, side))
    ring = jnp.maximum(jnp.abs(row - side // 2), jnp.abs(index - side * row - side // 2))
    unit = lax.broadcasted_iota(jnp.int32, rolled.shape, 1) + start
    keep = (ring <= radius_ref[0]) & (unit < half_ref[0] * (hid // 2))
    grad_dw[:, 0] = jnp.where(keep, rolled, 0.0)


def local_grads(pieces, offsets, maps, layer, half, radius, place, parts, images, weights):
    teach_up, teach_dw, teach_down, cand_up, cand_dw, cand_down = weights
    weights = (teach_up, teach_dw.transpose(1, 0, 2), teach_down, cand_up, cand_dw.transpose(1, 0, 2), cand_down)
    channels, hid = teach_up.shape[1:]
    taps = teach_dw.shape[1]
    count = sum(piece.size for piece in pieces) // channels
    cells = count // maps
    side = int(round(cells**0.5))
    rows, constants = dft_matrices(side, taps)
    padded = round_up(hid, LANES)
    own = hid // parts
    spare = max((p * own) % LANES for p in range(parts))
    window = min(round_up(own + spare, LANES), padded)
    tap_rows = round_up(taps, 16)
    dims = (maps, cells, channels, hid, taps, rows, parts, 1.0 / images)
    smem = pl.BlockSpec(memory_space=pltpu.SMEM)
    vmem = pl.BlockSpec(memory_space=pltpu.VMEM)
    anywhere = pl.BlockSpec(memory_space=pl.ANY)
    grad_up, grad_dw, grad_down = pl.pallas_call(
        functools.partial(grads_kernel, dims, offsets),
        out_shape=(
            jax.ShapeDtypeStruct((1, channels, own), F32),
            jax.ShapeDtypeStruct((taps, 1, own), F32),
            jax.ShapeDtypeStruct((1, channels, own), F32),
        ),
        in_specs=[smem] * 4 + [vmem] * (len(pieces) + 5) + [anywhere] * 6,
        out_specs=(vmem, vmem, vmem),
        scratch_shapes=[
            pltpu.VMEM((3, channels, hid), BF16),
            pltpu.VMEM(weights[1].shape, F32),
            pltpu.VMEM(weights[4].shape, F32),
            pltpu.VMEM((3, channels, hid), BF16),
            pltpu.VMEM((3, tap_rows, padded), F32),
            pltpu.VMEM((channels, padded), BF16),
            pltpu.VMEM((channels, padded), BF16),
            pltpu.VMEM((count, window), BF16),
            pltpu.VMEM((maps, 2 * rows, window), BF16),
            pltpu.VMEM((count, window), BF16),
            pltpu.VMEM((count, window), BF16),
            pltpu.VMEM((count, channels), BF16),
            pltpu.VMEM((count, channels), BF16),
            pltpu.VMEM((count, channels), BF16),
            pltpu.VMEM((channels, count), BF16),
            pltpu.VMEM((count, channels), BF16),
            pltpu.VMEM((channels, count), BF16),
            pltpu.VMEM((count, channels), F32),
            pltpu.VMEM((channels, window), F32),
            pltpu.VMEM((tap_rows, window), F32),
            pltpu.VMEM((channels, window), F32),
            pltpu.SemaphoreType.DMA((3, 3)),
        ],
        compiler_params=pltpu.CompilerParams(vmem_limit_bytes=40 * 2**20),
        cost_estimate=pl.CostEstimate(
            flops=20 * count * channels * hid, bytes_accessed=12 * channels * hid, transcendentals=6 * count * hid
        ),
    )(layer, half, radius, place, *pieces, *constants, *weights)
    return grad_up, grad_dw.transpose(1, 0, 2), grad_down


def spread(block, cands, parts):
    sent = jnp.broadcast_to(block, (cands, *block.shape[1:]))
    image = lax.all_to_all(sent, "cand", split_axis=0, concat_axis=0, tiled=True)
    pieces, offsets = [image], [[(parts - 1, c * parts) for c in range(cands)]]
    for d in range(1, parts):
        pieces.append(lax.ppermute(image, "img", [(source, source ^ d) for source in range(parts)]))
        offsets.append([(parts - 1, c * parts + d) for c in range(cands)])
    return pieces, offsets


def body(
    first_maps,
    layer_of,
    expand_half,
    radius,
    teach_up,
    teach_dw,
    teach_down,
    cand_up,
    cand_dw,
    cand_down,
):
    parts = lax.axis_size("img")
    cands = lax.axis_size("cand")
    devices = parts * cands
    batch, own_cells, channels = first_maps.shape
    images = parts * batch
    part = lax.axis_index("img")
    place = jnp.stack([lax.axis_index("cand") * parts + part, part])
    weights = (teach_up, teach_dw, teach_down, cand_up, cand_dw, cand_down)
    scalars = (layer_of, expand_half, radius, place, parts, images, weights)
    mine = first_maps.astype(BF16)
    if batch == 1 and images == 2 and own_cells % 16 == 0 and devices & (devices - 1) == 0:
        pieces, offsets = spread(mine, cands, parts)
        return local_grads(pieces, offsets, images, *scalars)
    whole = lax.all_gather(mine, ("img", "cand")).reshape(parts, cands, batch, own_cells, channels)
    whole = whole.transpose(0, 2, 1, 3, 4).reshape(images, -1, channels)
    group = 2 if images % 2 == 0 else 1
    total = None
    for first in range(0, images, group):
        pieces = [whole[first : first + group].reshape(-1, channels)]
        grads = local_grads(pieces, [None], group, *scalars)
        total = grads if total is None else tuple(a + b for a, b in zip(total, grads))
    return total


def solution(mesh):
    placed = (
        P("img", "cand", None),
        P("cand"),
        P("cand"),
        P("cand"),
        P(),
        P(),
        P(),
        P("cand", None, None),
        P("cand", None, None),
        P("cand", None, None),
    )
    return jax.shard_map(
        body,
        mesh=mesh,
        in_specs=placed,
        out_specs=(P("cand", None, "img"), P("cand", None, "img"), P("cand", None, "img")),
        check_vma=False,
    )
```

```python
import functools
import itertools

import jax
import jax.numpy as jnp
import ml_dtypes
import numpy as np
from jax import lax
from jax.experimental import pallas as pl
from jax.experimental.pallas import tpu as pltpu
from jax.sharding import PartitionSpec as P

F32 = jnp.float32
BF16 = jnp.bfloat16
LANES = 128
UNIT = 512
BACK_UNIT = 384
DEPTH = 2
STAGGER = 5


def round_up(value, step):
    return -(-value // step) * step


def dft_matrices(side, taps):
    width = int(round(taps**0.5))
    reach = width // 2
    period = side + reach
    kept = []
    for u in range(period):
        for v in range(period):
            if (u, v) <= ((-u) % period, (-v) % period):
                kept.append((u, v))
    freqs = np.array(kept)
    count = len(kept)
    rows = round_up(count, 8)
    mirrored = ((-freqs) % period == freqs).all(axis=1)
    weight = np.where(mirrored, 1.0, 2.0) / period**2
    cell = np.stack(np.meshgrid(np.arange(side), np.arange(side), indexing="ij"), -1).reshape(-1, 2)
    half = len(cell) // 2
    cell = np.concatenate([cell[:half], cell[half:][::-1]]) - (side - 1) / 2
    tap = np.stack(np.meshgrid(np.arange(width), np.arange(width), indexing="ij"), -1).reshape(-1, 2) - reach
    cell_angle = 2 * np.pi * (freqs @ cell.T) / period
    tap_angle = 2 * np.pi * ((freqs @ tap.T) % period) / period
    tap_rows = round_up(taps, 16)

    analysis = np.zeros((2 * rows, side * side))
    analysis[:count] = np.cos(cell_angle)
    analysis[rows : rows + count] = -np.sin(cell_angle)
    even = np.zeros((half, rows))
    even[:, :count] = (weight[:, None] * np.cos(cell_angle)).T[:half]
    odd = np.zeros((half, rows))
    odd[:, :count] = -(weight[:, None] * np.sin(cell_angle)).T[:half]
    spectrum = np.zeros((2 * rows, tap_rows))
    spectrum[:count, :taps] = np.cos(tap_angle)
    spectrum[rows : rows + count, :taps] = np.sin(tap_angle)
    gather = np.zeros((tap_rows, 2 * rows))
    gather[:taps, :count] = (weight[:, None] * np.cos(tap_angle)).T
    gather[:taps, rows : rows + count] = -(weight[:, None] * np.sin(tap_angle)).T

    coarse = spectrum.astype(ml_dtypes.bfloat16).astype(np.float64)
    spectrum = np.concatenate([coarse, coarse, spectrum - coarse], axis=1)
    return rows, [jnp.asarray(m.astype(ml_dtypes.bfloat16)) for m in (analysis, even, odd, spectrum, gather)]


def dot(a, b):
    return jnp.dot(a, b, preferred_element_type=F32)


def dot_nt(a, b):
    return lax.dot_general(a, b, (((1,), (1,)), ((), ())), preferred_element_type=F32)


def interleave(units):
    waiting, running = list(units), []
    turn = 0
    while waiting or running:
        if waiting and len(running) < DEPTH and turn % STAGGER == 0:
            running.append(waiting.pop(0))
        turn += 1
        for unit in list(running):
            try:
                next(unit)
            except StopIteration:
                running.remove(unit)


def grads_kernel(
    dims,
    offsets,
    layer_ref,
    half_ref,
    radius_ref,
    place_ref,
    *refs,
):
    pieces = len(offsets)
    in_hbm, refs, in_vmem = refs[: pieces + 5], refs[pieces + 5 : -pieces - 5], refs[-pieces - 5 :]
    (
    teach_up,
    teach_dw,
    teach_down,
    cand_up,
    cand_dw,
    cand_down,
    grad_up,
    grad_dw,
    grad_down,
    up_buf,
    dw_buf,
    cand_dw_buf,
    down_buf,
    dw_pad,
    up_pad,
    down_pad,
    act,
    spec,
    slope_e,
    slope_k,
    out_up,
    out_dw,
    out_down,
    x_first,
    x_next,
    x_now,
    x_turned,
    err_now,
    err_turned,
    target,
    wide_up,
    wide_dw,
    sems,
    in_sems,
    out_sems,
    ) = refs
    maps, cells, channels, hid, taps, rows, parts, scale = dims
    padded = round_up(hid, LANES)
    own = hid // parts
    window = wide_up.shape[1]

    def copies(slot):
        if slot < 2:
            sources = (teach_up.at[slot], teach_dw, teach_down.at[slot])
            targets = (up_buf.at[slot], dw_buf, down_buf.at[slot])
        else:
            sources = (cand_up.at[0], cand_dw, cand_down.at[0])
            targets = (up_buf.at[slot], cand_dw_buf, down_buf.at[slot])
        if slot == 1:
            sources, targets = sources[::2], targets[::2]
        return [
            pltpu.make_async_copy(src, dst, sems.at[slot, n])
            for n, (src, dst) in enumerate(zip(sources, targets))
        ]

    staged = [
        pltpu.make_async_copy(src, dst, in_sems.at[n]) for n, (src, dst) in enumerate(zip(in_hbm, in_vmem))
    ]
    x_refs, (analysis_ref, even_ref, odd_ref, spectrum_ref, gather_ref) = in_vmem[:pieces], in_vmem[pieces:]
    first_copies = copies(0)
    for copy in [first_copies[1], *staged, first_copies[0], first_copies[2], *copies(2), *copies(1)]:
        copy.start()

    dw_pad[...] = jnp.zeros_like(dw_pad)

    half_cells = cells // 2
    bases = [min(p * own // LANES * LANES, padded - window) for p in range(parts)]
    start = place_ref[1] * own
    base = jnp.minimum(start // LANES * LANES, padded - window)

    def synthesis(re, im):
        same, other = dot(even, re.astype(BF16)), dot(odd, im.astype(BF16))
        return jnp.concatenate([same + other, same - other], axis=0)

    def tap_spectrum(slot, cols):
        weights = dw_pad[slot, :, cols]
        high = weights.astype(BF16)
        low = (weights - high.astype(F32)).astype(BF16)
        both = dot(spectrum, jnp.concatenate([high, low, high], axis=0))
        return both[:rows], both[rows:]

    def load(slot, mask_taps):
        if slot != 1:
            copies(slot)[1].wait()
        weights = cand_dw_buf[:, 0] if slot == 2 else dw_buf[:, slot]
        if mask_taps:
            side = int(round(taps**0.5))
            index = lax.broadcasted_iota(jnp.int32, weights.shape, 0)
            row = sum((index >= side * n).astype(jnp.int32) for n in range(1, side))
            ring = jnp.maximum(jnp.abs(row - side // 2), jnp.abs(index - side * row - side // 2))
            unit = lax.broadcasted_iota(jnp.int32, weights.shape, 1)
            keep = (ring <= radius_ref[0]) & (unit < half_ref[0] * (hid // 2))
            weights = jnp.where(keep, weights, 0.0)
        dw_pad[slot, :taps, :hid] = weights

    def forward(slot, lhs, up, down, cols, save, results):
        keep = save is not None
        pre = dot(lhs[...], up[:, cols])
        yield
        half = 0.5 * pre
        bend = jnp.tanh(half)
        more = 1.0 + bend
        wide = half * more
        units = wide.astype(BF16)
        if keep:
            slope_e[:, save] = (more + wide - wide * bend).astype(BF16)
        yield
        tap_re, tap_im = tap_spectrum(slot, cols)
        acts = []
        for m in range(maps):
            here = slice(m * cells, (m + 1) * cells)
            both = dot(analysis, units[here])
            yield
            re, im = both[:rows], both[rows:]
            if keep:
                spec[m, :, save] = both.astype(BF16)
            mixed_re, mixed_im = re * tap_re - im * tap_im, re * tap_im + im * tap_re
            yield
            mixed = synthesis(mixed_re, mixed_im)
            yield
            half_k = 0.5 * mixed
            bend_k = jnp.tanh(half_k)
            more_k = 1.0 + bend_k
            wide_k = half_k * more_k
            acts.append(wide_k.astype(BF16))
            if keep:
                act[here, save] = acts[-1]
                slope_k[here, save] = (more_k + wide_k - wide_k * bend_k).astype(BF16)
        yield
        results.append(dot_nt(jnp.concatenate(acts, axis=0), down[:, cols]))

    def teacher(slot, lhs, results):
        bounds = list(range(0, max(hid - UNIT // 2, 1), UNIT)) + [hid]
        return [
            forward(slot, lhs, up_buf.at[slot], down_buf.at[slot], slice(lo, hi), None, results)
            for lo, hi in zip(bounds, bounds[1:])
        ]

    def aligned(at, width):
        return pl.ds(pl.multiple_of(at, LANES), width)

    def candidate(lhs, results):
        units = []
        for at in range(0, window, BACK_UNIT):
            width = min(BACK_UNIT, window - at)
            cols = aligned(base + at, width)
            units.append(forward(2, lhs, up_pad, down_pad, cols, slice(at, at + width), results))
        step = max(w for w in (LANES, 2 * LANES, UNIT) if all(b % w == 0 for b in bases))
        for at in range(0, padded - window, step):
            cols = aligned(jnp.where(at < base, at, at + window), min(step, padded - window - at))
            units.append(forward(2, lhs, up_pad, down_pad, cols, None, results))
        return units

    load(0, False)
    for copy in staged:
        copy.wait()
    analysis = analysis_ref[...]
    even, odd = even_ref[...], odd_ref[...]
    spectrum = spectrum_ref[...]
    whole_turn = (
        lax.broadcasted_iota(jnp.int32, (half_cells, half_cells), 0)
        + lax.broadcasted_iota(jnp.int32, (half_cells, half_cells), 1)
    ) == half_cells - 1
    turn_half = whole_turn.astype(F32).astype(BF16)
    for x_ref, offset in zip(x_refs, offsets):
        if offset is None:
            x_first[...] = x_ref[...]
            continue
        block = x_ref.shape[1]
        for n, distance in enumerate(offset):
            source = place_ref[0] ^ distance
            source = (source & (parts - 1)) * (cells // block) + (source >> (parts.bit_length() - 1))
            at = pl.multiple_of(source * block, block)
            x_first[pl.ds(at, block), :] = x_ref[n]
    for m in range(maps):
        second = slice(m * cells + half_cells, (m + 1) * cells)
        x_first[second] = dot(turn_half, x_first[second]).astype(BF16)
    for copy in copies(0)[::2]:
        copy.wait()
    first = []
    interleave(teacher(0, x_first, first))
    branch = sum(first)
    x_next[...] = (x_first[...].astype(F32) + branch).astype(BF16)
    x_now[...] = jnp.where(layer_ref[0] == 0, x_first[...], x_next[...])
    target[...] = branch
    load(2, True)
    load(1, False)
    for copy in copies(2)[::2] + copies(1):
        copy.wait()
    for pad, buf in ((up_pad, up_buf), (down_pad, down_buf)):
        pad[:, hid // LANES * LANES :] = jnp.zeros((channels, padded - hid // LANES * LANES), BF16)
        pad[:, :hid] = buf[2]
    second, third = [], []
    units = [teacher(1, x_next, second), candidate(x_now, third)]
    interleave([unit for pair in itertools.zip_longest(*units) for unit in pair if unit is not None])
    err = (sum(third) - jnp.where(layer_ref[0] == 0, target[...], sum(second))) * scale
    err_now[...] = (0.5 * err).astype(BF16)
    err_turned[...] = jnp.transpose(err).astype(BF16)
    x_turned[...] = jnp.transpose(0.5 * x_now[...].astype(F32)).astype(BF16)

    offset = start - base
    shifts = sorted({p * own - at for p, at in enumerate(bases)})

    def leave(wide, out, n, grad):
        for shift in shifts:
            @pl.when(offset == shift)
            def _():
                out[...] = wide[:, shift : shift + own]
        pltpu.make_async_copy(out, grad.at[0], out_sems.at[n]).start()

    wide_up[...] = dot(err_turned[...], act[...])
    leave(wide_up, out_down, 0, grad_down)

    def back(at, width):
        cols = aligned(base + at, width)
        here = slice(at, at + width)
        grad_act = dot(err_now[...], down_pad[:, cols])
        yield
        grad_k = (grad_act * slope_k[:, here].astype(F32)).astype(BF16)
        yield
        tap_re, tap_im = tap_spectrum(2, cols)
        sum_re = sum_im = 0.0
        grad_pre = []
        for m in range(maps):
            rows_here = slice(m * cells, (m + 1) * cells)
            both = dot(analysis, grad_k[rows_here])
            yield
            re, im = both[:rows], both[rows:]
            kept = spec[m, :, here].astype(F32)
            e_re, e_im = kept[:rows], kept[rows:]
            sum_re += re * e_re + im * e_im
            sum_im += re * e_im - im * e_re
            mixed_re, mixed_im = re * tap_re + im * tap_im, im * tap_re - re * tap_im
            yield
            grad_e = synthesis(mixed_re, mixed_im)
            yield
            grad_pre.append((grad_e * slope_e[rows_here, here].astype(F32)).astype(BF16))
        yield
        wide_up[:, here] = dot(x_turned[...], jnp.concatenate(grad_pre, axis=0))
        sums = jnp.concatenate([sum_re, sum_im], axis=0).astype(BF16)
        wide_dw[:, here] = dot(gather_ref[...], sums)

    interleave([back(at, min(BACK_UNIT, window - at)) for at in range(0, window, BACK_UNIT)])

    leave(wide_up, out_up, 1, grad_up)
    for shift in shifts:
        @pl.when(offset == shift)
        def _():
            own_dw = wide_dw[:taps, shift : shift + own]
            side = int(round(taps**0.5))
            index = lax.broadcasted_iota(jnp.int32, own_dw.shape, 0)
            row = sum((index >= side * n).astype(jnp.int32) for n in range(1, side))
            ring = jnp.maximum(jnp.abs(row - side // 2), jnp.abs(index - side * row - side // 2))
            unit = lax.broadcasted_iota(jnp.int32, own_dw.shape, 1) + start
            keep = (ring <= radius_ref[0]) & (unit < half_ref[0] * (hid // 2))
            out_dw[:, 0] = jnp.where(keep, own_dw, 0.0)
    pltpu.make_async_copy(out_dw, grad_dw, out_sems.at[2]).start()
    pltpu.make_async_copy(out_down, grad_down.at[0], out_sems.at[0]).wait()
    pltpu.make_async_copy(out_up, grad_up.at[0], out_sems.at[1]).wait()
    pltpu.make_async_copy(out_dw, grad_dw, out_sems.at[2]).wait()


def local_grads(pieces, offsets, maps, layer, half, radius, place, parts, images, weights):
    teach_up, teach_dw, teach_down, cand_up, cand_dw, cand_down = weights
    weights = (teach_up, teach_dw.transpose(1, 0, 2), teach_down, cand_up, cand_dw.transpose(1, 0, 2), cand_down)
    channels, hid = teach_up.shape[1:]
    taps = teach_dw.shape[1]
    count = sum(piece.size for piece in pieces) // channels
    cells = count // maps
    side = int(round(cells**0.5))
    rows, constants = dft_matrices(side, taps)
    padded = round_up(hid, LANES)
    own = hid // parts
    spare = max((p * own) % LANES for p in range(parts))
    window = min(round_up(own + spare, LANES), padded)
    tap_rows = round_up(taps, 16)
    dims = (maps, cells, channels, hid, taps, rows, parts, 1.0 / images)
    smem = pl.BlockSpec(memory_space=pltpu.SMEM)
    anywhere = pl.BlockSpec(memory_space=pl.ANY)
    grad_up, grad_dw, grad_down = pl.pallas_call(
        functools.partial(grads_kernel, dims, offsets),
        out_shape=(
            jax.ShapeDtypeStruct((1, channels, own), F32),
            jax.ShapeDtypeStruct((taps, 1, own), F32),
            jax.ShapeDtypeStruct((1, channels, own), F32),
        ),
        in_specs=[smem] * 4 + [anywhere] * (len(pieces) + 11),
        out_specs=(anywhere, anywhere, anywhere),
        scratch_shapes=[
            pltpu.VMEM((3, channels, hid), BF16),
            pltpu.VMEM(weights[1].shape, F32),
            pltpu.VMEM(weights[4].shape, F32),
            pltpu.VMEM((3, channels, hid), BF16),
            pltpu.VMEM((3, tap_rows, padded), F32),
            pltpu.VMEM((channels, padded), BF16),
            pltpu.VMEM((channels, padded), BF16),
            pltpu.VMEM((count, window), BF16),
            pltpu.VMEM((maps, 2 * rows, window), BF16),
            pltpu.VMEM((count, window), BF16),
            pltpu.VMEM((count, window), BF16),
            pltpu.VMEM((channels, own), F32),
            pltpu.VMEM((taps, 1, own), F32),
            pltpu.VMEM((channels, own), F32),
            pltpu.VMEM((count, channels), BF16),
            pltpu.VMEM((count, channels), BF16),
            pltpu.VMEM((count, channels), BF16),
            pltpu.VMEM((channels, count), BF16),
            pltpu.VMEM((count, channels), BF16),
            pltpu.VMEM((channels, count), BF16),
            pltpu.VMEM((count, channels), F32),
            pltpu.VMEM((channels, window), F32),
            pltpu.VMEM((tap_rows, window), F32),
            pltpu.SemaphoreType.DMA((3, 3)),
            pltpu.SemaphoreType.DMA((len(pieces) + len(constants),)),
            pltpu.SemaphoreType.DMA((3,)),
            *[pltpu.VMEM(array.shape, BF16) for array in (*pieces, *constants)],
        ],
        compiler_params=pltpu.CompilerParams(vmem_limit_bytes=60 * 2**20),
        cost_estimate=pl.CostEstimate(
            flops=20 * count * channels * hid, bytes_accessed=12 * channels * hid, transcendentals=6 * count * hid
        ),
    )(layer, half, radius, place, *pieces, *constants, *weights)
    return grad_up, grad_dw.transpose(1, 0, 2), grad_down


def exchange(block, masks, devices):
    offset = [0]
    for mask in masks:
        distances = [d for d in range(1, devices) if d & ~mask == 0]
        parts = [block] + [
            lax.ppermute(block, ("cand", "img"), [(source, source ^ d) for source in range(devices)])
            for d in distances
        ]
        pieces = [[o ^ d for o in offset] for d in [0] + distances]
        offset = sum(pieces, [])
        if mask != masks[-1]:
            block = jnp.concatenate(parts, axis=0)
    return parts, pieces


def body(
    first_maps,
    layer_of,
    expand_half,
    radius,
    teach_up,
    teach_dw,
    teach_down,
    cand_up,
    cand_dw,
    cand_down,
):
    parts = lax.axis_size("img")
    cands = lax.axis_size("cand")
    devices = parts * cands
    batch, own_cells, channels = first_maps.shape
    images = parts * batch
    part = lax.axis_index("img")
    place = jnp.stack([lax.axis_index("cand") * parts + part, part])
    weights = (teach_up, teach_dw, teach_down, cand_up, cand_dw, cand_down)
    scalars = (layer_of, expand_half, radius, place, parts, images, weights)
    mine = first_maps.astype(BF16)
    if batch == 1 and images == 2 and own_cells % 16 == 0 and devices & (devices - 1) == 0:
        near = parts * min(2, cands) - 1
        pieces, offsets = exchange(mine, [(devices - 1) & ~near, near], devices)
        return local_grads(pieces, offsets, images, *scalars)
    whole = lax.all_gather(mine, ("img", "cand")).reshape(parts, cands, batch, own_cells, channels)
    whole = whole.transpose(0, 2, 1, 3, 4).reshape(images, -1, channels)
    group = 2 if images % 2 == 0 else 1
    total = None
    for first in range(0, images, group):
        pieces = [whole[first : first + group].reshape(-1, channels)]
        grads = local_grads(pieces, [None], group, *scalars)
        total = grads if total is None else tuple(a + b for a, b in zip(total, grads))
    return total


def solution(mesh):
    placed = (
        P("img", "cand", None),
        P("cand"),
        P("cand"),
        P("cand"),
        P(),
        P(),
        P(),
        P("cand", None, None),
        P("cand", None, None),
        P("cand", None, None),
    )
    return jax.shard_map(
        body,
        mesh=mesh,
        in_specs=placed,
        out_specs=(P("cand", None, "img"), P("cand", None, "img"), P("cand", None, "img")),
        check_vma=False,
    )
```

```python
import functools
import itertools

import jax
import jax.numpy as jnp
import ml_dtypes
import numpy as np
from jax import lax
from jax.experimental import pallas as pl
from jax.experimental.pallas import tpu as pltpu
from jax.sharding import PartitionSpec as P

F32 = jnp.float32
BF16 = jnp.bfloat16
LANES = 128
UNIT = 512
BACK_UNIT = 384
DEPTH = 2
STAGGER = 5


def round_up(value, step):
    return -(-value // step) * step


def dft_matrices(side, taps):
    width = int(round(taps**0.5))
    reach = width // 2
    period = side + reach
    kept = []
    for u in range(period):
        for v in range(period):
            if (u, v) <= ((-u) % period, (-v) % period):
                kept.append((u, v))
    freqs = np.array(kept)
    count = len(kept)
    rows = round_up(count, 8)
    mirrored = ((-freqs) % period == freqs).all(axis=1)
    weight = np.where(mirrored, 1.0, 2.0) / period**2
    cell = np.stack(np.meshgrid(np.arange(side), np.arange(side), indexing="ij"), -1).reshape(-1, 2)
    half = len(cell) // 2
    cell = np.concatenate([cell[:half], cell[half:][::-1]]) - (side - 1) / 2
    tap = np.stack(np.meshgrid(np.arange(width), np.arange(width), indexing="ij"), -1).reshape(-1, 2) - reach
    cell_angle = 2 * np.pi * (freqs @ cell.T) / period
    tap_angle = 2 * np.pi * ((freqs @ tap.T) % period) / period
    tap_rows = round_up(taps, 16)

    analysis = np.zeros((2 * rows, side * side))
    analysis[:count] = np.cos(cell_angle)
    analysis[rows : rows + count] = -np.sin(cell_angle)
    even = np.zeros((half, rows))
    even[:, :count] = (weight[:, None] * np.cos(cell_angle)).T[:half]
    odd = np.zeros((half, rows))
    odd[:, :count] = -(weight[:, None] * np.sin(cell_angle)).T[:half]
    spectrum = np.zeros((2 * rows, tap_rows))
    spectrum[:count, :taps] = np.cos(tap_angle)
    spectrum[rows : rows + count, :taps] = np.sin(tap_angle)
    gather_re, gather_im = np.zeros((tap_rows, rows)), np.zeros((tap_rows, rows))
    gather_re[:taps, :count] = (weight[:, None] * np.cos(tap_angle)).T
    gather_im[:taps, :count] = -(weight[:, None] * np.sin(tap_angle)).T

    coarse = spectrum.astype(ml_dtypes.bfloat16).astype(np.float64)
    spectrum = np.concatenate([coarse, coarse, spectrum - coarse], axis=1)
    matrices = (analysis, even, odd, spectrum, gather_re, gather_im)
    return rows, [jnp.asarray(m.astype(ml_dtypes.bfloat16)) for m in matrices]


def dot(a, b):
    return jnp.dot(a, b, preferred_element_type=F32)


def dot_nt(a, b):
    return lax.dot_general(a, b, (((1,), (1,)), ((), ())), preferred_element_type=F32)


def interleave(units):
    waiting, running = list(units), []
    turn = 0
    while waiting or running:
        if waiting and len(running) < DEPTH and turn % STAGGER == 0:
            running.append(waiting.pop(0))
        turn += 1
        for unit in list(running):
            try:
                next(unit)
            except StopIteration:
                running.remove(unit)


def grads_kernel(
    dims,
    offsets,
    layer_ref,
    half_ref,
    radius_ref,
    place_ref,
    *refs,
):
    pieces = len(offsets)
    in_hbm, refs, in_vmem = refs[: pieces + 6], refs[pieces + 6 : -pieces - 6], refs[-pieces - 6 :]
    (
    teach_up,
    teach_dw,
    teach_down,
    cand_up,
    cand_dw,
    cand_down,
    grad_up,
    grad_dw,
    grad_down,
    up_buf,
    dw_buf,
    cand_dw_buf,
    down_buf,
    dw_pad,
    up_pad,
    down_pad,
    act,
    spec,
    slope_e,
    slope_k,
    out_up,
    out_dw,
    out_down,
    x_first,
    x_next,
    x_now,
    x_turned,
    err_now,
    err_turned,
    target,
    wide_up,
    wide_dw,
    sems,
    in_sems,
    out_sems,
    ) = refs
    maps, cells, channels, hid, taps, rows, parts, scale = dims
    padded = round_up(hid, LANES)
    own = hid // parts
    window = wide_up.shape[1]

    def copies(slot):
        if slot < 2:
            sources = (teach_up.at[slot], teach_dw, teach_down.at[slot])
            targets = (up_buf.at[slot], dw_buf, down_buf.at[slot])
        else:
            sources = (cand_up.at[0], cand_dw, cand_down.at[0])
            targets = (up_buf.at[slot], cand_dw_buf, down_buf.at[slot])
        if slot == 1:
            sources, targets = sources[::2], targets[::2]
        return [
            pltpu.make_async_copy(src, dst, sems.at[slot, n])
            for n, (src, dst) in enumerate(zip(sources, targets))
        ]

    staged = [
        pltpu.make_async_copy(src, dst, in_sems.at[n]) for n, (src, dst) in enumerate(zip(in_hbm, in_vmem))
    ]
    x_refs, constants = in_vmem[:pieces], in_vmem[pieces:]
    first_copies = copies(0)
    for copy in [first_copies[1], *staged, first_copies[0], first_copies[2], *copies(2), *copies(1)]:
        copy.start()

    dw_pad[...] = jnp.zeros_like(dw_pad)

    half_cells = cells // 2
    bases = [min(p * own // LANES * LANES, padded - window) for p in range(parts)]
    start = place_ref[1] * own
    base = jnp.minimum(start // LANES * LANES, padded - window)

    def split(both):
        return both[:rows].astype(BF16), both[rows:].astype(BF16)

    def synthesis(re, im):
        same, other = dot(even, re), dot(odd, im)
        return jnp.concatenate([same + other, same - other], axis=0)

    def tap_spectrum(slot, cols):
        weights = dw_pad[slot, :, cols]
        high = weights.astype(BF16)
        low = (weights - high.astype(F32)).astype(BF16)
        return split(dot(spectrum, jnp.concatenate([high, low, high], axis=0)))

    def load(slot, mask_taps):
        if slot != 1:
            copies(slot)[1].wait()
        weights = cand_dw_buf[:, 0] if slot == 2 else dw_buf[:, slot]
        if mask_taps:
            side = int(round(taps**0.5))
            index = lax.broadcasted_iota(jnp.int32, weights.shape, 0)
            row = sum((index >= side * n).astype(jnp.int32) for n in range(1, side))
            ring = jnp.maximum(jnp.abs(row - side // 2), jnp.abs(index - side * row - side // 2))
            unit = lax.broadcasted_iota(jnp.int32, weights.shape, 1)
            keep = (ring <= radius_ref[0]) & (unit < half_ref[0] * (hid // 2))
            weights = jnp.where(keep, weights, 0.0)
        dw_pad[slot, :taps, :hid] = weights

    def forward(slot, lhs, up, down, cols, save, results):
        keep = save is not None
        pre = dot(lhs[...], up[:, cols])
        yield
        half = 0.5 * pre
        bend = jnp.tanh(half)
        more = 1.0 + bend
        wide = half * more
        units = wide.astype(BF16)
        if keep:
            slope_e[:, save] = (more + wide - wide * bend).astype(BF16)
        yield
        tap_re, tap_im = tap_spectrum(slot, cols)
        acts = []
        for m in range(maps):
            here = slice(m * cells, (m + 1) * cells)
            both = dot(analysis, units[here])
            yield
            re, im = split(both)
            if keep:
                spec[m, 0, :, save], spec[m, 1, :, save] = re, im
            mixed_re, mixed_im = re * tap_re - im * tap_im, re * tap_im + im * tap_re
            yield
            mixed = synthesis(mixed_re, mixed_im)
            yield
            half_k = 0.5 * mixed
            bend_k = jnp.tanh(half_k)
            more_k = 1.0 + bend_k
            wide_k = half_k * more_k
            acts.append(wide_k.astype(BF16))
            if keep:
                act[here, save] = acts[-1]
                slope_k[here, save] = (more_k + wide_k - wide_k * bend_k).astype(BF16)
        yield
        results.append(dot_nt(jnp.concatenate(acts, axis=0), down[:, cols]))

    def teacher(slot, lhs, results):
        bounds = list(range(0, max(hid - UNIT // 2, 1), UNIT)) + [hid]
        return [
            forward(slot, lhs, up_buf.at[slot], down_buf.at[slot], slice(lo, hi), None, results)
            for lo, hi in zip(bounds, bounds[1:])
        ]

    def aligned(at, width):
        return pl.ds(pl.multiple_of(at, LANES), width)

    def candidate(lhs, results):
        units = []
        for at in range(0, window, BACK_UNIT):
            width = min(BACK_UNIT, window - at)
            cols = aligned(base + at, width)
            units.append(forward(2, lhs, up_pad, down_pad, cols, slice(at, at + width), results))
        step = max(w for w in (LANES, 2 * LANES, UNIT) if all(b % w == 0 for b in bases))
        for at in range(0, padded - window, step):
            cols = aligned(jnp.where(at < base, at, at + window), min(step, padded - window - at))
            units.append(forward(2, lhs, up_pad, down_pad, cols, None, results))
        return units

    load(0, False)
    for copy in staged:
        copy.wait()
    analysis, even, odd, spectrum, gather_re, gather_im = (ref[...] for ref in constants)
    whole_turn = (
        lax.broadcasted_iota(jnp.int32, (half_cells, half_cells), 0)
        + lax.broadcasted_iota(jnp.int32, (half_cells, half_cells), 1)
    ) == half_cells - 1
    turn_half = whole_turn.astype(F32).astype(BF16)
    for x_ref, offset in zip(x_refs, offsets):
        if offset is None:
            x_first[...] = x_ref[...]
            continue
        block = x_ref.shape[1]
        for n, distance in enumerate(offset):
            source = place_ref[0] ^ distance
            source = (source & (parts - 1)) * (cells // block) + (source >> (parts.bit_length() - 1))
            at = pl.multiple_of(source * block, block)
            x_first[pl.ds(at, block), :] = x_ref[n]
    for m in range(maps):
        second = slice(m * cells + half_cells, (m + 1) * cells)
        x_first[second] = dot(turn_half, x_first[second]).astype(BF16)
    for copy in copies(0)[::2]:
        copy.wait()
    first = []
    interleave(teacher(0, x_first, first))
    branch = sum(first)
    x_next[...] = (x_first[...].astype(F32) + branch).astype(BF16)
    x_now[...] = jnp.where(layer_ref[0] == 0, x_first[...], x_next[...])
    target[...] = branch
    load(2, True)
    load(1, False)
    for copy in copies(2)[::2] + copies(1):
        copy.wait()
    for pad, buf in ((up_pad, up_buf), (down_pad, down_buf)):
        pad[:, hid // LANES * LANES :] = jnp.zeros((channels, padded - hid // LANES * LANES), BF16)
        pad[:, :hid] = buf[2]
    second, third = [], []
    units = [teacher(1, x_next, second), candidate(x_now, third)]
    interleave([unit for pair in itertools.zip_longest(*units) for unit in pair if unit is not None])
    err = (sum(third) - jnp.where(layer_ref[0] == 0, target[...], sum(second))) * scale
    err_now[...] = (0.5 * err).astype(BF16)
    err_turned[...] = jnp.transpose(err).astype(BF16)
    x_turned[...] = jnp.transpose(0.5 * x_now[...].astype(F32)).astype(BF16)

    offset = start - base
    shifts = sorted({p * own - at for p, at in enumerate(bases)})

    def leave(wide, out, n, grad):
        for shift in shifts:
            @pl.when(offset == shift)
            def _():
                out[...] = wide[:, shift : shift + own]
        pltpu.make_async_copy(out, grad.at[0], out_sems.at[n]).start()

    wide_up[...] = dot(err_turned[...], act[...])
    leave(wide_up, out_down, 0, grad_down)

    def back(at, width):
        cols = aligned(base + at, width)
        here = slice(at, at + width)
        grad_act = dot(err_now[...], down_pad[:, cols])
        yield
        grad_k = grad_act.astype(BF16) * slope_k[:, here]
        yield
        tap_re, tap_im = tap_spectrum(2, cols)
        sum_re, sum_im = [], []
        grad_pre = []
        for m in range(maps):
            rows_here = slice(m * cells, (m + 1) * cells)
            both = dot(analysis, grad_k[rows_here])
            yield
            re, im = split(both)
            e_re, e_im = spec[m, 0, :, here], spec[m, 1, :, here]
            sum_re.append(re * e_re + im * e_im)
            sum_im.append(re * e_im - im * e_re)
            mixed_re, mixed_im = re * tap_re + im * tap_im, im * tap_re - re * tap_im
            yield
            grad_e = synthesis(mixed_re, mixed_im)
            yield
            grad_pre.append(grad_e.astype(BF16) * slope_e[rows_here, here])
        yield
        wide_up[:, here] = dot(x_turned[...], jnp.concatenate(grad_pre, axis=0))
        wide_dw[:, here] = dot(gather_re, sum(sum_re[1:], sum_re[0])) + dot(gather_im, sum(sum_im[1:], sum_im[0]))

    interleave([back(at, min(BACK_UNIT, window - at)) for at in range(0, window, BACK_UNIT)])

    leave(wide_up, out_up, 1, grad_up)
    for shift in shifts:
        @pl.when(offset == shift)
        def _():
            own_dw = wide_dw[:taps, shift : shift + own]
            side = int(round(taps**0.5))
            index = lax.broadcasted_iota(jnp.int32, own_dw.shape, 0)
            row = sum((index >= side * n).astype(jnp.int32) for n in range(1, side))
            ring = jnp.maximum(jnp.abs(row - side // 2), jnp.abs(index - side * row - side // 2))
            unit = lax.broadcasted_iota(jnp.int32, own_dw.shape, 1) + start
            keep = (ring <= radius_ref[0]) & (unit < half_ref[0] * (hid // 2))
            out_dw[:, 0] = jnp.where(keep, own_dw, 0.0)
    pltpu.make_async_copy(out_dw, grad_dw, out_sems.at[2]).start()
    pltpu.make_async_copy(out_down, grad_down.at[0], out_sems.at[0]).wait()
    pltpu.make_async_copy(out_up, grad_up.at[0], out_sems.at[1]).wait()
    pltpu.make_async_copy(out_dw, grad_dw, out_sems.at[2]).wait()


def local_grads(pieces, offsets, maps, layer, half, radius, place, parts, images, weights):
    teach_up, teach_dw, teach_down, cand_up, cand_dw, cand_down = weights
    weights = (teach_up, teach_dw.transpose(1, 0, 2), teach_down, cand_up, cand_dw.transpose(1, 0, 2), cand_down)
    channels, hid = teach_up.shape[1:]
    taps = teach_dw.shape[1]
    count = sum(piece.size for piece in pieces) // channels
    cells = count // maps
    side = int(round(cells**0.5))
    rows, constants = dft_matrices(side, taps)
    padded = round_up(hid, LANES)
    own = hid // parts
    spare = max((p * own) % LANES for p in range(parts))
    window = min(round_up(own + spare, LANES), padded)
    tap_rows = round_up(taps, 16)
    dims = (maps, cells, channels, hid, taps, rows, parts, 1.0 / images)
    smem = pl.BlockSpec(memory_space=pltpu.SMEM)
    anywhere = pl.BlockSpec(memory_space=pl.ANY)
    grad_up, grad_dw, grad_down = pl.pallas_call(
        functools.partial(grads_kernel, dims, offsets),
        out_shape=(
            jax.ShapeDtypeStruct((1, channels, own), F32),
            jax.ShapeDtypeStruct((taps, 1, own), F32),
            jax.ShapeDtypeStruct((1, channels, own), F32),
        ),
        in_specs=[smem] * 4 + [anywhere] * (len(pieces) + 12),
        out_specs=(anywhere, anywhere, anywhere),
        scratch_shapes=[
            pltpu.VMEM((3, channels, hid), BF16),
            pltpu.VMEM(weights[1].shape, F32),
            pltpu.VMEM(weights[4].shape, F32),
            pltpu.VMEM((3, channels, hid), BF16),
            pltpu.VMEM((3, tap_rows, padded), F32),
            pltpu.VMEM((channels, padded), BF16),
            pltpu.VMEM((channels, padded), BF16),
            pltpu.VMEM((count, window), BF16),
            pltpu.VMEM((maps, 2, rows, window), BF16),
            pltpu.VMEM((count, window), BF16),
            pltpu.VMEM((count, window), BF16),
            pltpu.VMEM((channels, own), F32),
            pltpu.VMEM((taps, 1, own), F32),
            pltpu.VMEM((channels, own), F32),
            pltpu.VMEM((count, channels), BF16),
            pltpu.VMEM((count, channels), BF16),
            pltpu.VMEM((count, channels), BF16),
            pltpu.VMEM((channels, count), BF16),
            pltpu.VMEM((count, channels), BF16),
            pltpu.VMEM((channels, count), BF16),
            pltpu.VMEM((count, channels), F32),
            pltpu.VMEM((channels, window), F32),
            pltpu.VMEM((tap_rows, window), F32),
            pltpu.SemaphoreType.DMA((3, 3)),
            pltpu.SemaphoreType.DMA((len(pieces) + len(constants),)),
            pltpu.SemaphoreType.DMA((3,)),
            *[pltpu.VMEM(array.shape, BF16) for array in (*pieces, *constants)],
        ],
        compiler_params=pltpu.CompilerParams(vmem_limit_bytes=60 * 2**20),
        cost_estimate=pl.CostEstimate(
            flops=20 * count * channels * hid, bytes_accessed=12 * channels * hid, transcendentals=6 * count * hid
        ),
    )(layer, half, radius, place, *pieces, *constants, *weights)
    return grad_up, grad_dw.transpose(1, 0, 2), grad_down


def exchange(block, masks, devices):
    offset = [0]
    for mask in masks:
        distances = [d for d in range(1, devices) if d & ~mask == 0]
        parts = [block] + [
            lax.ppermute(block, ("cand", "img"), [(source, source ^ d) for source in range(devices)])
            for d in distances
        ]
        pieces = [[o ^ d for o in offset] for d in [0] + distances]
        offset = sum(pieces, [])
        if mask != masks[-1]:
            block = jnp.concatenate(parts, axis=0)
    return parts, pieces


def body(
    first_maps,
    layer_of,
    expand_half,
    radius,
    teach_up,
    teach_dw,
    teach_down,
    cand_up,
    cand_dw,
    cand_down,
):
    parts = lax.axis_size("img")
    cands = lax.axis_size("cand")
    devices = parts * cands
    batch, own_cells, channels = first_maps.shape
    images = parts * batch
    part = lax.axis_index("img")
    place = jnp.stack([lax.axis_index("cand") * parts + part, part])
    weights = (teach_up, teach_dw, teach_down, cand_up, cand_dw, cand_down)
    scalars = (layer_of, expand_half, radius, place, parts, images, weights)
    mine = first_maps.astype(BF16)
    if batch == 1 and images == 2 and own_cells % 16 == 0 and devices & (devices - 1) == 0:
        core = parts if cands > 1 else 0
        bits = [1 << n for n in reversed(range(devices.bit_length() - 1))]
        pieces, offsets = exchange(mine, [b for b in bits if b != core] + [core] * (core > 0), devices)
        return local_grads(pieces, offsets, images, *scalars)
    whole = lax.all_gather(mine, ("img", "cand")).reshape(parts, cands, batch, own_cells, channels)
    whole = whole.transpose(0, 2, 1, 3, 4).reshape(images, -1, channels)
    group = 2 if images % 2 == 0 else 1
    total = None
    for first in range(0, images, group):
        pieces = [whole[first : first + group].reshape(-1, channels)]
        grads = local_grads(pieces, [None], group, *scalars)
        total = grads if total is None else tuple(a + b for a, b in zip(total, grads))
    return total


def solution(mesh):
    placed = (
        P("img", "cand", None),
        P("cand"),
        P("cand"),
        P("cand"),
        P(),
        P(),
        P(),
        P("cand", None, None),
        P("cand", None, None),
        P("cand", None, None),
    )
    return jax.shard_map(
        body,
        mesh=mesh,
        in_specs=placed,
        out_specs=(P("cand", None, "img"), P("cand", None, "img"), P("cand", None, "img")),
        check_vma=False,
    )
```

```python
import functools
import itertools

import jax
import jax.numpy as jnp
import ml_dtypes
import numpy as np
from jax import lax
from jax.experimental import pallas as pl
from jax.experimental.pallas import tpu as pltpu
from jax.sharding import PartitionSpec as P

F32 = jnp.float32
BF16 = jnp.bfloat16
LANES = 128
UNIT = 512
BACK_UNIT = 384
DEPTH = 2
STAGGER = 5


def round_up(value, step):
    return -(-value // step) * step


def dft_matrices(side, taps):
    width = int(round(taps**0.5))
    reach = width // 2
    period = side + reach
    kept = []
    for u in range(period):
        for v in range(period):
            if (u, v) <= ((-u) % period, (-v) % period):
                kept.append((u, v))
    freqs = np.array(kept)
    count = len(kept)
    rows = round_up(count, 8)
    mirrored = ((-freqs) % period == freqs).all(axis=1)
    weight = np.where(mirrored, 1.0, 2.0) / period**2
    cell = np.stack(np.meshgrid(np.arange(side), np.arange(side), indexing="ij"), -1).reshape(-1, 2)
    half = len(cell) // 2
    cell = np.concatenate([cell[:half], cell[half:][::-1]]) - (side - 1) / 2
    tap = np.stack(np.meshgrid(np.arange(width), np.arange(width), indexing="ij"), -1).reshape(-1, 2) - reach
    cell_angle = 2 * np.pi * (freqs @ cell.T) / period
    tap_angle = 2 * np.pi * ((freqs @ tap.T) % period) / period
    tap_rows = round_up(taps, 16)

    analysis = np.zeros((2 * rows, side * side))
    analysis[:count] = np.cos(cell_angle)
    analysis[rows : rows + count] = -np.sin(cell_angle)
    even = np.zeros((half, rows))
    even[:, :count] = (weight[:, None] * np.cos(cell_angle)).T[:half]
    odd = np.zeros((half, rows))
    odd[:, :count] = -(weight[:, None] * np.sin(cell_angle)).T[:half]
    spectrum = np.zeros((2 * rows, tap_rows))
    spectrum[:count, :taps] = np.cos(tap_angle)
    spectrum[rows : rows + count, :taps] = np.sin(tap_angle)
    gather_re, gather_im = np.zeros((tap_rows, rows)), np.zeros((tap_rows, rows))
    gather_re[:taps, :count] = (weight[:, None] * np.cos(tap_angle)).T
    gather_im[:taps, :count] = -(weight[:, None] * np.sin(tap_angle)).T

    coarse = spectrum.astype(ml_dtypes.bfloat16).astype(np.float64)
    spectrum = np.concatenate([coarse, coarse, spectrum - coarse], axis=1)
    matrices = (analysis, even, odd, spectrum, gather_re, gather_im)
    return rows, [jnp.asarray(m.astype(ml_dtypes.bfloat16)) for m in matrices]


def dot(a, b):
    return jnp.dot(a, b, preferred_element_type=F32)


def dot_nt(a, b):
    return lax.dot_general(a, b, (((1,), (1,)), ((), ())), preferred_element_type=F32)


def interleave(units):
    waiting, running = list(units), []
    turn = 0
    while waiting or running:
        if waiting and len(running) < DEPTH and turn % STAGGER == 0:
            running.append(waiting.pop(0))
        turn += 1
        for unit in list(running):
            try:
                next(unit)
            except StopIteration:
                running.remove(unit)


def grads_kernel(
    dims,
    offsets,
    layer_ref,
    half_ref,
    radius_ref,
    place_ref,
    *refs,
):
    pieces = len(offsets)
    x_refs, in_hbm, refs, constants = refs[:pieces], refs[pieces : pieces + 6], refs[pieces + 6 : -6], refs[-6:]
    (
    teach_up,
    teach_dw,
    teach_down,
    cand_up,
    cand_dw,
    cand_down,
    grad_up,
    grad_dw,
    grad_down,
    up_buf,
    dw_buf,
    cand_dw_buf,
    down_buf,
    dw_pad,
    up_pad,
    down_pad,
    act,
    spec,
    slope_e,
    slope_k,
    out_up,
    out_dw,
    out_down,
    x_first,
    x_next,
    x_now,
    x_turned,
    err_now,
    err_turned,
    target,
    wide_up,
    wide_dw,
    sems,
    in_sems,
    out_sems,
    ) = refs
    maps, cells, channels, hid, taps, rows, parts, scale = dims
    padded = round_up(hid, LANES)
    own = hid // parts
    window = wide_up.shape[1]

    def copies(slot):
        if slot < 2:
            sources = (teach_up.at[slot], teach_dw, teach_down.at[slot])
            targets = (up_buf.at[slot], dw_buf, down_buf.at[slot])
        else:
            sources = (cand_up.at[0], cand_dw, cand_down.at[0])
            targets = (up_buf.at[slot], cand_dw_buf, down_buf.at[slot])
        if slot == 1:
            sources, targets = sources[::2], targets[::2]
        return [
            pltpu.make_async_copy(src, dst, sems.at[slot, n])
            for n, (src, dst) in enumerate(zip(sources, targets))
        ]

    staged = [
        pltpu.make_async_copy(src, dst, in_sems.at[n]) for n, (src, dst) in enumerate(zip(in_hbm, constants))
    ]
    first_copies = copies(0)
    for copy in [first_copies[1], *staged, first_copies[0], first_copies[2], *copies(2), *copies(1)]:
        copy.start()

    dw_pad[...] = jnp.zeros_like(dw_pad)

    half_cells = cells // 2
    bases = [min(p * own // LANES * LANES, padded - window) for p in range(parts)]
    start = place_ref[1] * own
    base = jnp.minimum(start // LANES * LANES, padded - window)

    def split(both):
        return both[:rows].astype(BF16), both[rows:].astype(BF16)

    def synthesis(re, im):
        same, other = dot(even, re), dot(odd, im)
        return jnp.concatenate([same + other, same - other], axis=0)

    def tap_spectrum(slot, cols):
        weights = dw_pad[slot, :, cols]
        high = weights.astype(BF16)
        low = (weights - high.astype(F32)).astype(BF16)
        return split(dot(spectrum, jnp.concatenate([high, low, high], axis=0)))

    def load(slot, mask_taps):
        if slot != 1:
            copies(slot)[1].wait()
        weights = cand_dw_buf[:, 0] if slot == 2 else dw_buf[:, slot]
        if mask_taps:
            side = int(round(taps**0.5))
            index = lax.broadcasted_iota(jnp.int32, weights.shape, 0)
            row = sum((index >= side * n).astype(jnp.int32) for n in range(1, side))
            ring = jnp.maximum(jnp.abs(row - side // 2), jnp.abs(index - side * row - side // 2))
            unit = lax.broadcasted_iota(jnp.int32, weights.shape, 1)
            keep = (ring <= radius_ref[0]) & (unit < half_ref[0] * (hid // 2))
            weights = jnp.where(keep, weights, 0.0)
        dw_pad[slot, :taps, :hid] = weights

    def forward(slot, lhs, up, down, cols, save, results):
        keep = save is not None
        pre = dot(lhs[...], up[:, cols])
        yield
        half = 0.5 * pre
        bend = jnp.tanh(half)
        more = 1.0 + bend
        wide = half * more
        units = wide.astype(BF16)
        if keep:
            slope_e[:, save] = (more + wide - wide * bend).astype(BF16)
        yield
        tap_re, tap_im = tap_spectrum(slot, cols)
        acts = []
        for m in range(maps):
            here = slice(m * cells, (m + 1) * cells)
            both = dot(analysis, units[here])
            yield
            re, im = split(both)
            if keep:
                spec[m, 0, :, save], spec[m, 1, :, save] = re, im
            mixed_re, mixed_im = re * tap_re - im * tap_im, re * tap_im + im * tap_re
            yield
            mixed = synthesis(mixed_re, mixed_im)
            yield
            half_k = 0.5 * mixed
            bend_k = jnp.tanh(half_k)
            more_k = 1.0 + bend_k
            wide_k = half_k * more_k
            acts.append(wide_k.astype(BF16))
            if keep:
                act[here, save] = acts[-1]
                slope_k[here, save] = (more_k + wide_k - wide_k * bend_k).astype(BF16)
        yield
        results.append(dot_nt(down[:, cols], jnp.concatenate(acts, axis=0)))

    def teacher(slot, lhs, results):
        bounds = list(range(0, max(hid - UNIT // 2, 1), UNIT)) + [hid]
        return [
            forward(slot, lhs, up_buf.at[slot], down_buf.at[slot], slice(lo, hi), None, results)
            for lo, hi in zip(bounds, bounds[1:])
        ]

    def aligned(at, width):
        return pl.ds(pl.multiple_of(at, LANES), width)

    def candidate(lhs, results):
        units = []
        for at in range(0, window, BACK_UNIT):
            width = min(BACK_UNIT, window - at)
            cols = aligned(base + at, width)
            units.append(forward(2, lhs, up_pad, down_pad, cols, slice(at, at + width), results))
        step = max(w for w in (LANES, 2 * LANES, UNIT) if all(b % w == 0 for b in bases))
        for at in range(0, padded - window, step):
            cols = aligned(jnp.where(at < base, at, at + window), min(step, padded - window - at))
            units.append(forward(2, lhs, up_pad, down_pad, cols, None, results))
        return units

    load(0, False)
    for copy in staged:
        copy.wait()
    analysis, even, odd, spectrum, gather_re, gather_im = (ref[...] for ref in constants)
    whole_turn = (
        lax.broadcasted_iota(jnp.int32, (half_cells, half_cells), 0)
        + lax.broadcasted_iota(jnp.int32, (half_cells, half_cells), 1)
    ) == half_cells - 1
    turn_half = whole_turn.astype(F32).astype(BF16)
    for x_ref, offset in zip(x_refs, offsets):
        if offset is None:
            x_first[...] = x_ref[...]
            continue
        block = x_ref.shape[1]
        for n, distance in enumerate(offset):
            source = place_ref[0] ^ distance
            source = (source & (parts - 1)) * (cells // block) + (source >> (parts.bit_length() - 1))
            at = pl.multiple_of(source * block, block)
            x_first[pl.ds(at, block), :] = x_ref[n]
    for m in range(maps):
        second = slice(m * cells + half_cells, (m + 1) * cells)
        x_first[second] = dot(turn_half, x_first[second]).astype(BF16)
    for copy in copies(0)[::2]:
        copy.wait()
    first = []
    interleave(teacher(0, x_first, first))
    branch = sum(first)
    x_next[...] = (x_first[...].astype(F32) + jnp.transpose(branch)).astype(BF16)
    x_now[...] = jnp.where(layer_ref[0] == 0, x_first[...], x_next[...])
    target[...] = branch
    load(2, True)
    load(1, False)
    for copy in copies(2)[::2] + copies(1):
        copy.wait()
    for pad, buf in ((up_pad, up_buf), (down_pad, down_buf)):
        pad[:, hid // LANES * LANES :] = jnp.zeros((channels, padded - hid // LANES * LANES), BF16)
        pad[:, :hid] = buf[2]
    second, third = [], []
    units = [teacher(1, x_next, second), candidate(x_now, third)]
    interleave([unit for pair in itertools.zip_longest(*units) for unit in pair if unit is not None])
    err = (sum(third) - jnp.where(layer_ref[0] == 0, target[...], sum(second))) * scale
    err_now[...] = jnp.transpose(0.5 * err).astype(BF16)
    err_turned[...] = err.astype(BF16)
    x_turned[...] = jnp.transpose(0.5 * x_now[...].astype(F32)).astype(BF16)

    offset = start - base
    shifts = sorted({p * own - at for p, at in enumerate(bases)})

    def leave(wide, out, n, grad):
        for shift in shifts:
            @pl.when(offset == shift)
            def _():
                out[...] = wide[:, shift : shift + own]
        pltpu.make_async_copy(out, grad.at[0], out_sems.at[n]).start()

    wide_up[...] = dot(err_turned[...], act[...])
    leave(wide_up, out_down, 0, grad_down)

    def back(at, width):
        cols = aligned(base + at, width)
        here = slice(at, at + width)
        grad_act = dot(err_now[...], down_pad[:, cols])
        yield
        grad_k = grad_act.astype(BF16) * slope_k[:, here]
        yield
        tap_re, tap_im = tap_spectrum(2, cols)
        sum_re, sum_im = [], []
        grad_pre = []
        for m in range(maps):
            rows_here = slice(m * cells, (m + 1) * cells)
            both = dot(analysis, grad_k[rows_here])
            yield
            re, im = split(both)
            e_re, e_im = spec[m, 0, :, here], spec[m, 1, :, here]
            sum_re.append(re * e_re + im * e_im)
            sum_im.append(re * e_im - im * e_re)
            mixed_re, mixed_im = re * tap_re + im * tap_im, im * tap_re - re * tap_im
            yield
            grad_e = synthesis(mixed_re, mixed_im)
            yield
            grad_pre.append(grad_e.astype(BF16) * slope_e[rows_here, here])
        yield
        wide_up[:, here] = dot(x_turned[...], jnp.concatenate(grad_pre, axis=0))
        wide_dw[:, here] = dot(gather_re, sum(sum_re[1:], sum_re[0])) + dot(gather_im, sum(sum_im[1:], sum_im[0]))

    interleave([back(at, min(BACK_UNIT, window - at)) for at in range(0, window, BACK_UNIT)])

    leave(wide_up, out_up, 1, grad_up)
    for shift in shifts:
        @pl.when(offset == shift)
        def _():
            own_dw = wide_dw[:taps, shift : shift + own]
            side = int(round(taps**0.5))
            index = lax.broadcasted_iota(jnp.int32, own_dw.shape, 0)
            row = sum((index >= side * n).astype(jnp.int32) for n in range(1, side))
            ring = jnp.maximum(jnp.abs(row - side // 2), jnp.abs(index - side * row - side // 2))
            unit = lax.broadcasted_iota(jnp.int32, own_dw.shape, 1) + start
            keep = (ring <= radius_ref[0]) & (unit < half_ref[0] * (hid // 2))
            out_dw[:, 0] = jnp.where(keep, own_dw, 0.0)
    pltpu.make_async_copy(out_dw, grad_dw, out_sems.at[2]).start()
    pltpu.make_async_copy(out_down, grad_down.at[0], out_sems.at[0]).wait()
    pltpu.make_async_copy(out_up, grad_up.at[0], out_sems.at[1]).wait()
    pltpu.make_async_copy(out_dw, grad_dw, out_sems.at[2]).wait()


def local_grads(pieces, offsets, maps, layer, half, radius, place, parts, images, weights):
    teach_up, teach_dw, teach_down, cand_up, cand_dw, cand_down = weights
    weights = (teach_up, teach_dw.transpose(1, 0, 2), teach_down, cand_up, cand_dw.transpose(1, 0, 2), cand_down)
    channels, hid = teach_up.shape[1:]
    taps = teach_dw.shape[1]
    count = sum(piece.size for piece in pieces) // channels
    cells = count // maps
    side = int(round(cells**0.5))
    rows, constants = dft_matrices(side, taps)
    padded = round_up(hid, LANES)
    own = hid // parts
    spare = max((p * own) % LANES for p in range(parts))
    window = min(round_up(own + spare, LANES), padded)
    tap_rows = round_up(taps, 16)
    dims = (maps, cells, channels, hid, taps, rows, parts, 1.0 / images)
    smem = pl.BlockSpec(memory_space=pltpu.SMEM)
    vmem = pl.BlockSpec(memory_space=pltpu.VMEM)
    anywhere = pl.BlockSpec(memory_space=pl.ANY)
    grad_up, grad_dw, grad_down = pl.pallas_call(
        functools.partial(grads_kernel, dims, offsets),
        out_shape=(
            jax.ShapeDtypeStruct((1, channels, own), F32),
            jax.ShapeDtypeStruct((taps, 1, own), F32),
            jax.ShapeDtypeStruct((1, channels, own), F32),
        ),
        in_specs=[smem] * 4 + [vmem] * len(pieces) + [anywhere] * 12,
        out_specs=(anywhere, anywhere, anywhere),
        scratch_shapes=[
            pltpu.VMEM((3, channels, hid), BF16),
            pltpu.VMEM(weights[1].shape, F32),
            pltpu.VMEM(weights[4].shape, F32),
            pltpu.VMEM((3, channels, hid), BF16),
            pltpu.VMEM((3, tap_rows, padded), F32),
            pltpu.VMEM((channels, padded), BF16),
            pltpu.VMEM((channels, padded), BF16),
            pltpu.VMEM((count, window), BF16),
            pltpu.VMEM((maps, 2, rows, window), BF16),
            pltpu.VMEM((count, window), BF16),
            pltpu.VMEM((count, window), BF16),
            pltpu.VMEM((channels, own), F32),
            pltpu.VMEM((taps, 1, own), F32),
            pltpu.VMEM((channels, own), F32),
            pltpu.VMEM((count, channels), BF16),
            pltpu.VMEM((count, channels), BF16),
            pltpu.VMEM((count, channels), BF16),
            pltpu.VMEM((channels, count), BF16),
            pltpu.VMEM((count, channels), BF16),
            pltpu.VMEM((channels, count), BF16),
            pltpu.VMEM((channels, count), F32),
            pltpu.VMEM((channels, window), F32),
            pltpu.VMEM((tap_rows, window), F32),
            pltpu.SemaphoreType.DMA((3, 3)),
            pltpu.SemaphoreType.DMA((len(constants),)),
            pltpu.SemaphoreType.DMA((3,)),
            *[pltpu.VMEM(array.shape, BF16) for array in constants],
        ],
        compiler_params=pltpu.CompilerParams(vmem_limit_bytes=60 * 2**20),
        cost_estimate=pl.CostEstimate(
            flops=20 * count * channels * hid, bytes_accessed=12 * channels * hid, transcendentals=6 * count * hid
        ),
    )(layer, half, radius, place, *pieces, *constants, *weights)
    return grad_up, grad_dw.transpose(1, 0, 2), grad_down


def exchange(block, masks, devices):
    offset = [0]
    for mask in masks:
        distances = [d for d in range(1, devices) if d & ~mask == 0]
        parts = [block] + [
            lax.ppermute(block, ("cand", "img"), [(source, source ^ d) for source in range(devices)])
            for d in distances
        ]
        pieces = [[o ^ d for o in offset] for d in [0] + distances]
        offset = sum(pieces, [])
        if mask != masks[-1]:
            block = jnp.concatenate(parts, axis=0).astype(BF16)
    return parts, pieces


def body(
    first_maps,
    layer_of,
    expand_half,
    radius,
    teach_up,
    teach_dw,
    teach_down,
    cand_up,
    cand_dw,
    cand_down,
):
    parts = lax.axis_size("img")
    cands = lax.axis_size("cand")
    devices = parts * cands
    batch, own_cells, channels = first_maps.shape
    images = parts * batch
    part = lax.axis_index("img")
    place = jnp.stack([lax.axis_index("cand") * parts + part, part])
    weights = (teach_up, teach_dw, teach_down, cand_up, cand_dw, cand_down)
    scalars = (layer_of, expand_half, radius, place, parts, images, weights)
    if batch == 1 and images == 2 and own_cells % 16 == 0 and devices & (devices - 1) == 0:
        core = parts * (cands > 1)
        near = (parts - 1) | (2 * core)
        masks = [(devices - 1) & ~near & ~core, near, core]
        pieces, offsets = exchange(first_maps, masks, devices)
        return local_grads(pieces, offsets, images, *scalars)
    whole = lax.all_gather(first_maps.astype(BF16), ("img", "cand")).reshape(parts, cands, batch, own_cells, channels)
    whole = whole.transpose(0, 2, 1, 3, 4).reshape(images, -1, channels)
    group = 2 if images % 2 == 0 else 1
    total = None
    for first in range(0, images, group):
        pieces = [whole[first : first + group].reshape(-1, channels)]
        grads = local_grads(pieces, [None], group, *scalars)
        total = grads if total is None else tuple(a + b for a, b in zip(total, grads))
    return total


def solution(mesh):
    placed = (
        P("img", "cand", None),
        P("cand"),
        P("cand"),
        P("cand"),
        P(),
        P(),
        P(),
        P("cand", None, None),
        P("cand", None, None),
        P("cand", None, None),
    )
    return jax.shard_map(
        body,
        mesh=mesh,
        in_specs=placed,
        out_specs=(P("cand", None, "img"), P("cand", None, "img"), P("cand", None, "img")),
        check_vma=False,
    )
```

```python
import functools
import itertools

import jax
import jax.numpy as jnp
import ml_dtypes
import numpy as np
from jax import lax
from jax.experimental import pallas as pl
from jax.experimental.pallas import tpu as pltpu
from jax.sharding import PartitionSpec as P

F32 = jnp.float32
BF16 = jnp.bfloat16
LANES = 128
UNIT = 512
BACK_UNIT = 384
DEPTH = 2
STAGGER = 5


def round_up(value, step):
    return -(-value // step) * step


def dft_matrices(side, taps):
    width = int(round(taps**0.5))
    reach = width // 2
    period = side + reach
    kept = []
    for u in range(period):
        for v in range(period):
            if (u, v) <= ((-u) % period, (-v) % period):
                kept.append((u, v))
    freqs = np.array(kept)
    count = len(kept)
    rows = round_up(count, 8)
    mirrored = ((-freqs) % period == freqs).all(axis=1)
    weight = np.where(mirrored, 1.0, 2.0) / period**2
    cell = np.stack(np.meshgrid(np.arange(side), np.arange(side), indexing="ij"), -1).reshape(-1, 2)
    half = len(cell) // 2
    cell = np.concatenate([cell[:half], cell[half:][::-1]]) - (side - 1) / 2
    tap = np.stack(np.meshgrid(np.arange(width), np.arange(width), indexing="ij"), -1).reshape(-1, 2) - reach
    cell_angle = 2 * np.pi * (freqs @ cell.T) / period
    tap_angle = 2 * np.pi * ((freqs @ tap.T) % period) / period
    tap_rows = round_up(taps, 16)

    analysis = np.zeros((2 * rows, side * side))
    analysis[:count] = np.cos(cell_angle)
    analysis[rows : rows + count] = -np.sin(cell_angle)
    even = np.zeros((half, rows))
    even[:, :count] = (weight[:, None] * np.cos(cell_angle)).T[:half]
    odd = np.zeros((half, rows))
    odd[:, :count] = -(weight[:, None] * np.sin(cell_angle)).T[:half]
    spectrum = np.zeros((2 * rows, tap_rows))
    spectrum[:count, :taps] = np.cos(tap_angle)
    spectrum[rows : rows + count, :taps] = np.sin(tap_angle)
    gather_re, gather_im = np.zeros((tap_rows, rows)), np.zeros((tap_rows, rows))
    gather_re[:taps, :count] = (weight[:, None] * np.cos(tap_angle)).T
    gather_im[:taps, :count] = -(weight[:, None] * np.sin(tap_angle)).T

    coarse = spectrum.astype(ml_dtypes.bfloat16).astype(np.float64)
    spectrum = np.concatenate([coarse, coarse, spectrum - coarse], axis=1)
    matrices = (analysis, even, odd, spectrum, gather_re, gather_im)
    return rows, [jnp.asarray(m.astype(ml_dtypes.bfloat16)) for m in matrices]


def dot(a, b):
    return jnp.dot(a, b, preferred_element_type=F32)


def dot_nt(a, b):
    return lax.dot_general(a, b, (((1,), (1,)), ((), ())), preferred_element_type=F32)


def interleave(units):
    waiting, running = list(units), []
    turn = 0
    while waiting or running:
        if waiting and len(running) < DEPTH and turn % STAGGER == 0:
            running.append(waiting.pop(0))
        turn += 1
        for unit in list(running):
            try:
                next(unit)
            except StopIteration:
                running.remove(unit)


def grads_kernel(
    dims,
    offsets,
    layer_ref,
    half_ref,
    radius_ref,
    place_ref,
    *refs,
):
    pieces = len(offsets)
    x_refs, in_hbm, refs, constants = refs[:pieces], refs[pieces : pieces + 6], refs[pieces + 6 : -6], refs[-6:]
    (
    teach_up,
    teach_dw,
    teach_down,
    cand_up,
    cand_dw,
    cand_down,
    grad_up,
    grad_dw,
    grad_down,
    up_buf,
    dw_buf,
    cand_dw_buf,
    down_buf,
    dw_pad,
    up_pad,
    down_pad,
    act,
    spec,
    slope_e,
    slope_k,
    out_up,
    out_dw,
    out_down,
    x_first,
    x_next,
    x_now,
    x_turned,
    err_now,
    err_turned,
    target,
    wide_up,
    wide_dw,
    sems,
    in_sems,
    out_sems,
    ) = refs
    maps, cells, channels, hid, taps, rows, parts, scale = dims
    padded = round_up(hid, LANES)
    own = hid // parts
    window = wide_up.shape[1]

    def copies(slot):
        if slot < 2:
            sources = (teach_up.at[slot], teach_dw, teach_down.at[slot])
            targets = (up_buf.at[slot], dw_buf, down_buf.at[slot])
        else:
            sources = (cand_up.at[0], cand_dw, cand_down.at[0])
            targets = (up_buf.at[slot], cand_dw_buf, down_buf.at[slot])
        if slot == 1:
            sources, targets = sources[::2], targets[::2]
        return [
            pltpu.make_async_copy(src, dst, sems.at[slot, n])
            for n, (src, dst) in enumerate(zip(sources, targets))
        ]

    staged = [
        pltpu.make_async_copy(src, dst, in_sems.at[n]) for n, (src, dst) in enumerate(zip(in_hbm, constants))
    ]
    first_copies = copies(0)
    for copy in [first_copies[1], *staged, first_copies[0], first_copies[2], *copies(2), *copies(1)]:
        copy.start()

    dw_pad[...] = jnp.zeros_like(dw_pad)

    half_cells = cells // 2
    bases = [min(p * own // LANES * LANES, padded - window) for p in range(parts)]
    start = place_ref[1] * own
    base = jnp.minimum(start // LANES * LANES, padded - window)

    def split(both):
        return both[:rows].astype(BF16), both[rows:].astype(BF16)

    def synthesis(re, im):
        same, other = dot(even, re), dot(odd, im)
        return jnp.concatenate([same + other, same - other], axis=0)

    def tap_spectrum(slot, cols):
        weights = dw_pad[slot, :, cols]
        high = weights.astype(BF16)
        low = (weights - high.astype(F32)).astype(BF16)
        return split(dot(spectrum, jnp.concatenate([high, low, high], axis=0)))

    def load(slot, mask_taps):
        if slot != 1:
            copies(slot)[1].wait()
        weights = cand_dw_buf[:, 0] if slot == 2 else dw_buf[:, slot]
        if mask_taps:
            side = int(round(taps**0.5))
            index = lax.broadcasted_iota(jnp.int32, weights.shape, 0)
            row = sum((index >= side * n).astype(jnp.int32) for n in range(1, side))
            ring = jnp.maximum(jnp.abs(row - side // 2), jnp.abs(index - side * row - side // 2))
            unit = lax.broadcasted_iota(jnp.int32, weights.shape, 1)
            keep = (ring <= radius_ref[0]) & (unit < half_ref[0] * (hid // 2))
            weights = jnp.where(keep, weights, 0.0)
        dw_pad[slot, :taps, :hid] = weights

    def forward(slot, lhs, up, down, cols, save, results):
        keep = save is not None
        pre = dot(lhs[...], up[:, cols])
        yield
        half = 0.5 * pre
        bend = jnp.tanh(half)
        more = 1.0 + bend
        wide = half * more
        units = wide.astype(BF16)
        if keep:
            slope_e[:, save] = (more + wide - wide * bend).astype(BF16)
        yield
        tap_re, tap_im = tap_spectrum(slot, cols)
        acts = []
        for m in range(maps):
            here = slice(m * cells, (m + 1) * cells)
            both = dot(analysis, units[here])
            yield
            re, im = split(both)
            if keep:
                spec[m, 0, :, save], spec[m, 1, :, save] = re, im
            mixed_re, mixed_im = re * tap_re - im * tap_im, re * tap_im + im * tap_re
            yield
            mixed = synthesis(mixed_re, mixed_im)
            yield
            half_k = 0.5 * mixed
            bend_k = jnp.tanh(half_k)
            more_k = 1.0 + bend_k
            wide_k = half_k * more_k
            acts.append(wide_k.astype(BF16))
            if keep:
                act[here, save] = acts[-1]
                slope_k[here, save] = (more_k + wide_k - wide_k * bend_k).astype(BF16)
        yield
        results.append(dot_nt(down[:, cols], jnp.concatenate(acts, axis=0)))

    def teacher(slot, lhs, results):
        bounds = list(range(0, max(hid - UNIT // 2, 1), UNIT)) + [hid]
        return [
            forward(slot, lhs, up_buf.at[slot], down_buf.at[slot], slice(lo, hi), None, results)
            for lo, hi in zip(bounds, bounds[1:])
        ]

    def aligned(at, width):
        return pl.ds(pl.multiple_of(at, LANES), width)

    def candidate(lhs, results):
        units = []
        for at in range(0, window, BACK_UNIT):
            width = min(BACK_UNIT, window - at)
            cols = aligned(base + at, width)
            units.append(forward(2, lhs, up_pad, down_pad, cols, slice(at, at + width), results))
        step = max(w for w in (LANES, 2 * LANES, UNIT) if all(b % w == 0 for b in bases))
        for at in range(0, padded - window, step):
            cols = aligned(jnp.where(at < base, at, at + window), min(step, padded - window - at))
            units.append(forward(2, lhs, up_pad, down_pad, cols, None, results))
        return units

    load(0, False)
    for copy in staged:
        copy.wait()
    analysis, even, odd, spectrum, gather_re, gather_im = (ref[...] for ref in constants)
    whole_turn = (
        lax.broadcasted_iota(jnp.int32, (half_cells, half_cells), 0)
        + lax.broadcasted_iota(jnp.int32, (half_cells, half_cells), 1)
    ) == half_cells - 1
    turn_half = whole_turn.astype(F32).astype(BF16)
    for x_ref, offset in zip(x_refs, offsets):
        if offset is None:
            x_first[...] = x_ref[...]
            continue
        block = x_ref.shape[1]
        for n, owner in enumerate(offset):
            at = owner % parts * cells + owner // parts * block
            x_first[at : at + block] = x_ref[n]
    for m in range(maps):
        second = slice(m * cells + half_cells, (m + 1) * cells)
        x_first[second] = dot(turn_half, x_first[second]).astype(BF16)
    for copy in copies(0)[::2]:
        copy.wait()
    first = []
    interleave(teacher(0, x_first, first))
    branch = sum(first)
    x_next[...] = (x_first[...].astype(F32) + jnp.transpose(branch)).astype(BF16)
    x_now[...] = jnp.where(layer_ref[0] == 0, x_first[...], x_next[...])
    target[...] = branch
    load(2, True)
    load(1, False)
    for copy in copies(2)[::2] + copies(1):
        copy.wait()
    for pad, buf in ((up_pad, up_buf), (down_pad, down_buf)):
        pad[:, hid // LANES * LANES :] = jnp.zeros((channels, padded - hid // LANES * LANES), BF16)
        pad[:, :hid] = buf[2]
    second, third = [], []
    units = [teacher(1, x_next, second), candidate(x_now, third)]
    interleave([unit for pair in itertools.zip_longest(*units) for unit in pair if unit is not None])
    err = (sum(third) - jnp.where(layer_ref[0] == 0, target[...], sum(second))) * scale
    err_now[...] = jnp.transpose(0.5 * err).astype(BF16)
    err_turned[...] = err.astype(BF16)
    x_turned[...] = jnp.transpose(0.5 * x_now[...].astype(F32)).astype(BF16)

    offset = start - base
    shifts = sorted({p * own - at for p, at in enumerate(bases)})

    def leave(wide, out, n, grad):
        for shift in shifts:
            @pl.when(offset == shift)
            def _():
                out[...] = wide[:, shift : shift + own]
        pltpu.make_async_copy(out, grad.at[0], out_sems.at[n]).start()

    wide_up[...] = dot(err_turned[...], act[...])
    leave(wide_up, out_down, 0, grad_down)

    def back(at, width):
        cols = aligned(base + at, width)
        here = slice(at, at + width)
        grad_act = dot(err_now[...], down_pad[:, cols])
        yield
        grad_k = grad_act.astype(BF16) * slope_k[:, here]
        yield
        tap_re, tap_im = tap_spectrum(2, cols)
        sum_re, sum_im = [], []
        grad_pre = []
        for m in range(maps):
            rows_here = slice(m * cells, (m + 1) * cells)
            both = dot(analysis, grad_k[rows_here])
            yield
            re, im = split(both)
            e_re, e_im = spec[m, 0, :, here], spec[m, 1, :, here]
            sum_re.append(re * e_re + im * e_im)
            sum_im.append(re * e_im - im * e_re)
            mixed_re, mixed_im = re * tap_re + im * tap_im, im * tap_re - re * tap_im
            yield
            grad_e = synthesis(mixed_re, mixed_im)
            yield
            grad_pre.append(grad_e.astype(BF16) * slope_e[rows_here, here])
        yield
        wide_up[:, here] = dot(x_turned[...], jnp.concatenate(grad_pre, axis=0))
        wide_dw[:, here] = dot(gather_re, sum(sum_re[1:], sum_re[0])) + dot(gather_im, sum(sum_im[1:], sum_im[0]))

    interleave([back(at, min(BACK_UNIT, window - at)) for at in range(0, window, BACK_UNIT)])

    leave(wide_up, out_up, 1, grad_up)
    for shift in shifts:
        @pl.when(offset == shift)
        def _():
            own_dw = wide_dw[:taps, shift : shift + own]
            side = int(round(taps**0.5))
            index = lax.broadcasted_iota(jnp.int32, own_dw.shape, 0)
            row = sum((index >= side * n).astype(jnp.int32) for n in range(1, side))
            ring = jnp.maximum(jnp.abs(row - side // 2), jnp.abs(index - side * row - side // 2))
            unit = lax.broadcasted_iota(jnp.int32, own_dw.shape, 1) + start
            keep = (ring <= radius_ref[0]) & (unit < half_ref[0] * (hid // 2))
            out_dw[:, 0] = jnp.where(keep, own_dw, 0.0)
    pltpu.make_async_copy(out_dw, grad_dw, out_sems.at[2]).start()
    pltpu.make_async_copy(out_down, grad_down.at[0], out_sems.at[0]).wait()
    pltpu.make_async_copy(out_up, grad_up.at[0], out_sems.at[1]).wait()
    pltpu.make_async_copy(out_dw, grad_dw, out_sems.at[2]).wait()


def local_grads(pieces, offsets, maps, layer, half, radius, place, parts, images, weights):
    teach_up, teach_dw, teach_down, cand_up, cand_dw, cand_down = weights
    weights = (teach_up, teach_dw.transpose(1, 0, 2), teach_down, cand_up, cand_dw.transpose(1, 0, 2), cand_down)
    channels, hid = teach_up.shape[1:]
    taps = teach_dw.shape[1]
    count = sum(piece.size for piece in pieces) // channels
    cells = count // maps
    side = int(round(cells**0.5))
    rows, constants = dft_matrices(side, taps)
    padded = round_up(hid, LANES)
    own = hid // parts
    spare = max((p * own) % LANES for p in range(parts))
    window = min(round_up(own + spare, LANES), padded)
    tap_rows = round_up(taps, 16)
    dims = (maps, cells, channels, hid, taps, rows, parts, 1.0 / images)
    smem = pl.BlockSpec(memory_space=pltpu.SMEM)
    vmem = pl.BlockSpec(memory_space=pltpu.VMEM)
    anywhere = pl.BlockSpec(memory_space=pl.ANY)
    grad_up, grad_dw, grad_down = pl.pallas_call(
        functools.partial(grads_kernel, dims, offsets),
        out_shape=(
            jax.ShapeDtypeStruct((1, channels, own), F32),
            jax.ShapeDtypeStruct((taps, 1, own), F32),
            jax.ShapeDtypeStruct((1, channels, own), F32),
        ),
        in_specs=[smem] * 4 + [vmem] * len(pieces) + [anywhere] * 12,
        out_specs=(anywhere, anywhere, anywhere),
        scratch_shapes=[
            pltpu.VMEM((3, channels, hid), BF16),
            pltpu.VMEM(weights[1].shape, F32),
            pltpu.VMEM(weights[4].shape, F32),
            pltpu.VMEM((3, channels, hid), BF16),
            pltpu.VMEM((3, tap_rows, padded), F32),
            pltpu.VMEM((channels, padded), BF16),
            pltpu.VMEM((channels, padded), BF16),
            pltpu.VMEM((count, window), BF16),
            pltpu.VMEM((maps, 2, rows, window), BF16),
            pltpu.VMEM((count, window), BF16),
            pltpu.VMEM((count, window), BF16),
            pltpu.VMEM((channels, own), F32),
            pltpu.VMEM((taps, 1, own), F32),
            pltpu.VMEM((channels, own), F32),
            pltpu.VMEM((count, channels), BF16),
            pltpu.VMEM((count, channels), BF16),
            pltpu.VMEM((count, channels), BF16),
            pltpu.VMEM((channels, count), BF16),
            pltpu.VMEM((count, channels), BF16),
            pltpu.VMEM((channels, count), BF16),
            pltpu.VMEM((channels, count), F32),
            pltpu.VMEM((channels, window), F32),
            pltpu.VMEM((tap_rows, window), F32),
            pltpu.SemaphoreType.DMA((3, 3)),
            pltpu.SemaphoreType.DMA((len(constants),)),
            pltpu.SemaphoreType.DMA((3,)),
            *[pltpu.VMEM(array.shape, BF16) for array in constants],
        ],
        compiler_params=pltpu.CompilerParams(vmem_limit_bytes=60 * 2**20),
        cost_estimate=pl.CostEstimate(
            flops=20 * count * channels * hid, bytes_accessed=12 * channels * hid, transcendentals=6 * count * hid
        ),
    )(layer, half, radius, place, *pieces, *constants, *weights)
    return grad_up, grad_dw.transpose(1, 0, 2), grad_down


def spread(block, cands, parts):
    stages = [("cand", 4, cands // 4), ("cand", 2, 2), ("img", 1, parts), ("cand", 1, 2)]
    owners = [0]
    for axis, stride, size in stages:
        count = parts if axis == "img" else cands
        starts = [n for n in range(count) if n // stride % size == 0]
        groups = [[n + stride * j for j in range(size)] for n in starts]
        block = lax.all_gather(block, axis, axis_index_groups=groups, axis=0, tiled=True)
        weight = stride * (parts if axis == "cand" else 1)
        owners = [owner + weight * j for j in range(size) for owner in owners]
    return [block], [owners]


def body(
    first_maps,
    layer_of,
    expand_half,
    radius,
    teach_up,
    teach_dw,
    teach_down,
    cand_up,
    cand_dw,
    cand_down,
):
    parts = lax.axis_size("img")
    cands = lax.axis_size("cand")
    devices = parts * cands
    batch, own_cells, channels = first_maps.shape
    images = parts * batch
    part = lax.axis_index("img")
    place = jnp.stack([lax.axis_index("cand") * parts + part, part])
    weights = (teach_up, teach_dw, teach_down, cand_up, cand_dw, cand_down)
    scalars = (layer_of, expand_half, radius, place, parts, images, weights)
    if batch == 1 and images == 2 and own_cells % 16 == 0 and devices & (devices - 1) == 0 and cands >= 4:
        pieces, owners = spread(first_maps.astype(BF16), cands, parts)
        return local_grads(pieces, owners, images, *scalars)
    whole = lax.all_gather(first_maps.astype(BF16), ("img", "cand")).reshape(parts, cands, batch, own_cells, channels)
    whole = whole.transpose(0, 2, 1, 3, 4).reshape(images, -1, channels)
    group = 2 if images % 2 == 0 else 1
    total = None
    for first in range(0, images, group):
        pieces = [whole[first : first + group].reshape(-1, channels)]
        grads = local_grads(pieces, [None], group, *scalars)
        total = grads if total is None else tuple(a + b for a, b in zip(total, grads))
    return total


def solution(mesh):
    placed = (
        P("img", "cand", None),
        P("cand"),
        P("cand"),
        P("cand"),
        P(),
        P(),
        P(),
        P("cand", None, None),
        P("cand", None, None),
        P("cand", None, None),
    )
    return jax.shard_map(
        body,
        mesh=mesh,
        in_specs=placed,
        out_specs=(P("cand", None, "img"), P("cand", None, "img"), P("cand", None, "img")),
        check_vma=False,
    )
```

```python
import functools
import itertools

import jax
import jax.numpy as jnp
import ml_dtypes
import numpy as np
from jax import lax
from jax.experimental import pallas as pl
from jax.experimental.pallas import tpu as pltpu
from jax.sharding import PartitionSpec as P

F32 = jnp.float32
BF16 = jnp.bfloat16
LANES = 128
UNIT = 512
BACK_UNIT = 384
DEPTH = 2
STAGGER = 5


def round_up(value, step):
    return -(-value // step) * step


def dft_matrices(side, taps):
    width = int(round(taps**0.5))
    reach = width // 2
    period = side + reach
    kept = []
    for u in range(period):
        for v in range(period):
            if (u, v) <= ((-u) % period, (-v) % period):
                kept.append((u, v))
    freqs = np.array(kept)
    count = len(kept)
    rows = round_up(count, 8)
    mirrored = ((-freqs) % period == freqs).all(axis=1)
    weight = np.where(mirrored, 1.0, 2.0) / period**2
    cell = np.stack(np.meshgrid(np.arange(side), np.arange(side), indexing="ij"), -1).reshape(-1, 2)
    half = len(cell) // 2
    cell = np.concatenate([cell[:half], cell[half:][::-1]]) - (side - 1) / 2
    tap = np.stack(np.meshgrid(np.arange(width), np.arange(width), indexing="ij"), -1).reshape(-1, 2) - reach
    cell_angle = 2 * np.pi * (freqs @ cell.T) / period
    tap_angle = 2 * np.pi * ((freqs @ tap.T) % period) / period
    tap_rows = round_up(taps, 16)

    analysis = np.zeros((2 * rows, side * side))
    analysis[:count] = np.cos(cell_angle)
    analysis[rows : rows + count] = -np.sin(cell_angle)
    even = np.zeros((half, rows))
    even[:, :count] = (weight[:, None] * np.cos(cell_angle)).T[:half]
    odd = np.zeros((half, rows))
    odd[:, :count] = -(weight[:, None] * np.sin(cell_angle)).T[:half]
    spectrum = np.zeros((2 * rows, tap_rows))
    spectrum[:count, :taps] = np.cos(tap_angle)
    spectrum[rows : rows + count, :taps] = np.sin(tap_angle)
    gather_re, gather_im = np.zeros((tap_rows, rows)), np.zeros((tap_rows, rows))
    gather_re[:taps, :count] = (weight[:, None] * np.cos(tap_angle)).T
    gather_im[:taps, :count] = -(weight[:, None] * np.sin(tap_angle)).T

    coarse = spectrum.astype(ml_dtypes.bfloat16).astype(np.float64)
    spectrum = np.concatenate([coarse, coarse, spectrum - coarse], axis=1)
    matrices = (analysis, even, odd, spectrum, gather_re, gather_im)
    return rows, [jnp.asarray(m.astype(ml_dtypes.bfloat16)) for m in matrices]


def dot(a, b):
    return jnp.dot(a, b, preferred_element_type=F32)


def dot_nt(a, b):
    return lax.dot_general(a, b, (((1,), (1,)), ((), ())), preferred_element_type=F32)


def interleave(units):
    waiting, running = list(units), []
    turn = 0
    while waiting or running:
        if waiting and len(running) < DEPTH and turn % STAGGER == 0:
            running.append(waiting.pop(0))
        turn += 1
        for unit in list(running):
            try:
                next(unit)
            except StopIteration:
                running.remove(unit)


def grads_kernel(
    dims,
    offsets,
    *refs,
):
    pieces = len(offsets)
    flags, refs = refs[0], refs[1:]
    layer, half_units, radius = flags[:, 0:1], flags[:, 1:2], flags[:, 2:3]
    x_refs, in_hbm, refs, constants = refs[:pieces], refs[pieces : pieces + 6], refs[pieces + 6 : -6], refs[-6:]
    (
    teach_up,
    teach_dw,
    teach_down,
    cand_up,
    cand_dw,
    cand_down,
    grad_up,
    grad_dw,
    grad_down,
    up_buf,
    dw_buf,
    cand_dw_buf,
    down_buf,
    dw_pad,
    up_pad,
    down_pad,
    act,
    spec,
    slope_e,
    slope_k,
    out_up,
    out_dw,
    out_down,
    x_first,
    x_next,
    x_now,
    x_turned,
    err_now,
    err_turned,
    target,
    wide_up,
    wide_dw,
    sems,
    in_sems,
    out_sems,
    ) = refs
    maps, cells, channels, hid, taps, rows, parts, scale = dims
    padded = round_up(hid, LANES)
    own = hid // parts
    window = wide_up.shape[1]

    def copies(slot):
        if slot < 2:
            sources = (teach_up.at[slot], teach_dw, teach_down.at[slot])
            targets = (up_buf.at[slot], dw_buf, down_buf.at[slot])
        else:
            sources = (cand_up.at[0], cand_dw, cand_down.at[0])
            targets = (up_buf.at[slot], cand_dw_buf, down_buf.at[slot])
        if slot == 1:
            sources, targets = sources[::2], targets[::2]
        return [
            pltpu.make_async_copy(src, dst, sems.at[slot, n])
            for n, (src, dst) in enumerate(zip(sources, targets))
        ]

    staged = [
        pltpu.make_async_copy(src, dst, in_sems.at[n]) for n, (src, dst) in enumerate(zip(in_hbm, constants))
    ]
    first_copies = copies(0)
    for copy in [first_copies[1], *staged, first_copies[0], first_copies[2], *copies(2), *copies(1)]:
        copy.start()

    dw_pad[...] = jnp.zeros_like(dw_pad)

    half_cells = cells // 2
    bases = [min(p * own // LANES * LANES, padded - window) for p in range(parts)]
    part = lax.axis_index("img")
    place = lax.axis_index("cand") * parts + part
    start = part * own
    base = jnp.minimum(start // LANES * LANES, padded - window)

    def split(both):
        return both[:rows].astype(BF16), both[rows:].astype(BF16)

    def synthesis(re, im):
        same, other = dot(even, re), dot(odd, im)
        return jnp.concatenate([same + other, same - other], axis=0)

    def tap_spectrum(slot, cols):
        weights = dw_pad[slot, :, cols]
        high = weights.astype(BF16)
        low = (weights - high.astype(F32)).astype(BF16)
        return split(dot(spectrum, jnp.concatenate([high, low, high], axis=0)))

    def load(slot, mask_taps):
        if slot != 1:
            copies(slot)[1].wait()
        weights = cand_dw_buf[:, 0] if slot == 2 else dw_buf[:, slot]
        if mask_taps:
            side = int(round(taps**0.5))
            index = lax.broadcasted_iota(jnp.int32, weights.shape, 0)
            row = sum((index >= side * n).astype(jnp.int32) for n in range(1, side))
            ring = jnp.maximum(jnp.abs(row - side // 2), jnp.abs(index - side * row - side // 2))
            unit = lax.broadcasted_iota(jnp.int32, weights.shape, 1)
            keep = (ring <= radius) & (unit < half_units * (hid // 2))
            weights = jnp.where(keep, weights, 0.0)
        dw_pad[slot, :taps, :hid] = weights

    def forward(slot, lhs, up, down, cols, save, results):
        keep = save is not None
        pre = dot(lhs[...], up[:, cols])
        yield
        half = 0.5 * pre
        bend = jnp.tanh(half)
        more = 1.0 + bend
        wide = half * more
        units = wide.astype(BF16)
        if keep:
            slope_e[:, save] = (more + wide - wide * bend).astype(BF16)
        yield
        tap_re, tap_im = tap_spectrum(slot, cols)
        acts = []
        for m in range(maps):
            here = slice(m * cells, (m + 1) * cells)
            both = dot(analysis, units[here])
            yield
            re, im = split(both)
            if keep:
                spec[m, 0, :, save], spec[m, 1, :, save] = re, im
            mixed_re, mixed_im = re * tap_re - im * tap_im, re * tap_im + im * tap_re
            yield
            mixed = synthesis(mixed_re, mixed_im)
            yield
            half_k = 0.5 * mixed
            bend_k = jnp.tanh(half_k)
            more_k = 1.0 + bend_k
            wide_k = half_k * more_k
            acts.append(wide_k.astype(BF16))
            if keep:
                act[here, save] = acts[-1]
                slope_k[here, save] = (more_k + wide_k - wide_k * bend_k).astype(BF16)
        yield
        results.append(dot_nt(down[:, cols], jnp.concatenate(acts, axis=0)))

    def teacher(slot, lhs, results):
        bounds = list(range(0, max(hid - UNIT // 2, 1), UNIT)) + [hid]
        return [
            forward(slot, lhs, up_buf.at[slot], down_buf.at[slot], slice(lo, hi), None, results)
            for lo, hi in zip(bounds, bounds[1:])
        ]

    def aligned(at, width):
        return pl.ds(pl.multiple_of(at, LANES), width)

    def candidate(lhs, results):
        units = []
        for at in range(0, window, BACK_UNIT):
            width = min(BACK_UNIT, window - at)
            cols = aligned(base + at, width)
            units.append(forward(2, lhs, up_pad, down_pad, cols, slice(at, at + width), results))
        step = max(w for w in (LANES, 2 * LANES, UNIT) if all(b % w == 0 for b in bases))
        for at in range(0, padded - window, step):
            cols = aligned(jnp.where(at < base, at, at + window), min(step, padded - window - at))
            units.append(forward(2, lhs, up_pad, down_pad, cols, None, results))
        return units

    load(0, False)
    for copy in staged:
        copy.wait()
    analysis, even, odd, spectrum, gather_re, gather_im = (ref[...] for ref in constants)
    whole_turn = (
        lax.broadcasted_iota(jnp.int32, (half_cells, half_cells), 0)
        + lax.broadcasted_iota(jnp.int32, (half_cells, half_cells), 1)
    ) == half_cells - 1
    turn_half = whole_turn.astype(F32).astype(BF16)
    for x_ref, offset in zip(x_refs, offsets):
        if offset is None:
            x_first[...] = x_ref[...]
            continue
        block = x_ref.shape[1]
        for n, distance in enumerate(offset):
            source = place ^ distance
            source = (source & (parts - 1)) * (cells // block) + (source >> (parts.bit_length() - 1))
            at = pl.multiple_of(source * block, block)
            x_first[pl.ds(at, block), :] = x_ref[n]
    for m in range(maps):
        second = slice(m * cells + half_cells, (m + 1) * cells)
        x_first[second] = dot(turn_half, x_first[second]).astype(BF16)
    for copy in copies(0)[::2]:
        copy.wait()
    first = []
    interleave(teacher(0, x_first, first))
    branch = sum(first)
    x_next[...] = (x_first[...].astype(F32) + jnp.transpose(branch)).astype(BF16)
    x_now[...] = jnp.where(layer == 0, x_first[...], x_next[...])
    target[...] = branch
    load(2, True)
    load(1, False)
    for copy in copies(2)[::2] + copies(1):
        copy.wait()
    for pad, buf in ((up_pad, up_buf), (down_pad, down_buf)):
        pad[:, hid // LANES * LANES :] = jnp.zeros((channels, padded - hid // LANES * LANES), BF16)
        pad[:, :hid] = buf[2]
    second, third = [], []
    units = [teacher(1, x_next, second), candidate(x_now, third)]
    interleave([unit for pair in itertools.zip_longest(*units) for unit in pair if unit is not None])
    err = (sum(third) - jnp.where(layer == 0, target[...], sum(second))) * scale
    err_now[...] = jnp.transpose(0.5 * err).astype(BF16)
    err_turned[...] = err.astype(BF16)
    x_turned[...] = jnp.transpose(0.5 * x_now[...].astype(F32)).astype(BF16)

    offset = start - base
    shifts = sorted({p * own - at for p, at in enumerate(bases)})

    def leave(wide, out, n, grad):
        for shift in shifts:
            @pl.when(offset == shift)
            def _():
                out[...] = wide[:, shift : shift + own]
        pltpu.make_async_copy(out, grad.at[0], out_sems.at[n]).start()

    wide_up[...] = dot(err_turned[...], act[...])
    leave(wide_up, out_down, 0, grad_down)

    def back(at, width):
        cols = aligned(base + at, width)
        here = slice(at, at + width)
        grad_act = dot(err_now[...], down_pad[:, cols])
        yield
        grad_k = grad_act.astype(BF16) * slope_k[:, here]
        yield
        tap_re, tap_im = tap_spectrum(2, cols)
        sum_re, sum_im = [], []
        grad_pre = []
        for m in range(maps):
            rows_here = slice(m * cells, (m + 1) * cells)
            both = dot(analysis, grad_k[rows_here])
            yield
            re, im = split(both)
            e_re, e_im = spec[m, 0, :, here], spec[m, 1, :, here]
            sum_re.append(re * e_re + im * e_im)
            sum_im.append(re * e_im - im * e_re)
            mixed_re, mixed_im = re * tap_re + im * tap_im, im * tap_re - re * tap_im
            yield
            grad_e = synthesis(mixed_re, mixed_im)
            yield
            grad_pre.append(grad_e.astype(BF16) * slope_e[rows_here, here])
        yield
        wide_up[:, here] = dot(x_turned[...], jnp.concatenate(grad_pre, axis=0))
        wide_dw[:, here] = dot(gather_re, sum(sum_re[1:], sum_re[0])) + dot(gather_im, sum(sum_im[1:], sum_im[0]))

    interleave([back(at, min(BACK_UNIT, window - at)) for at in range(0, window, BACK_UNIT)])

    leave(wide_up, out_up, 1, grad_up)
    for shift in shifts:
        @pl.when(offset == shift)
        def _():
            own_dw = wide_dw[:taps, shift : shift + own]
            side = int(round(taps**0.5))
            index = lax.broadcasted_iota(jnp.int32, own_dw.shape, 0)
            row = sum((index >= side * n).astype(jnp.int32) for n in range(1, side))
            ring = jnp.maximum(jnp.abs(row - side // 2), jnp.abs(index - side * row - side // 2))
            unit = lax.broadcasted_iota(jnp.int32, own_dw.shape, 1) + start
            keep = (ring <= radius) & (unit < half_units * (hid // 2))
            out_dw[:, 0] = jnp.where(keep, own_dw, 0.0)
    pltpu.make_async_copy(out_dw, grad_dw, out_sems.at[2]).start()
    pltpu.make_async_copy(out_down, grad_down.at[0], out_sems.at[0]).wait()
    pltpu.make_async_copy(out_up, grad_up.at[0], out_sems.at[1]).wait()
    pltpu.make_async_copy(out_dw, grad_dw, out_sems.at[2]).wait()


def local_grads(pieces, offsets, maps, flags, parts, images, weights):
    teach_up, teach_dw, teach_down, cand_up, cand_dw, cand_down = weights
    weights = (teach_up, teach_dw.transpose(1, 0, 2), teach_down, cand_up, cand_dw.transpose(1, 0, 2), cand_down)
    channels, hid = teach_up.shape[1:]
    taps = teach_dw.shape[1]
    count = sum(piece.size for piece in pieces) // channels
    cells = count // maps
    side = int(round(cells**0.5))
    rows, constants = dft_matrices(side, taps)
    padded = round_up(hid, LANES)
    own = hid // parts
    spare = max((p * own) % LANES for p in range(parts))
    window = min(round_up(own + spare, LANES), padded)
    tap_rows = round_up(taps, 16)
    dims = (maps, cells, channels, hid, taps, rows, parts, 1.0 / images)
    vmem = pl.BlockSpec(memory_space=pltpu.VMEM)
    anywhere = pl.BlockSpec(memory_space=pl.ANY)
    grad_up, grad_dw, grad_down = pl.pallas_call(
        functools.partial(grads_kernel, dims, offsets),
        out_shape=(
            jax.ShapeDtypeStruct((1, channels, own), F32),
            jax.ShapeDtypeStruct((taps, 1, own), F32),
            jax.ShapeDtypeStruct((1, channels, own), F32),
        ),
        in_specs=[vmem] * (1 + len(pieces)) + [anywhere] * 12,
        out_specs=(anywhere, anywhere, anywhere),
        scratch_shapes=[
            pltpu.VMEM((3, channels, hid), BF16),
            pltpu.VMEM(weights[1].shape, F32),
            pltpu.VMEM(weights[4].shape, F32),
            pltpu.VMEM((3, channels, hid), BF16),
            pltpu.VMEM((3, tap_rows, padded), F32),
            pltpu.VMEM((channels, padded), BF16),
            pltpu.VMEM((channels, padded), BF16),
            pltpu.VMEM((count, window), BF16),
            pltpu.VMEM((maps, 2, rows, window), BF16),
            pltpu.VMEM((count, window), BF16),
            pltpu.VMEM((count, window), BF16),
            pltpu.VMEM((channels, own), F32),
            pltpu.VMEM((taps, 1, own), F32),
            pltpu.VMEM((channels, own), F32),
            pltpu.VMEM((count, channels), BF16),
            pltpu.VMEM((count, channels), BF16),
            pltpu.VMEM((count, channels), BF16),
            pltpu.VMEM((channels, count), BF16),
            pltpu.VMEM((count, channels), BF16),
            pltpu.VMEM((channels, count), BF16),
            pltpu.VMEM((channels, count), F32),
            pltpu.VMEM((channels, window), F32),
            pltpu.VMEM((tap_rows, window), F32),
            pltpu.SemaphoreType.DMA((3, 3)),
            pltpu.SemaphoreType.DMA((len(constants),)),
            pltpu.SemaphoreType.DMA((3,)),
            *[pltpu.VMEM(array.shape, BF16) for array in constants],
        ],
        compiler_params=pltpu.CompilerParams(vmem_limit_bytes=60 * 2**20),
        cost_estimate=pl.CostEstimate(
            flops=20 * count * channels * hid, bytes_accessed=12 * channels * hid, transcendentals=6 * count * hid
        ),
    )(flags, *pieces, *constants, *weights)
    return grad_up, grad_dw.transpose(1, 0, 2), grad_down


def exchange(block, masks, devices, flags):
    offset = [0]
    for mask in masks:
        distances = [d for d in range(1, devices) if d & ~mask == 0]
        parts = [block] + [
            lax.ppermute(block, ("cand", "img"), [(source, source ^ d) for source in range(devices)])
            for d in distances
        ]
        pieces = [[o ^ d for o in offset] for d in [0] + distances]
        offset = sum(pieces, [])
        if mask != masks[-1]:
            block, flags = lax.optimization_barrier((jnp.concatenate(parts, axis=0), flags))
    return parts, pieces, flags


def body(
    first_maps,
    layer_of,
    expand_half,
    radius,
    teach_up,
    teach_dw,
    teach_down,
    cand_up,
    cand_dw,
    cand_down,
):
    parts = lax.axis_size("img")
    cands = lax.axis_size("cand")
    devices = parts * cands
    batch, own_cells, channels = first_maps.shape
    images = parts * batch
    weights = (teach_up, teach_dw, teach_down, cand_up, cand_dw, cand_down)
    flags = jnp.concatenate([layer_of, expand_half, radius]).reshape(1, 3)
    scalars = (flags, parts, images, weights)
    if batch == 1 and images == 2 and own_cells % 16 == 0 and devices & (devices - 1) == 0:
        core = parts * (cands > 1)
        near = (parts - 1) | (2 * core)
        masks = [(devices - 1) & ~near & ~core, near, core]
        pieces, offsets, flags = exchange(first_maps.astype(BF16), masks, devices, flags)
        return local_grads(pieces, offsets, images, flags, *scalars[1:])
    whole = lax.all_gather(first_maps.astype(BF16), ("img", "cand")).reshape(parts, cands, batch, own_cells, channels)
    whole = whole.transpose(0, 2, 1, 3, 4).reshape(images, -1, channels)
    group = 2 if images % 2 == 0 else 1
    total = None
    for first in range(0, images, group):
        pieces = [whole[first : first + group].reshape(-1, channels)]
        grads = local_grads(pieces, [None], group, *scalars)
        total = grads if total is None else tuple(a + b for a, b in zip(total, grads))
    return total


def solution(mesh):
    placed = (
        P("img", "cand", None),
        P("cand"),
        P("cand"),
        P("cand"),
        P(),
        P(),
        P(),
        P("cand", None, None),
        P("cand", None, None),
        P("cand", None, None),
    )
    return jax.shard_map(
        body,
        mesh=mesh,
        in_specs=placed,
        out_specs=(P("cand", None, "img"), P("cand", None, "img"), P("cand", None, "img")),
        check_vma=False,
    )
```

```python
import functools
import itertools

import jax
import jax.numpy as jnp
import ml_dtypes
import numpy as np
from jax import lax
from jax.experimental import pallas as pl
from jax.experimental.pallas import tpu as pltpu
from jax.sharding import PartitionSpec as P

F32 = jnp.float32
BF16 = jnp.bfloat16
LANES = 128
UNIT = 1024
BACK_UNIT = 640
DEPTH = 2
STAGGER = 5


def round_up(value, step):
    return -(-value // step) * step


def dft_matrices(side, taps):
    width = int(round(taps**0.5))
    reach = width // 2
    period = side + reach
    kept = []
    for u in range(period):
        for v in range(period):
            if (u, v) <= ((-u) % period, (-v) % period):
                kept.append((u, v))
    freqs = np.array(kept)
    count = len(kept)
    rows = round_up(count, 8)
    mirrored = ((-freqs) % period == freqs).all(axis=1)
    weight = np.where(mirrored, 1.0, 2.0) / period**2
    cell = np.stack(np.meshgrid(np.arange(side), np.arange(side), indexing="ij"), -1).reshape(-1, 2)
    half = len(cell) // 2
    cell = np.concatenate([cell[:half], cell[half:][::-1]]) - (side - 1) / 2
    tap = np.stack(np.meshgrid(np.arange(width), np.arange(width), indexing="ij"), -1).reshape(-1, 2) - reach
    cell_angle = 2 * np.pi * (freqs @ cell.T) / period
    tap_angle = 2 * np.pi * ((freqs @ tap.T) % period) / period
    tap_rows = round_up(taps, 16)

    analysis = np.zeros((2 * rows, side * side))
    analysis[:count] = np.cos(cell_angle)
    analysis[rows : rows + count] = -np.sin(cell_angle)
    even = np.zeros((half, rows))
    even[:, :count] = (weight[:, None] * np.cos(cell_angle)).T[:half]
    odd = np.zeros((half, rows))
    odd[:, :count] = -(weight[:, None] * np.sin(cell_angle)).T[:half]
    spectrum = np.zeros((2 * rows, tap_rows))
    spectrum[:count, :taps] = np.cos(tap_angle)
    spectrum[rows : rows + count, :taps] = np.sin(tap_angle)
    gather_re, gather_im = np.zeros((tap_rows, rows)), np.zeros((tap_rows, rows))
    gather_re[:taps, :count] = (weight[:, None] * np.cos(tap_angle)).T
    gather_im[:taps, :count] = -(weight[:, None] * np.sin(tap_angle)).T

    coarse = spectrum.astype(ml_dtypes.bfloat16).astype(np.float64)
    spectrum = np.concatenate([coarse, coarse, spectrum - coarse], axis=1)
    matrices = (analysis, even, odd, spectrum, gather_re, gather_im)
    return rows, [jnp.asarray(m.astype(ml_dtypes.bfloat16)) for m in matrices]


def dot(a, b):
    return jnp.dot(a, b, preferred_element_type=F32)


def dot_nt(a, b):
    return lax.dot_general(a, b, (((1,), (1,)), ((), ())), preferred_element_type=F32)


def interleave(units):
    waiting, running = list(units), []
    turn = 0
    while waiting or running:
        if waiting and len(running) < DEPTH and turn % STAGGER == 0:
            running.append(waiting.pop(0))
        turn += 1
        for unit in list(running):
            try:
                next(unit)
            except StopIteration:
                running.remove(unit)


def grads_kernel(
    dims,
    offsets,
    *refs,
):
    pieces = len(offsets)
    flags, refs = refs[0], refs[1:]
    layer, half_units, radius = flags[:, 0:1], flags[:, 1:2], flags[:, 2:3]
    x_refs, in_hbm, refs, constants = refs[:pieces], refs[pieces : pieces + 6], refs[pieces + 6 : -6], refs[-6:]
    (
    teach_up,
    teach_dw,
    teach_down,
    cand_up,
    cand_dw,
    cand_down,
    grad_up,
    grad_dw,
    grad_down,
    up_buf,
    dw_buf,
    cand_dw_buf,
    down_buf,
    dw_pad,
    up_pad,
    down_pad,
    act,
    spec,
    slope_e,
    slope_k,
    out_up,
    out_dw,
    out_down,
    x_first,
    x_next,
    x_now,
    x_turned,
    err_now,
    err_turned,
    target,
    wide_up,
    wide_dw,
    sems,
    in_sems,
    out_sems,
    ) = refs
    maps, cells, channels, hid, taps, rows, parts, scale = dims
    padded = round_up(hid, LANES)
    own = hid // parts
    window = wide_up.shape[1]

    def copies(slot):
        if slot < 2:
            sources = (teach_up.at[slot], teach_dw, teach_down.at[slot])
            targets = (up_buf.at[slot], dw_buf, down_buf.at[slot])
        else:
            sources = (cand_up.at[0], cand_dw, cand_down.at[0])
            targets = (up_buf.at[slot], cand_dw_buf, down_buf.at[slot])
        if slot == 1:
            sources, targets = sources[::2], targets[::2]
        return [
            pltpu.make_async_copy(src, dst, sems.at[slot, n])
            for n, (src, dst) in enumerate(zip(sources, targets))
        ]

    staged = [
        pltpu.make_async_copy(src, dst, in_sems.at[n]) for n, (src, dst) in enumerate(zip(in_hbm, constants))
    ]
    first_copies = copies(0)
    for copy in [first_copies[1], *staged, first_copies[0], first_copies[2], *copies(2), *copies(1)]:
        copy.start()

    dw_pad[...] = jnp.zeros_like(dw_pad)

    half_cells = cells // 2
    bases = [min(p * own // LANES * LANES, padded - window) for p in range(parts)]
    part = lax.axis_index("img")
    place = lax.axis_index("cand") * parts + part
    start = part * own
    base = jnp.minimum(start // LANES * LANES, padded - window)

    def split(both):
        return both[:rows].astype(BF16), both[rows:].astype(BF16)

    def synthesis(re, im):
        same, other = dot(even, re), dot(odd, im)
        return jnp.concatenate([same + other, same - other], axis=0)

    def tap_spectrum(slot, cols):
        weights = dw_pad[slot, :, cols]
        high = weights.astype(BF16)
        low = (weights - high.astype(F32)).astype(BF16)
        return split(dot(spectrum, jnp.concatenate([high, low, high], axis=0)))

    def load(slot, mask_taps):
        if slot != 1:
            copies(slot)[1].wait()
        weights = cand_dw_buf[:, 0] if slot == 2 else dw_buf[:, slot]
        if mask_taps:
            side = int(round(taps**0.5))
            index = lax.broadcasted_iota(jnp.int32, weights.shape, 0)
            row = sum((index >= side * n).astype(jnp.int32) for n in range(1, side))
            ring = jnp.maximum(jnp.abs(row - side // 2), jnp.abs(index - side * row - side // 2))
            unit = lax.broadcasted_iota(jnp.int32, weights.shape, 1)
            keep = (ring <= radius) & (unit < half_units * (hid // 2))
            weights = jnp.where(keep, weights, 0.0)
        dw_pad[slot, :taps, :hid] = weights

    def forward(slot, lhs, up, down, cols, save, results):
        keep = save is not None
        pre = dot(lhs[...], up[:, cols])
        yield
        half = 0.5 * pre
        bend = jnp.tanh(half)
        more = 1.0 + bend
        wide = half * more
        units = wide.astype(BF16)
        if keep:
            slope_e[:, save] = (more + wide - wide * bend).astype(BF16)
        yield
        tap_re, tap_im = tap_spectrum(slot, cols)
        acts = []
        for m in range(maps):
            here = slice(m * cells, (m + 1) * cells)
            both = dot(analysis, units[here])
            yield
            re, im = split(both)
            if keep:
                spec[m, 0, :, save], spec[m, 1, :, save] = re, im
            mixed_re, mixed_im = re * tap_re - im * tap_im, re * tap_im + im * tap_re
            yield
            mixed = synthesis(mixed_re, mixed_im)
            yield
            half_k = 0.5 * mixed
            bend_k = jnp.tanh(half_k)
            more_k = 1.0 + bend_k
            wide_k = half_k * more_k
            acts.append(wide_k.astype(BF16))
            if keep:
                act[here, save] = acts[-1]
                slope_k[here, save] = (more_k + wide_k - wide_k * bend_k).astype(BF16)
        yield
        results.append(dot_nt(down[:, cols], jnp.concatenate(acts, axis=0)))

    def teacher(slot, lhs, results):
        bounds = list(range(0, max(hid - UNIT // 2, 1), UNIT)) + [hid]
        return [
            forward(slot, lhs, up_buf.at[slot], down_buf.at[slot], slice(lo, hi), None, results)
            for lo, hi in zip(bounds, bounds[1:])
        ]

    def aligned(at, width):
        return pl.ds(pl.multiple_of(at, LANES), width)

    def candidate(lhs, results):
        units = []
        for at in range(0, window, BACK_UNIT):
            width = min(BACK_UNIT, window - at)
            cols = aligned(base + at, width)
            units.append(forward(2, lhs, up_pad, down_pad, cols, slice(at, at + width), results))
        step = max(w for w in (LANES, 2 * LANES, UNIT) if all(b % w == 0 for b in bases))
        for at in range(0, padded - window, step):
            cols = aligned(jnp.where(at < base, at, at + window), min(step, padded - window - at))
            units.append(forward(2, lhs, up_pad, down_pad, cols, None, results))
        return units

    load(0, False)
    for copy in staged:
        copy.wait()
    analysis, even, odd, spectrum, gather_re, gather_im = (ref[...] for ref in constants)
    whole_turn = (
        lax.broadcasted_iota(jnp.int32, (half_cells, half_cells), 0)
        + lax.broadcasted_iota(jnp.int32, (half_cells, half_cells), 1)
    ) == half_cells - 1
    turn_half = whole_turn.astype(F32).astype(BF16)
    for x_ref, offset in zip(x_refs, offsets):
        if offset is None:
            x_first[...] = x_ref[...]
            continue
        block = x_ref.shape[1]
        for n, distance in enumerate(offset):
            source = place ^ distance
            source = (source & (parts - 1)) * (cells // block) + (source >> (parts.bit_length() - 1))
            at = pl.multiple_of(source * block, block)
            x_first[pl.ds(at, block), :] = x_ref[n]
    for m in range(maps):
        second = slice(m * cells + half_cells, (m + 1) * cells)
        x_first[second] = dot(turn_half, x_first[second]).astype(BF16)
    for copy in copies(0)[::2]:
        copy.wait()
    first = []
    interleave(teacher(0, x_first, first))
    branch = sum(first)
    x_next[...] = (x_first[...].astype(F32) + jnp.transpose(branch)).astype(BF16)
    x_now[...] = jnp.where(layer == 0, x_first[...], x_next[...])
    target[...] = branch
    load(2, True)
    load(1, False)
    for copy in copies(2)[::2] + copies(1):
        copy.wait()
    for pad, buf in ((up_pad, up_buf), (down_pad, down_buf)):
        pad[:, hid // LANES * LANES :] = jnp.zeros((channels, padded - hid // LANES * LANES), BF16)
        pad[:, :hid] = buf[2]
    second, third = [], []
    units = [teacher(1, x_next, second), candidate(x_now, third)]
    interleave([unit for pair in itertools.zip_longest(*units) for unit in pair if unit is not None])
    err = (sum(third) - jnp.where(layer == 0, target[...], sum(second))) * scale
    err_now[...] = jnp.transpose(0.5 * err).astype(BF16)
    err_turned[...] = err.astype(BF16)
    x_turned[...] = jnp.transpose(0.5 * x_now[...].astype(F32)).astype(BF16)

    offset = start - base
    shifts = sorted({p * own - at for p, at in enumerate(bases)})

    def leave(wide, out, n, grad):
        for shift in shifts:
            @pl.when(offset == shift)
            def _():
                out[...] = wide[:, shift : shift + own]
        pltpu.make_async_copy(out, grad.at[0], out_sems.at[n]).start()

    wide_up[...] = dot(err_turned[...], act[...])
    leave(wide_up, out_down, 0, grad_down)

    def back(at, width):
        cols = aligned(base + at, width)
        here = slice(at, at + width)
        grad_act = dot(err_now[...], down_pad[:, cols])
        yield
        grad_k = grad_act.astype(BF16) * slope_k[:, here]
        yield
        tap_re, tap_im = tap_spectrum(2, cols)
        sum_re, sum_im = [], []
        grad_pre = []
        for m in range(maps):
            rows_here = slice(m * cells, (m + 1) * cells)
            both = dot(analysis, grad_k[rows_here])
            yield
            re, im = split(both)
            e_re, e_im = spec[m, 0, :, here], spec[m, 1, :, here]
            sum_re.append(re * e_re + im * e_im)
            sum_im.append(re * e_im - im * e_re)
            mixed_re, mixed_im = re * tap_re + im * tap_im, im * tap_re - re * tap_im
            yield
            grad_e = synthesis(mixed_re, mixed_im)
            yield
            grad_pre.append(grad_e.astype(BF16) * slope_e[rows_here, here])
        yield
        wide_up[:, here] = dot(x_turned[...], jnp.concatenate(grad_pre, axis=0))
        wide_dw[:, here] = dot(gather_re, sum(sum_re[1:], sum_re[0])) + dot(gather_im, sum(sum_im[1:], sum_im[0]))

    interleave([back(at, min(BACK_UNIT, window - at)) for at in range(0, window, BACK_UNIT)])

    leave(wide_up, out_up, 1, grad_up)
    for shift in shifts:
        @pl.when(offset == shift)
        def _():
            own_dw = wide_dw[:taps, shift : shift + own]
            side = int(round(taps**0.5))
            index = lax.broadcasted_iota(jnp.int32, own_dw.shape, 0)
            row = sum((index >= side * n).astype(jnp.int32) for n in range(1, side))
            ring = jnp.maximum(jnp.abs(row - side // 2), jnp.abs(index - side * row - side // 2))
            unit = lax.broadcasted_iota(jnp.int32, own_dw.shape, 1) + start
            keep = (ring <= radius) & (unit < half_units * (hid // 2))
            out_dw[:, 0] = jnp.where(keep, own_dw, 0.0)
    pltpu.make_async_copy(out_dw, grad_dw, out_sems.at[2]).start()
    pltpu.make_async_copy(out_down, grad_down.at[0], out_sems.at[0]).wait()
    pltpu.make_async_copy(out_up, grad_up.at[0], out_sems.at[1]).wait()
    pltpu.make_async_copy(out_dw, grad_dw, out_sems.at[2]).wait()


def local_grads(pieces, offsets, maps, flags, parts, images, weights):
    teach_up, teach_dw, teach_down, cand_up, cand_dw, cand_down = weights
    weights = (teach_up, teach_dw.transpose(1, 0, 2), teach_down, cand_up, cand_dw.transpose(1, 0, 2), cand_down)
    channels, hid = teach_up.shape[1:]
    taps = teach_dw.shape[1]
    count = sum(piece.size for piece in pieces) // channels
    cells = count // maps
    side = int(round(cells**0.5))
    rows, constants = dft_matrices(side, taps)
    padded = round_up(hid, LANES)
    own = hid // parts
    spare = max((p * own) % LANES for p in range(parts))
    window = min(round_up(own + spare, LANES), padded)
    tap_rows = round_up(taps, 16)
    dims = (maps, cells, channels, hid, taps, rows, parts, 1.0 / images)
    vmem = pl.BlockSpec(memory_space=pltpu.VMEM)
    anywhere = pl.BlockSpec(memory_space=pl.ANY)
    grad_up, grad_dw, grad_down = pl.pallas_call(
        functools.partial(grads_kernel, dims, offsets),
        out_shape=(
            jax.ShapeDtypeStruct((1, channels, own), F32),
            jax.ShapeDtypeStruct((taps, 1, own), F32),
            jax.ShapeDtypeStruct((1, channels, own), F32),
        ),
        in_specs=[vmem] * (1 + len(pieces)) + [anywhere] * 12,
        out_specs=(anywhere, anywhere, anywhere),
        scratch_shapes=[
            pltpu.VMEM((3, channels, hid), BF16),
            pltpu.VMEM(weights[1].shape, F32),
            pltpu.VMEM(weights[4].shape, F32),
            pltpu.VMEM((3, channels, hid), BF16),
            pltpu.VMEM((3, tap_rows, padded), F32),
            pltpu.VMEM((channels, padded), BF16),
            pltpu.VMEM((channels, padded), BF16),
            pltpu.VMEM((count, window), BF16),
            pltpu.VMEM((maps, 2, rows, window), BF16),
            pltpu.VMEM((count, window), BF16),
            pltpu.VMEM((count, window), BF16),
            pltpu.VMEM((channels, own), F32),
            pltpu.VMEM((taps, 1, own), F32),
            pltpu.VMEM((channels, own), F32),
            pltpu.VMEM((count, channels), BF16),
            pltpu.VMEM((count, channels), BF16),
            pltpu.VMEM((count, channels), BF16),
            pltpu.VMEM((channels, count), BF16),
            pltpu.VMEM((count, channels), BF16),
            pltpu.VMEM((channels, count), BF16),
            pltpu.VMEM((channels, count), F32),
            pltpu.VMEM((channels, window), F32),
            pltpu.VMEM((tap_rows, window), F32),
            pltpu.SemaphoreType.DMA((3, 3)),
            pltpu.SemaphoreType.DMA((len(constants),)),
            pltpu.SemaphoreType.DMA((3,)),
            *[pltpu.VMEM(array.shape, BF16) for array in constants],
        ],
        compiler_params=pltpu.CompilerParams(vmem_limit_bytes=60 * 2**20),
        cost_estimate=pl.CostEstimate(
            flops=20 * count * channels * hid, bytes_accessed=12 * channels * hid, transcendentals=6 * count * hid
        ),
    )(flags, *pieces, *constants, *weights)
    return grad_up, grad_dw.transpose(1, 0, 2), grad_down


def exchange(block, masks, devices, flags):
    offset = [0]
    for mask in masks:
        distances = [d for d in range(1, devices) if d & ~mask == 0]
        parts = [block] + [
            lax.ppermute(block, ("cand", "img"), [(source, source ^ d) for source in range(devices)])
            for d in distances
        ]
        pieces = [[o ^ d for o in offset] for d in [0] + distances]
        offset = sum(pieces, [])
        if mask != masks[-1]:
            block = jnp.concatenate(parts, axis=0)
        if mask == masks[-2]:
            block, flags = lax.optimization_barrier((block, flags))
    return parts, pieces, flags


def body(
    first_maps,
    layer_of,
    expand_half,
    radius,
    teach_up,
    teach_dw,
    teach_down,
    cand_up,
    cand_dw,
    cand_down,
):
    parts = lax.axis_size("img")
    cands = lax.axis_size("cand")
    devices = parts * cands
    batch, own_cells, channels = first_maps.shape
    images = parts * batch
    weights = (teach_up, teach_dw, teach_down, cand_up, cand_dw, cand_down)
    flags = jnp.concatenate([layer_of, expand_half, radius]).reshape(1, 3)
    scalars = (flags, parts, images, weights)
    if batch == 1 and images == 2 and own_cells % 16 == 0 and devices & (devices - 1) == 0:
        core = parts * (cands > 1)
        near = (parts - 1) | (2 * core)
        masks = [(devices - 1) & ~near & ~core, near, core]
        pieces, offsets, flags = exchange(first_maps.astype(BF16), masks, devices, flags)
        return local_grads(pieces, offsets, images, flags, *scalars[1:])
    whole = lax.all_gather(first_maps.astype(BF16), ("img", "cand")).reshape(parts, cands, batch, own_cells, channels)
    whole = whole.transpose(0, 2, 1, 3, 4).reshape(images, -1, channels)
    group = 2 if images % 2 == 0 else 1
    total = None
    for first in range(0, images, group):
        pieces = [whole[first : first + group].reshape(-1, channels)]
        grads = local_grads(pieces, [None], group, *scalars)
        total = grads if total is None else tuple(a + b for a, b in zip(total, grads))
    return total


def solution(mesh):
    placed = (
        P("img", "cand", None),
        P("cand"),
        P("cand"),
        P("cand"),
        P(),
        P(),
        P(),
        P("cand", None, None),
        P("cand", None, None),
        P("cand", None, None),
    )
    return jax.shard_map(
        body,
        mesh=mesh,
        in_specs=placed,
        out_specs=(P("cand", None, "img"), P("cand", None, "img"), P("cand", None, "img")),
        check_vma=False,
    )
```

```python
import functools
import itertools

import jax
import jax.numpy as jnp
import ml_dtypes
import numpy as np
from jax import lax
from jax.experimental import pallas as pl
from jax.experimental.pallas import tpu as pltpu
from jax.sharding import PartitionSpec as P

F32 = jnp.float32
BF16 = jnp.bfloat16
LANES = 128
UNIT = 1024
BACK_UNIT = 640
DEPTH = 2
STAGGER = 5


def round_up(value, step):
    return -(-value // step) * step


def dft_matrices(side, taps):
    width = int(round(taps**0.5))
    reach = width // 2
    period = side + reach
    kept = []
    for u in range(period):
        for v in range(period):
            if (u, v) <= ((-u) % period, (-v) % period):
                kept.append((u, v))
    freqs = np.array(kept)
    count = len(kept)
    rows = round_up(count, 8)
    mirrored = ((-freqs) % period == freqs).all(axis=1)
    weight = np.where(mirrored, 1.0, 2.0) / period**2
    cell = np.stack(np.meshgrid(np.arange(side), np.arange(side), indexing="ij"), -1).reshape(-1, 2)
    half = len(cell) // 2
    cell = np.concatenate([cell[:half], cell[half:][::-1]]) - (side - 1) / 2
    tap = np.stack(np.meshgrid(np.arange(width), np.arange(width), indexing="ij"), -1).reshape(-1, 2) - reach
    cell_angle = 2 * np.pi * (freqs @ cell.T) / period
    tap_angle = 2 * np.pi * ((freqs @ tap.T) % period) / period
    tap_rows = round_up(taps, 16)

    analysis = np.zeros((2 * rows, side * side))
    analysis[:count] = np.cos(cell_angle)
    analysis[rows : rows + count] = -np.sin(cell_angle)
    even = np.zeros((half, rows))
    even[:, :count] = (weight[:, None] * np.cos(cell_angle)).T[:half]
    odd = np.zeros((half, rows))
    odd[:, :count] = -(weight[:, None] * np.sin(cell_angle)).T[:half]
    spectrum = np.zeros((2 * rows, tap_rows))
    spectrum[:count, :taps] = np.cos(tap_angle)
    spectrum[rows : rows + count, :taps] = np.sin(tap_angle)
    gather_re, gather_im = np.zeros((tap_rows, rows)), np.zeros((tap_rows, rows))
    gather_re[:taps, :count] = (weight[:, None] * np.cos(tap_angle)).T
    gather_im[:taps, :count] = -(weight[:, None] * np.sin(tap_angle)).T

    coarse = spectrum.astype(ml_dtypes.bfloat16).astype(np.float64)
    spectrum = np.concatenate([coarse, coarse, spectrum - coarse], axis=1)
    matrices = (analysis, even, odd, spectrum, gather_re, gather_im)
    return rows, [jnp.asarray(m.astype(ml_dtypes.bfloat16)) for m in matrices]


def dot(a, b):
    return jnp.dot(a, b, preferred_element_type=F32)


def dot_nt(a, b):
    return lax.dot_general(a, b, (((1,), (1,)), ((), ())), preferred_element_type=F32)


def interleave(units):
    waiting, running = list(units), []
    turn = 0
    while waiting or running:
        if waiting and len(running) < DEPTH and turn % STAGGER == 0:
            running.append(waiting.pop(0))
        turn += 1
        for unit in list(running):
            try:
                next(unit)
            except StopIteration:
                running.remove(unit)


def grads_kernel(
    dims,
    offsets,
    *refs,
):
    pieces = len(offsets)
    flags, refs = refs[0], refs[1:]
    layer, half_units, radius = flags[:, 0:1], flags[:, 1:2], flags[:, 2:3]
    count = pieces + 6
    in_hbm, refs, in_vmem = refs[:count], refs[count:-count], refs[-count:]
    x_refs, constants = in_vmem[:pieces], in_vmem[pieces:]
    (
    teach_up,
    teach_dw,
    teach_down,
    cand_up,
    cand_dw,
    cand_down,
    grad_up,
    grad_dw,
    grad_down,
    up_buf,
    dw_buf,
    cand_dw_buf,
    down_buf,
    dw_pad,
    up_pad,
    down_pad,
    act,
    spec,
    slope_e,
    slope_k,
    out_up,
    out_dw,
    out_down,
    x_first,
    x_next,
    x_now,
    x_turned,
    err_now,
    err_turned,
    target,
    wide_up,
    wide_dw,
    sems,
    in_sems,
    out_sems,
    ) = refs
    maps, cells, channels, hid, taps, rows, parts, scale = dims
    padded = round_up(hid, LANES)
    own = hid // parts
    window = wide_up.shape[1]

    def copies(slot):
        if slot < 2:
            sources = (teach_up.at[slot], teach_dw, teach_down.at[slot])
            targets = (up_buf.at[slot], dw_buf, down_buf.at[slot])
        else:
            sources = (cand_up.at[0], cand_dw, cand_down.at[0])
            targets = (up_buf.at[slot], cand_dw_buf, down_buf.at[slot])
        if slot == 1:
            sources, targets = sources[::2], targets[::2]
        return [
            pltpu.make_async_copy(src, dst, sems.at[slot, n])
            for n, (src, dst) in enumerate(zip(sources, targets))
        ]

    staged = [
        pltpu.make_async_copy(src, dst, in_sems.at[n]) for n, (src, dst) in enumerate(zip(in_hbm, in_vmem))
    ]
    first_copies = copies(0)
    for copy in [first_copies[1], *staged, first_copies[0], first_copies[2]]:
        copy.start()

    dw_pad[...] = jnp.zeros_like(dw_pad)

    half_cells = cells // 2
    bases = [min(p * own // LANES * LANES, padded - window) for p in range(parts)]
    part = lax.axis_index("img")
    place = lax.axis_index("cand") * parts + part
    start = part * own
    base = jnp.minimum(start // LANES * LANES, padded - window)

    def split(both):
        return both[:rows].astype(BF16), both[rows:].astype(BF16)

    def synthesis(re, im):
        same, other = dot(even, re), dot(odd, im)
        return jnp.concatenate([same + other, same - other], axis=0)

    def tap_spectrum(slot, cols):
        weights = dw_pad[slot, :, cols]
        high = weights.astype(BF16)
        low = (weights - high.astype(F32)).astype(BF16)
        return split(dot(spectrum, jnp.concatenate([high, low, high], axis=0)))

    def load(slot, mask_taps):
        if slot != 1:
            copies(slot)[1].wait()
        weights = cand_dw_buf[:, 0] if slot == 2 else dw_buf[:, slot]
        if mask_taps:
            side = int(round(taps**0.5))
            index = lax.broadcasted_iota(jnp.int32, weights.shape, 0)
            row = sum((index >= side * n).astype(jnp.int32) for n in range(1, side))
            ring = jnp.maximum(jnp.abs(row - side // 2), jnp.abs(index - side * row - side // 2))
            unit = lax.broadcasted_iota(jnp.int32, weights.shape, 1)
            keep = (ring <= radius) & (unit < half_units * (hid // 2))
            weights = jnp.where(keep, weights, 0.0)
        dw_pad[slot, :taps, :hid] = weights

    def forward(slot, lhs, up, down, cols, save, results):
        keep = save is not None
        pre = dot(lhs[...], up[:, cols])
        yield
        half = 0.5 * pre
        bend = jnp.tanh(half)
        more = 1.0 + bend
        wide = half * more
        units = wide.astype(BF16)
        if keep:
            slope_e[:, save] = (more + wide - wide * bend).astype(BF16)
        yield
        tap_re, tap_im = tap_spectrum(slot, cols)
        acts = []
        for m in range(maps):
            here = slice(m * cells, (m + 1) * cells)
            both = dot(analysis, units[here])
            yield
            re, im = split(both)
            if keep:
                spec[m, 0, :, save], spec[m, 1, :, save] = re, im
            mixed_re, mixed_im = re * tap_re - im * tap_im, re * tap_im + im * tap_re
            yield
            mixed = synthesis(mixed_re, mixed_im)
            yield
            half_k = 0.5 * mixed
            bend_k = jnp.tanh(half_k)
            more_k = 1.0 + bend_k
            wide_k = half_k * more_k
            acts.append(wide_k.astype(BF16))
            if keep:
                act[here, save] = acts[-1]
                slope_k[here, save] = (more_k + wide_k - wide_k * bend_k).astype(BF16)
        yield
        results.append(dot_nt(down[:, cols], jnp.concatenate(acts, axis=0)))

    def teacher(slot, lhs, results):
        bounds = list(range(0, max(hid - UNIT // 2, 1), UNIT)) + [hid]
        return [
            forward(slot, lhs, up_buf.at[slot], down_buf.at[slot], slice(lo, hi), None, results)
            for lo, hi in zip(bounds, bounds[1:])
        ]

    def aligned(at, width):
        return pl.ds(pl.multiple_of(at, LANES), width)

    def candidate(lhs, results):
        units = []
        for at in range(0, window, BACK_UNIT):
            width = min(BACK_UNIT, window - at)
            cols = aligned(base + at, width)
            units.append(forward(2, lhs, up_pad, down_pad, cols, slice(at, at + width), results))
        step = max(w for w in (LANES, 2 * LANES, UNIT) if all(b % w == 0 for b in bases))
        for at in range(0, padded - window, step):
            cols = aligned(jnp.where(at < base, at, at + window), min(step, padded - window - at))
            units.append(forward(2, lhs, up_pad, down_pad, cols, None, results))
        return units

    load(0, False)
    for copy in staged:
        copy.wait()
    analysis, even, odd, spectrum, gather_re, gather_im = (ref[...] for ref in constants)
    whole_turn = (
        lax.broadcasted_iota(jnp.int32, (half_cells, half_cells), 0)
        + lax.broadcasted_iota(jnp.int32, (half_cells, half_cells), 1)
    ) == half_cells - 1
    turn_half = whole_turn.astype(F32).astype(BF16)
    for x_ref, offset in zip(x_refs, offsets):
        if offset is None:
            x_first[...] = x_ref[...]
            continue
        block = x_ref.shape[1]
        for n, distance in enumerate(offset):
            source = place ^ distance
            source = (source & (parts - 1)) * (cells // block) + (source >> (parts.bit_length() - 1))
            at = pl.multiple_of(source * block, block)
            x_first[pl.ds(at, block), :] = x_ref[n]
    for m in range(maps):
        second = slice(m * cells + half_cells, (m + 1) * cells)
        x_first[second] = dot(turn_half, x_first[second]).astype(BF16)
    for copy in copies(0)[::2]:
        copy.wait()
    for copy in copies(2) + copies(1):
        copy.start()
    first = []
    interleave(teacher(0, x_first, first))
    branch = sum(first)
    x_next[...] = (x_first[...].astype(F32) + jnp.transpose(branch)).astype(BF16)
    x_now[...] = jnp.where(layer == 0, x_first[...], x_next[...])
    target[...] = branch
    load(2, True)
    load(1, False)
    for copy in copies(2)[::2] + copies(1):
        copy.wait()
    for pad, buf in ((up_pad, up_buf), (down_pad, down_buf)):
        pad[:, hid // LANES * LANES :] = jnp.zeros((channels, padded - hid // LANES * LANES), BF16)
        pad[:, :hid] = buf[2]
    second, third = [], []
    units = [teacher(1, x_next, second), candidate(x_now, third)]
    interleave([unit for pair in itertools.zip_longest(*units) for unit in pair if unit is not None])
    err = (sum(third) - jnp.where(layer == 0, target[...], sum(second))) * scale
    err_now[...] = jnp.transpose(0.5 * err).astype(BF16)
    err_turned[...] = err.astype(BF16)
    x_turned[...] = jnp.transpose(0.5 * x_now[...].astype(F32)).astype(BF16)

    offset = start - base
    shifts = sorted({p * own - at for p, at in enumerate(bases)})

    def leave(wide, out, n, grad):
        for shift in shifts:
            @pl.when(offset == shift)
            def _():
                out[...] = wide[:, shift : shift + own]
        pltpu.make_async_copy(out, grad.at[0], out_sems.at[n]).start()

    wide_up[...] = dot(err_turned[...], act[...])
    leave(wide_up, out_down, 0, grad_down)

    def back(at, width):
        cols = aligned(base + at, width)
        here = slice(at, at + width)
        grad_act = dot(err_now[...], down_pad[:, cols])
        yield
        grad_k = grad_act.astype(BF16) * slope_k[:, here]
        yield
        tap_re, tap_im = tap_spectrum(2, cols)
        sum_re, sum_im = [], []
        grad_pre = []
        for m in range(maps):
            rows_here = slice(m * cells, (m + 1) * cells)
            both = dot(analysis, grad_k[rows_here])
            yield
            re, im = split(both)
            e_re, e_im = spec[m, 0, :, here], spec[m, 1, :, here]
            sum_re.append(re * e_re + im * e_im)
            sum_im.append(re * e_im - im * e_re)
            mixed_re, mixed_im = re * tap_re + im * tap_im, im * tap_re - re * tap_im
            yield
            grad_e = synthesis(mixed_re, mixed_im)
            yield
            grad_pre.append(grad_e.astype(BF16) * slope_e[rows_here, here])
        yield
        wide_up[:, here] = dot(x_turned[...], jnp.concatenate(grad_pre, axis=0))
        wide_dw[:, here] = dot(gather_re, sum(sum_re[1:], sum_re[0])) + dot(gather_im, sum(sum_im[1:], sum_im[0]))

    interleave([back(at, min(BACK_UNIT, window - at)) for at in range(0, window, BACK_UNIT)])

    leave(wide_up, out_up, 1, grad_up)
    for shift in shifts:
        @pl.when(offset == shift)
        def _():
            own_dw = wide_dw[:taps, shift : shift + own]
            side = int(round(taps**0.5))
            index = lax.broadcasted_iota(jnp.int32, own_dw.shape, 0)
            row = sum((index >= side * n).astype(jnp.int32) for n in range(1, side))
            ring = jnp.maximum(jnp.abs(row - side // 2), jnp.abs(index - side * row - side // 2))
            unit = lax.broadcasted_iota(jnp.int32, own_dw.shape, 1) + start
            keep = (ring <= radius) & (unit < half_units * (hid // 2))
            out_dw[:, 0] = jnp.where(keep, own_dw, 0.0)
    pltpu.make_async_copy(out_dw, grad_dw, out_sems.at[2]).start()
    pltpu.make_async_copy(out_down, grad_down.at[0], out_sems.at[0]).wait()
    pltpu.make_async_copy(out_up, grad_up.at[0], out_sems.at[1]).wait()
    pltpu.make_async_copy(out_dw, grad_dw, out_sems.at[2]).wait()


def local_grads(pieces, offsets, maps, flags, parts, images, weights):
    teach_up, teach_dw, teach_down, cand_up, cand_dw, cand_down = weights
    weights = (teach_up, teach_dw.transpose(1, 0, 2), teach_down, cand_up, cand_dw.transpose(1, 0, 2), cand_down)
    channels, hid = teach_up.shape[1:]
    taps = teach_dw.shape[1]
    count = sum(piece.size for piece in pieces) // channels
    cells = count // maps
    side = int(round(cells**0.5))
    rows, constants = dft_matrices(side, taps)
    padded = round_up(hid, LANES)
    own = hid // parts
    spare = max((p * own) % LANES for p in range(parts))
    window = min(round_up(own + spare, LANES), padded)
    tap_rows = round_up(taps, 16)
    dims = (maps, cells, channels, hid, taps, rows, parts, 1.0 / images)
    vmem = pl.BlockSpec(memory_space=pltpu.VMEM)
    anywhere = pl.BlockSpec(memory_space=pl.ANY)
    grad_up, grad_dw, grad_down = pl.pallas_call(
        functools.partial(grads_kernel, dims, offsets),
        out_shape=(
            jax.ShapeDtypeStruct((1, channels, own), F32),
            jax.ShapeDtypeStruct((taps, 1, own), F32),
            jax.ShapeDtypeStruct((1, channels, own), F32),
        ),
        in_specs=[vmem] + [anywhere] * (len(pieces) + 12),
        out_specs=(anywhere, anywhere, anywhere),
        scratch_shapes=[
            pltpu.VMEM((3, channels, hid), BF16),
            pltpu.VMEM(weights[1].shape, F32),
            pltpu.VMEM(weights[4].shape, F32),
            pltpu.VMEM((3, channels, hid), BF16),
            pltpu.VMEM((3, tap_rows, padded), F32),
            pltpu.VMEM((channels, padded), BF16),
            pltpu.VMEM((channels, padded), BF16),
            pltpu.VMEM((count, window), BF16),
            pltpu.VMEM((maps, 2, rows, window), BF16),
            pltpu.VMEM((count, window), BF16),
            pltpu.VMEM((count, window), BF16),
            pltpu.VMEM((channels, own), F32),
            pltpu.VMEM((taps, 1, own), F32),
            pltpu.VMEM((channels, own), F32),
            pltpu.VMEM((count, channels), BF16),
            pltpu.VMEM((count, channels), BF16),
            pltpu.VMEM((count, channels), BF16),
            pltpu.VMEM((channels, count), BF16),
            pltpu.VMEM((count, channels), BF16),
            pltpu.VMEM((channels, count), BF16),
            pltpu.VMEM((channels, count), F32),
            pltpu.VMEM((channels, window), F32),
            pltpu.VMEM((tap_rows, window), F32),
            pltpu.SemaphoreType.DMA((3, 3)),
            pltpu.SemaphoreType.DMA((len(pieces) + len(constants),)),
            pltpu.SemaphoreType.DMA((3,)),
            *[pltpu.VMEM(array.shape, BF16) for array in (*pieces, *constants)],
        ],
        compiler_params=pltpu.CompilerParams(vmem_limit_bytes=60 * 2**20),
        cost_estimate=pl.CostEstimate(
            flops=20 * count * channels * hid, bytes_accessed=12 * channels * hid, transcendentals=6 * count * hid
        ),
    )(flags, *pieces, *constants, *weights)
    return grad_up, grad_dw.transpose(1, 0, 2), grad_down


def exchange(block, masks, devices, flags):
    offset = [0]
    for mask in masks:
        distances = [d for d in range(1, devices) if d & ~mask == 0]
        parts = [block] + [
            lax.ppermute(block, ("cand", "img"), [(source, source ^ d) for source in range(devices)])
            for d in distances
        ]
        pieces = [[o ^ d for o in offset] for d in [0] + distances]
        offset = sum(pieces, [])
        if mask != masks[-1]:
            block = jnp.concatenate(parts, axis=0)
        if mask == masks[0]:
            block, flags = lax.optimization_barrier((block, flags))
            flags = jnp.concatenate(flags).reshape(1, 3)
        elif mask == masks[1]:
            block, flags = lax.optimization_barrier((block, flags))
    return parts, pieces, flags


def body(
    first_maps,
    layer_of,
    expand_half,
    radius,
    teach_up,
    teach_dw,
    teach_down,
    cand_up,
    cand_dw,
    cand_down,
):
    parts = lax.axis_size("img")
    cands = lax.axis_size("cand")
    devices = parts * cands
    batch, own_cells, channels = first_maps.shape
    images = parts * batch
    weights = (teach_up, teach_dw, teach_down, cand_up, cand_dw, cand_down)
    flags = (layer_of, expand_half, radius)
    scalars = (jnp.concatenate(flags).reshape(1, 3), parts, images, weights)
    if batch == 1 and images == 2 and own_cells % 16 == 0 and devices & (devices - 1) == 0:
        core = parts * (cands > 1)
        near = (parts - 1) | (2 * core)
        masks = [(devices - 1) & ~near & ~core, near, core]
        pieces, offsets, flags = exchange(first_maps.astype(BF16), masks, devices, flags)
        return local_grads(pieces, offsets, images, flags, *scalars[1:])
    whole = lax.all_gather(first_maps.astype(BF16), ("img", "cand")).reshape(parts, cands, batch, own_cells, channels)
    whole = whole.transpose(0, 2, 1, 3, 4).reshape(images, -1, channels)
    group = 2 if images % 2 == 0 else 1
    total = None
    for first in range(0, images, group):
        pieces = [whole[first : first + group].reshape(-1, channels)]
        grads = local_grads(pieces, [None], group, *scalars)
        total = grads if total is None else tuple(a + b for a, b in zip(total, grads))
    return total


def solution(mesh):
    placed = (
        P("img", "cand", None),
        P("cand"),
        P("cand"),
        P("cand"),
        P(),
        P(),
        P(),
        P("cand", None, None),
        P("cand", None, None),
        P("cand", None, None),
    )
    return jax.shard_map(
        body,
        mesh=mesh,
        in_specs=placed,
        out_specs=(P("cand", None, "img"), P("cand", None, "img"), P("cand", None, "img")),
        check_vma=False,
    )
```

```python
import functools
import itertools

import jax
import jax.numpy as jnp
import ml_dtypes
import numpy as np
from jax import lax
from jax.experimental import pallas as pl
from jax.experimental.pallas import tpu as pltpu
from jax.sharding import PartitionSpec as P

F32 = jnp.float32
BF16 = jnp.bfloat16
LANES = 128
UNIT = 1024
BACK_UNIT = 640
DEPTH = 3
STAGGER = 2


def round_up(value, step):
    return -(-value // step) * step


def dft_matrices(side, taps):
    width = int(round(taps**0.5))
    reach = width // 2
    period = side + reach
    kept = []
    for u in range(period):
        for v in range(period):
            if (u, v) <= ((-u) % period, (-v) % period):
                kept.append((u, v))
    freqs = np.array(kept)
    count = len(kept)
    rows = round_up(count, 8)
    mirrored = ((-freqs) % period == freqs).all(axis=1)
    weight = np.where(mirrored, 1.0, 2.0) / period**2
    cell = np.stack(np.meshgrid(np.arange(side), np.arange(side), indexing="ij"), -1).reshape(-1, 2)
    half = len(cell) // 2
    cell = np.concatenate([cell[:half], cell[half:][::-1]]) - (side - 1) / 2
    tap = np.stack(np.meshgrid(np.arange(width), np.arange(width), indexing="ij"), -1).reshape(-1, 2) - reach
    cell_angle = 2 * np.pi * (freqs @ cell.T) / period
    tap_angle = 2 * np.pi * ((freqs @ tap.T) % period) / period
    tap_rows = round_up(taps, 16)

    analysis = np.zeros((2 * rows, side * side))
    analysis[:count] = np.cos(cell_angle)
    analysis[rows : rows + count] = -np.sin(cell_angle)
    even = np.zeros((half, rows))
    even[:, :count] = (weight[:, None] * np.cos(cell_angle)).T[:half]
    odd = np.zeros((half, rows))
    odd[:, :count] = -(weight[:, None] * np.sin(cell_angle)).T[:half]
    spectrum = np.zeros((2 * rows, tap_rows))
    spectrum[:count, :taps] = np.cos(tap_angle)
    spectrum[rows : rows + count, :taps] = np.sin(tap_angle)
    gather_re, gather_im = np.zeros((tap_rows, rows)), np.zeros((tap_rows, rows))
    gather_re[:taps, :count] = (weight[:, None] * np.cos(tap_angle)).T
    gather_im[:taps, :count] = -(weight[:, None] * np.sin(tap_angle)).T

    coarse = spectrum.astype(ml_dtypes.bfloat16).astype(np.float64)
    spectrum = np.concatenate([coarse, coarse, spectrum - coarse], axis=1)
    matrices = (analysis, even, odd, spectrum, gather_re, gather_im)
    return rows, [jnp.asarray(m.astype(ml_dtypes.bfloat16)) for m in matrices]


def dot(a, b):
    return jnp.dot(a, b, preferred_element_type=F32)


def dot_nt(a, b):
    return lax.dot_general(a, b, (((1,), (1,)), ((), ())), preferred_element_type=F32)


def interleave(units):
    waiting, running = list(units), []
    turn = 0
    while waiting or running:
        if waiting and len(running) < DEPTH and turn % STAGGER == 0:
            running.append(waiting.pop(0))
        turn += 1
        for unit in list(running):
            try:
                next(unit)
            except StopIteration:
                running.remove(unit)


def grads_kernel(
    dims,
    offsets,
    *refs,
):
    pieces = len(offsets)
    flags, refs = refs[0], refs[1:]
    layer, half_units, radius = flags[:, 0:1], flags[:, 1:2], flags[:, 2:3]
    count = pieces + 6
    in_hbm, refs, in_vmem = refs[:count], refs[count:-count], refs[-count:]
    x_refs, constants = in_vmem[:pieces], in_vmem[pieces:]
    (
    teach_up,
    teach_dw,
    teach_down,
    cand_up,
    cand_dw,
    cand_down,
    grad_up,
    grad_dw,
    grad_down,
    up_buf,
    dw_buf,
    cand_dw_buf,
    down_buf,
    dw_pad,
    up_pad,
    down_pad,
    act,
    spec,
    slope_e,
    slope_k,
    out_up,
    out_dw,
    out_down,
    x_first,
    x_next,
    x_now,
    x_turned,
    err_now,
    err_turned,
    target,
    wide_up,
    wide_dw,
    sems,
    in_sems,
    out_sems,
    ) = refs
    maps, cells, channels, hid, taps, rows, parts, scale = dims
    padded = round_up(hid, LANES)
    own = hid // parts
    window = wide_up.shape[1]

    def copies(slot):
        if slot < 2:
            sources = (teach_up.at[slot], teach_dw, teach_down.at[slot])
            targets = (up_buf.at[slot], dw_buf, down_buf.at[slot])
        else:
            sources = (cand_up.at[0], cand_dw, cand_down.at[0])
            targets = (up_buf.at[slot], cand_dw_buf, down_buf.at[slot])
        if slot == 1:
            sources, targets = sources[::2], targets[::2]
        return [
            pltpu.make_async_copy(src, dst, sems.at[slot, n])
            for n, (src, dst) in enumerate(zip(sources, targets))
        ]

    staged = [
        pltpu.make_async_copy(src, dst, in_sems.at[n]) for n, (src, dst) in enumerate(zip(in_hbm, in_vmem))
    ]
    first_copies = copies(0)
    for copy in [first_copies[1], *staged, first_copies[0], first_copies[2]]:
        copy.start()

    dw_pad[...] = jnp.zeros_like(dw_pad)

    half_cells = cells // 2
    bases = [min(p * own // LANES * LANES, padded - window) for p in range(parts)]
    part = lax.axis_index("img")
    place = lax.axis_index("cand") * parts + part
    start = part * own
    base = jnp.minimum(start // LANES * LANES, padded - window)

    def split(both):
        return both[:rows].astype(BF16), both[rows:].astype(BF16)

    def synthesis(re, im):
        same, other = dot(even, re), dot(odd, im)
        return jnp.concatenate([same + other, same - other], axis=0)

    def tap_spectrum(slot, cols):
        weights = dw_pad[slot, :, cols]
        high = weights.astype(BF16)
        low = (weights - high.astype(F32)).astype(BF16)
        return split(dot(spectrum, jnp.concatenate([high, low, high], axis=0)))

    def load(slot, mask_taps):
        if slot != 1:
            copies(slot)[1].wait()
        weights = cand_dw_buf[:, 0] if slot == 2 else dw_buf[:, slot]
        if mask_taps:
            side = int(round(taps**0.5))
            index = lax.broadcasted_iota(jnp.int32, weights.shape, 0)
            row = sum((index >= side * n).astype(jnp.int32) for n in range(1, side))
            ring = jnp.maximum(jnp.abs(row - side // 2), jnp.abs(index - side * row - side // 2))
            unit = lax.broadcasted_iota(jnp.int32, weights.shape, 1)
            keep = (ring <= radius) & (unit < half_units * (hid // 2))
            weights = jnp.where(keep, weights, 0.0)
        dw_pad[slot, :taps, :hid] = weights

    def forward(slot, lhs, up, down, cols, save, results, copy=None):
        keep = save is not None
        pre = dot(lhs[...], up[:, cols])
        yield
        half = 0.5 * pre
        bend = jnp.tanh(half)
        more = 1.0 + bend
        wide = half * more
        units = wide.astype(BF16)
        if keep:
            slope_e[:, save] = (more + wide - wide * bend).astype(BF16)
        yield
        tap_re, tap_im = tap_spectrum(slot, cols)
        acts = []
        for m in range(maps):
            here = slice(m * cells, (m + 1) * cells)
            both = dot(analysis, units[here])
            yield
            re, im = split(both)
            if keep:
                spec[m, 0, :, save], spec[m, 1, :, save] = re, im
            mixed_re, mixed_im = re * tap_re - im * tap_im, re * tap_im + im * tap_re
            yield
            mixed = synthesis(mixed_re, mixed_im)
            yield
            half_k = 0.5 * mixed
            bend_k = jnp.tanh(half_k)
            more_k = 1.0 + bend_k
            wide_k = half_k * more_k
            acts.append(wide_k.astype(BF16))
            if keep:
                act[here, save] = acts[-1]
                slope_k[here, save] = (more_k + wide_k - wide_k * bend_k).astype(BF16)
        yield
        if copy is not None:
            copy.wait()
        results.append(dot_nt(down[:, cols], jnp.concatenate(acts, axis=0)))

    def teacher(slot, lhs, results, copy=None):
        bounds = list(range(0, max(hid - UNIT // 2, 1), UNIT)) + [hid]
        return [
            forward(slot, lhs, up_buf.at[slot], down_buf.at[slot], slice(lo, hi), None, results, copy if lo == 0 else None)
            for lo, hi in zip(bounds, bounds[1:])
        ]

    def aligned(at, width):
        return pl.ds(pl.multiple_of(at, LANES), width)

    def candidate(lhs, results):
        units = []
        for at in range(0, window, BACK_UNIT):
            width = min(BACK_UNIT, window - at)
            cols = aligned(base + at, width)
            units.append(forward(2, lhs, up_pad, down_pad, cols, slice(at, at + width), results))
        step = max(w for w in (LANES, 2 * LANES, UNIT) if all(b % w == 0 for b in bases))
        for at in range(0, padded - window, step):
            cols = aligned(jnp.where(at < base, at, at + window), min(step, padded - window - at))
            units.append(forward(2, lhs, up_pad, down_pad, cols, None, results))
        return units

    load(0, False)
    for copy in staged:
        copy.wait()
    analysis, even, odd, spectrum, gather_re, gather_im = (ref[...] for ref in constants)
    whole_turn = (
        lax.broadcasted_iota(jnp.int32, (half_cells, half_cells), 0)
        + lax.broadcasted_iota(jnp.int32, (half_cells, half_cells), 1)
    ) == half_cells - 1
    turn_half = whole_turn.astype(F32).astype(BF16)
    for x_ref, offset in zip(x_refs, offsets):
        if offset is None:
            x_first[...] = x_ref[...]
            continue
        block = x_ref.shape[1]
        for n, distance in enumerate(offset):
            source = place ^ distance
            source = (source & (parts - 1)) * (cells // block) + (source >> (parts.bit_length() - 1))
            at = pl.multiple_of(source * block, block)
            x_first[pl.ds(at, block), :] = x_ref[n]
    for m in range(maps):
        second = slice(m * cells + half_cells, (m + 1) * cells)
        x_first[second] = dot(turn_half, x_first[second]).astype(BF16)
    first_copies[0].wait()
    for copy in copies(2) + copies(1):
        copy.start()
    first = []
    interleave(teacher(0, x_first, first, first_copies[2]))
    branch = sum(first)
    x_next[...] = (x_first[...].astype(F32) + jnp.transpose(branch)).astype(BF16)
    x_now[...] = jnp.where(layer == 0, x_first[...], x_next[...])
    target[...] = branch
    load(2, True)
    load(1, False)
    for copy in copies(2)[::2] + copies(1):
        copy.wait()
    for pad, buf in ((up_pad, up_buf), (down_pad, down_buf)):
        pad[:, hid // LANES * LANES :] = jnp.zeros((channels, padded - hid // LANES * LANES), BF16)
        pad[:, :hid] = buf[2]
    second, third = [], []
    units = [teacher(1, x_next, second), candidate(x_now, third)]
    interleave([unit for pair in itertools.zip_longest(*units) for unit in pair if unit is not None])
    err = (sum(third) - jnp.where(layer == 0, target[...], sum(second))) * scale
    err_now[...] = jnp.transpose(0.5 * err).astype(BF16)
    err_turned[...] = err.astype(BF16)
    x_turned[...] = jnp.transpose(0.5 * x_now[...].astype(F32)).astype(BF16)

    offset = start - base
    shifts = sorted({p * own - at for p, at in enumerate(bases)})

    def leave(wide, out, n, grad):
        for shift in shifts:
            @pl.when(offset == shift)
            def _():
                out[...] = wide[:, shift : shift + own]
        pltpu.make_async_copy(out, grad.at[0], out_sems.at[n]).start()

    wide_up[...] = dot(err_turned[...], act[...])
    leave(wide_up, out_down, 0, grad_down)

    def back(at, width):
        cols = aligned(base + at, width)
        here = slice(at, at + width)
        grad_act = dot(err_now[...], down_pad[:, cols])
        yield
        grad_k = grad_act.astype(BF16) * slope_k[:, here]
        yield
        tap_re, tap_im = tap_spectrum(2, cols)
        sum_re, sum_im = [], []
        grad_pre = []
        for m in range(maps):
            rows_here = slice(m * cells, (m + 1) * cells)
            both = dot(analysis, grad_k[rows_here])
            yield
            re, im = split(both)
            e_re, e_im = spec[m, 0, :, here], spec[m, 1, :, here]
            sum_re.append(re * e_re + im * e_im)
            sum_im.append(re * e_im - im * e_re)
            mixed_re, mixed_im = re * tap_re + im * tap_im, im * tap_re - re * tap_im
            yield
            grad_e = synthesis(mixed_re, mixed_im)
            yield
            grad_pre.append(grad_e.astype(BF16) * slope_e[rows_here, here])
        yield
        wide_up[:, here] = dot(x_turned[...], jnp.concatenate(grad_pre, axis=0))
        wide_dw[:, here] = dot(gather_re, sum(sum_re[1:], sum_re[0])) + dot(gather_im, sum(sum_im[1:], sum_im[0]))

    interleave([back(at, min(BACK_UNIT, window - at)) for at in range(0, window, BACK_UNIT)])

    leave(wide_up, out_up, 1, grad_up)
    for shift in shifts:
        @pl.when(offset == shift)
        def _():
            own_dw = wide_dw[:taps, shift : shift + own]
            side = int(round(taps**0.5))
            index = lax.broadcasted_iota(jnp.int32, own_dw.shape, 0)
            row = sum((index >= side * n).astype(jnp.int32) for n in range(1, side))
            ring = jnp.maximum(jnp.abs(row - side // 2), jnp.abs(index - side * row - side // 2))
            unit = lax.broadcasted_iota(jnp.int32, own_dw.shape, 1) + start
            keep = (ring <= radius) & (unit < half_units * (hid // 2))
            out_dw[:, 0] = jnp.where(keep, own_dw, 0.0)
    pltpu.make_async_copy(out_dw, grad_dw, out_sems.at[2]).start()
    pltpu.make_async_copy(out_down, grad_down.at[0], out_sems.at[0]).wait()
    pltpu.make_async_copy(out_up, grad_up.at[0], out_sems.at[1]).wait()
    pltpu.make_async_copy(out_dw, grad_dw, out_sems.at[2]).wait()


def local_grads(pieces, offsets, maps, flags, parts, images, weights):
    teach_up, teach_dw, teach_down, cand_up, cand_dw, cand_down = weights
    weights = (teach_up, teach_dw.transpose(1, 0, 2), teach_down, cand_up, cand_dw.transpose(1, 0, 2), cand_down)
    channels, hid = teach_up.shape[1:]
    taps = teach_dw.shape[1]
    count = sum(piece.size for piece in pieces) // channels
    cells = count // maps
    side = int(round(cells**0.5))
    rows, constants = dft_matrices(side, taps)
    padded = round_up(hid, LANES)
    own = hid // parts
    spare = max((p * own) % LANES for p in range(parts))
    window = min(round_up(own + spare, LANES), padded)
    tap_rows = round_up(taps, 16)
    dims = (maps, cells, channels, hid, taps, rows, parts, 1.0 / images)
    vmem = pl.BlockSpec(memory_space=pltpu.VMEM)
    anywhere = pl.BlockSpec(memory_space=pl.ANY)
    grad_up, grad_dw, grad_down = pl.pallas_call(
        functools.partial(grads_kernel, dims, offsets),
        out_shape=(
            jax.ShapeDtypeStruct((1, channels, own), F32),
            jax.ShapeDtypeStruct((taps, 1, own), F32),
            jax.ShapeDtypeStruct((1, channels, own), F32),
        ),
        in_specs=[vmem] + [anywhere] * (len(pieces) + 12),
        out_specs=(anywhere, anywhere, anywhere),
        scratch_shapes=[
            pltpu.VMEM((3, channels, hid), BF16),
            pltpu.VMEM(weights[1].shape, F32),
            pltpu.VMEM(weights[4].shape, F32),
            pltpu.VMEM((3, channels, hid), BF16),
            pltpu.VMEM((3, tap_rows, padded), F32),
            pltpu.VMEM((channels, padded), BF16),
            pltpu.VMEM((channels, padded), BF16),
            pltpu.VMEM((count, window), BF16),
            pltpu.VMEM((maps, 2, rows, window), BF16),
            pltpu.VMEM((count, window), BF16),
            pltpu.VMEM((count, window), BF16),
            pltpu.VMEM((channels, own), F32),
            pltpu.VMEM((taps, 1, own), F32),
            pltpu.VMEM((channels, own), F32),
            pltpu.VMEM((count, channels), BF16),
            pltpu.VMEM((count, channels), BF16),
            pltpu.VMEM((count, channels), BF16),
            pltpu.VMEM((channels, count), BF16),
            pltpu.VMEM((count, channels), BF16),
            pltpu.VMEM((channels, count), BF16),
            pltpu.VMEM((channels, count), F32),
            pltpu.VMEM((channels, window), F32),
            pltpu.VMEM((tap_rows, window), F32),
            pltpu.SemaphoreType.DMA((3, 3)),
            pltpu.SemaphoreType.DMA((len(pieces) + len(constants),)),
            pltpu.SemaphoreType.DMA((3,)),
            *[pltpu.VMEM(array.shape, BF16) for array in (*pieces, *constants)],
        ],
        compiler_params=pltpu.CompilerParams(vmem_limit_bytes=60 * 2**20),
        cost_estimate=pl.CostEstimate(
            flops=20 * count * channels * hid, bytes_accessed=12 * channels * hid, transcendentals=6 * count * hid
        ),
    )(flags, *pieces, *constants, *weights)
    return grad_up, grad_dw.transpose(1, 0, 2), grad_down


def exchange(block, masks, devices, flags):
    offset = [0]
    for mask in masks:
        distances = [d for d in range(1, devices) if d & ~mask == 0]
        parts = [block] + [
            lax.ppermute(block, ("cand", "img"), [(source, source ^ d) for source in range(devices)])
            for d in distances
        ]
        pieces = [[o ^ d for o in offset] for d in [0] + distances]
        offset = sum(pieces, [])
        if mask != masks[-1]:
            block = jnp.concatenate(parts, axis=0)
        if mask == masks[0]:
            block, flags = lax.optimization_barrier((block, flags))
            flags = jnp.concatenate(flags).reshape(1, 3)
        elif mask == masks[1]:
            block, flags = lax.optimization_barrier((block, flags))
    return parts, pieces, flags


def body(
    first_maps,
    layer_of,
    expand_half,
    radius,
    teach_up,
    teach_dw,
    teach_down,
    cand_up,
    cand_dw,
    cand_down,
):
    parts = lax.axis_size("img")
    cands = lax.axis_size("cand")
    devices = parts * cands
    batch, own_cells, channels = first_maps.shape
    images = parts * batch
    weights = (teach_up, teach_dw, teach_down, cand_up, cand_dw, cand_down)
    flags = (layer_of, expand_half, radius)
    scalars = (jnp.concatenate(flags).reshape(1, 3), parts, images, weights)
    if batch == 1 and images == 2 and own_cells % 16 == 0 and devices & (devices - 1) == 0:
        core = parts * (cands > 1)
        near = (parts - 1) | (2 * core)
        masks = [(devices - 1) & ~near & ~core, near, core]
        pieces, offsets, flags = exchange(first_maps.astype(BF16), masks, devices, flags)
        return local_grads(pieces, offsets, images, flags, *scalars[1:])
    whole = lax.all_gather(first_maps.astype(BF16), ("img", "cand")).reshape(parts, cands, batch, own_cells, channels)
    whole = whole.transpose(0, 2, 1, 3, 4).reshape(images, -1, channels)
    group = 2 if images % 2 == 0 else 1
    total = None
    for first in range(0, images, group):
        pieces = [whole[first : first + group].reshape(-1, channels)]
        grads = local_grads(pieces, [None], group, *scalars)
        total = grads if total is None else tuple(a + b for a, b in zip(total, grads))
    return total


def solution(mesh):
    placed = (
        P("img", "cand", None),
        P("cand"),
        P("cand"),
        P("cand"),
        P(),
        P(),
        P(),
        P("cand", None, None),
        P("cand", None, None),
        P("cand", None, None),
    )
    return jax.shard_map(
        body,
        mesh=mesh,
        in_specs=placed,
        out_specs=(P("cand", None, "img"), P("cand", None, "img"), P("cand", None, "img")),
        check_vma=False,
    )
```

```python
import functools
import itertools

import jax
import jax.numpy as jnp
import ml_dtypes
import numpy as np
from jax import lax
from jax.experimental import pallas as pl
from jax.experimental.pallas import tpu as pltpu
from jax.sharding import PartitionSpec as P

F32 = jnp.float32
BF16 = jnp.bfloat16
LANES = 128
UNIT = 1024
BACK_UNIT = 384
DEPTH = 3
STAGGER = 2


def round_up(value, step):
    return -(-value // step) * step


def dft_matrices(side, taps):
    width = int(round(taps**0.5))
    reach = width // 2
    period = side + reach
    kept = []
    for u in range(period):
        for v in range(period):
            if (u, v) <= ((-u) % period, (-v) % period):
                kept.append((u, v))
    freqs = np.array(kept)
    count = len(kept)
    rows = round_up(count, 8)
    mirrored = ((-freqs) % period == freqs).all(axis=1)
    weight = np.where(mirrored, 1.0, 2.0) / period**2
    cell = np.stack(np.meshgrid(np.arange(side), np.arange(side), indexing="ij"), -1).reshape(-1, 2)
    half = len(cell) // 2
    cell = np.concatenate([cell[:half], cell[half:][::-1]]) - (side - 1) / 2
    tap = np.stack(np.meshgrid(np.arange(width), np.arange(width), indexing="ij"), -1).reshape(-1, 2) - reach
    cell_angle = 2 * np.pi * (freqs @ cell.T) / period
    tap_angle = 2 * np.pi * ((freqs @ tap.T) % period) / period
    tap_rows = round_up(taps, 16)

    analysis = np.zeros((2 * rows, side * side))
    analysis[:count] = np.cos(cell_angle)
    analysis[rows : rows + count] = -np.sin(cell_angle)
    even = np.zeros((half, rows))
    even[:, :count] = (weight[:, None] * np.cos(cell_angle)).T[:half]
    odd = np.zeros((half, rows))
    odd[:, :count] = -(weight[:, None] * np.sin(cell_angle)).T[:half]
    spectrum = np.zeros((2 * rows, tap_rows))
    spectrum[:count, :taps] = np.cos(tap_angle)
    spectrum[rows : rows + count, :taps] = np.sin(tap_angle)
    gather_re, gather_im = np.zeros((tap_rows, rows)), np.zeros((tap_rows, rows))
    gather_re[:taps, :count] = (weight[:, None] * np.cos(tap_angle)).T
    gather_im[:taps, :count] = -(weight[:, None] * np.sin(tap_angle)).T

    coarse = spectrum.astype(ml_dtypes.bfloat16).astype(np.float64)
    spectrum = np.concatenate([coarse, coarse, spectrum - coarse], axis=1)
    matrices = (analysis, even, odd, spectrum, gather_re, gather_im)
    return rows, [jnp.asarray(m.astype(ml_dtypes.bfloat16)) for m in matrices]


def dot(a, b):
    return jnp.dot(a, b, preferred_element_type=F32)


def dot_nt(a, b):
    return lax.dot_general(a, b, (((1,), (1,)), ((), ())), preferred_element_type=F32)


def interleave(units):
    waiting, running = list(units), []
    turn = 0
    while waiting or running:
        if waiting and len(running) < DEPTH and turn % STAGGER == 0:
            running.append(waiting.pop(0))
        turn += 1
        for unit in list(running):
            try:
                next(unit)
            except StopIteration:
                running.remove(unit)


def grads_kernel(
    dims,
    offsets,
    *refs,
):
    pieces = len(offsets)
    flags, refs = refs[0], refs[1:]
    layer, half_units, radius = flags[:, 0:1], flags[:, 1:2], flags[:, 2:3]
    count = pieces + 6
    in_hbm, refs, in_vmem = refs[:count], refs[count:-count], refs[-count:]
    x_refs, constants = in_vmem[:pieces], in_vmem[pieces:]
    (
    teach_up,
    teach_dw,
    teach_down,
    cand_up,
    cand_dw,
    cand_down,
    grad_up,
    grad_dw,
    grad_down,
    up_buf,
    dw_buf,
    cand_dw_buf,
    down_buf,
    dw_pad,
    up_pad,
    down_pad,
    act,
    spec,
    slope_e,
    slope_k,
    out_up,
    out_dw,
    out_down,
    x_first,
    x_next,
    x_now,
    x_turned,
    err_now,
    err_turned,
    target,
    wide_up,
    wide_dw,
    sems,
    in_sems,
    out_sems,
    ) = refs
    maps, cells, channels, hid, taps, rows, parts, scale = dims
    padded = round_up(hid, LANES)
    own = hid // parts
    window = wide_up.shape[1]

    def copies(slot):
        if slot < 2:
            sources = (teach_up.at[slot], teach_dw, teach_down.at[slot])
            targets = (up_buf.at[slot], dw_buf, down_buf.at[slot])
        else:
            sources = (cand_up.at[0], cand_dw, cand_down.at[0])
            targets = (up_buf.at[slot], cand_dw_buf, down_buf.at[slot])
        if slot == 1:
            sources, targets = sources[::2], targets[::2]
        return [
            pltpu.make_async_copy(src, dst, sems.at[slot, n])
            for n, (src, dst) in enumerate(zip(sources, targets))
        ]

    staged = [
        pltpu.make_async_copy(src, dst, in_sems.at[n]) for n, (src, dst) in enumerate(zip(in_hbm, in_vmem))
    ]
    first_copies = copies(0)
    for copy in [first_copies[1], *staged, first_copies[0], first_copies[2]]:
        copy.start()

    dw_pad[...] = jnp.zeros_like(dw_pad)

    half_cells = cells // 2
    bases = [min(p * own // LANES * LANES, padded - window) for p in range(parts)]
    part = lax.axis_index("img")
    place = lax.axis_index("cand") * parts + part
    start = part * own
    base = jnp.minimum(start // LANES * LANES, padded - window)

    def split(both):
        return both[:rows].astype(BF16), both[rows:].astype(BF16)

    def synthesis(re, im):
        same, other = dot(even, re), dot(odd, im)
        return jnp.concatenate([same + other, same - other], axis=0)

    def tap_spectrum(slot, cols):
        weights = dw_pad[slot, :, cols]
        high = weights.astype(BF16)
        low = (weights - high.astype(F32)).astype(BF16)
        return split(dot(spectrum, jnp.concatenate([high, low, high], axis=0)))

    def load(slot, mask_taps):
        if slot != 1:
            copies(slot)[1].wait()
        weights = cand_dw_buf[:, 0] if slot == 2 else dw_buf[:, slot]
        if mask_taps:
            side = int(round(taps**0.5))
            index = lax.broadcasted_iota(jnp.int32, weights.shape, 0)
            row = sum((index >= side * n).astype(jnp.int32) for n in range(1, side))
            ring = jnp.maximum(jnp.abs(row - side // 2), jnp.abs(index - side * row - side // 2))
            unit = lax.broadcasted_iota(jnp.int32, weights.shape, 1)
            keep = (ring <= radius) & (unit < half_units * (hid // 2))
            weights = jnp.where(keep, weights, 0.0)
        dw_pad[slot, :taps, :hid] = weights

    def forward(slot, lhs, up, down, cols, save, results, copy=None):
        keep = save is not None
        pre = dot(lhs[...], up[:, cols])
        yield
        half = 0.5 * pre
        bend = jnp.tanh(half)
        more = 1.0 + bend
        wide = half * more
        units = wide.astype(BF16)
        if keep:
            slope_e[:, save] = (more + wide - wide * bend).astype(BF16)
        yield
        tap_re, tap_im = tap_spectrum(slot, cols)
        acts = []
        for m in range(maps):
            here = slice(m * cells, (m + 1) * cells)
            both = dot(analysis, units[here])
            yield
            re, im = split(both)
            if keep:
                spec[m, 0, :, save], spec[m, 1, :, save] = re, im
            mixed_re, mixed_im = re * tap_re - im * tap_im, re * tap_im + im * tap_re
            yield
            mixed = synthesis(mixed_re, mixed_im)
            yield
            half_k = 0.5 * mixed
            bend_k = jnp.tanh(half_k)
            more_k = 1.0 + bend_k
            wide_k = half_k * more_k
            acts.append(wide_k.astype(BF16))
            if keep:
                act[here, save] = acts[-1]
                slope_k[here, save] = (more_k + wide_k - wide_k * bend_k).astype(BF16)
        yield
        if copy is not None:
            copy.wait()
        results.append(dot_nt(down[:, cols], jnp.concatenate(acts, axis=0)))

    def teacher(slot, lhs, results, copy=None):
        bounds = list(range(0, max(hid - UNIT // 2, 1), UNIT)) + [hid]
        return [
            forward(slot, lhs, up_buf.at[slot], down_buf.at[slot], slice(lo, hi), None, results, copy if lo == 0 else None)
            for lo, hi in zip(bounds, bounds[1:])
        ]

    def aligned(at, width):
        return pl.ds(pl.multiple_of(at, LANES), width)

    def candidate(lhs, results):
        units = []
        for at in range(0, window, BACK_UNIT):
            width = min(BACK_UNIT, window - at)
            cols = aligned(base + at, width)
            units.append(forward(2, lhs, up_pad, down_pad, cols, slice(at, at + width), results))
        step = max(w for w in (LANES, 2 * LANES, UNIT) if all(b % w == 0 for b in bases))
        for at in range(0, padded - window, step):
            cols = aligned(jnp.where(at < base, at, at + window), min(step, padded - window - at))
            units.append(forward(2, lhs, up_pad, down_pad, cols, None, results))
        return units

    load(0, False)
    for copy in staged:
        copy.wait()
    analysis, even, odd, spectrum, gather_re, gather_im = (ref[...] for ref in constants)
    whole_turn = (
        lax.broadcasted_iota(jnp.int32, (half_cells, half_cells), 0)
        + lax.broadcasted_iota(jnp.int32, (half_cells, half_cells), 1)
    ) == half_cells - 1
    turn_half = whole_turn.astype(F32).astype(BF16)
    for x_ref, offset in zip(x_refs, offsets):
        if offset is None:
            x_first[...] = x_ref[...]
            continue
        block = x_ref.shape[1]
        for n, distance in enumerate(offset):
            source = place ^ distance
            source = (source & (parts - 1)) * (cells // block) + (source >> (parts.bit_length() - 1))
            at = pl.multiple_of(source * block, block)
            x_first[pl.ds(at, block), :] = x_ref[n]
    for m in range(maps):
        second = slice(m * cells + half_cells, (m + 1) * cells)
        x_first[second] = dot(turn_half, x_first[second]).astype(BF16)
    first_copies[0].wait()
    for copy in copies(2) + copies(1):
        copy.start()
    first = []
    interleave(teacher(0, x_first, first, first_copies[2]))
    branch = sum(first)
    x_next[...] = (x_first[...].astype(F32) + jnp.transpose(branch)).astype(BF16)
    x_now[...] = jnp.where(layer == 0, x_first[...], x_next[...])
    target[...] = branch
    load(2, True)
    load(1, False)
    for copy in copies(2)[::2] + copies(1):
        copy.wait()
    for pad, buf in ((up_pad, up_buf), (down_pad, down_buf)):
        pad[:, hid // LANES * LANES :] = jnp.zeros((channels, padded - hid // LANES * LANES), BF16)
        pad[:, :hid] = buf[2]
    second, third = [], []
    units = [teacher(1, x_next, second), candidate(x_now, third)]
    interleave([unit for pair in itertools.zip_longest(*units) for unit in pair if unit is not None])
    err = (sum(third) - jnp.where(layer == 0, target[...], sum(second))) * scale
    err_now[...] = jnp.transpose(0.5 * err).astype(BF16)
    err_turned[...] = err.astype(BF16)
    x_turned[...] = jnp.transpose(0.5 * x_now[...].astype(F32)).astype(BF16)

    offset = start - base
    shifts = sorted({p * own - at for p, at in enumerate(bases)})

    def leave(wide, out, n, grad):
        for shift in shifts:
            @pl.when(offset == shift)
            def _():
                out[...] = (pltpu.roll(wide[...], window - shift, 1) if shift else wide[...])[:, :own]
        pltpu.make_async_copy(out, grad.at[0], out_sems.at[n]).start()

    wide_up[...] = dot(err_turned[...], act[...])
    leave(wide_up, out_down, 0, grad_down)

    def back(at, width):
        cols = aligned(base + at, width)
        here = slice(at, at + width)
        grad_act = dot(err_now[...], down_pad[:, cols])
        yield
        grad_k = grad_act.astype(BF16) * slope_k[:, here]
        yield
        tap_re, tap_im = tap_spectrum(2, cols)
        sum_re, sum_im = [], []
        grad_pre = []
        for m in range(maps):
            rows_here = slice(m * cells, (m + 1) * cells)
            both = dot(analysis, grad_k[rows_here])
            yield
            re, im = split(both)
            e_re, e_im = spec[m, 0, :, here], spec[m, 1, :, here]
            sum_re.append(re * e_re + im * e_im)
            sum_im.append(re * e_im - im * e_re)
            mixed_re, mixed_im = re * tap_re + im * tap_im, im * tap_re - re * tap_im
            yield
            grad_e = synthesis(mixed_re, mixed_im)
            yield
            grad_pre.append(grad_e.astype(BF16) * slope_e[rows_here, here])
        yield
        wide_up[:, here] = dot(x_turned[...], jnp.concatenate(grad_pre, axis=0))
        wide_dw[:, here] = dot(gather_re, sum(sum_re[1:], sum_re[0])) + dot(gather_im, sum(sum_im[1:], sum_im[0]))

    interleave([back(at, min(BACK_UNIT, window - at)) for at in range(0, window, BACK_UNIT)])

    leave(wide_up, out_up, 1, grad_up)
    for shift in shifts:
        @pl.when(offset == shift)
        def _():
            own_dw = wide_dw[:taps, shift : shift + own]
            side = int(round(taps**0.5))
            index = lax.broadcasted_iota(jnp.int32, own_dw.shape, 0)
            row = sum((index >= side * n).astype(jnp.int32) for n in range(1, side))
            ring = jnp.maximum(jnp.abs(row - side // 2), jnp.abs(index - side * row - side // 2))
            unit = lax.broadcasted_iota(jnp.int32, own_dw.shape, 1) + start
            keep = (ring <= radius) & (unit < half_units * (hid // 2))
            out_dw[:, 0] = jnp.where(keep, own_dw, 0.0)
    pltpu.make_async_copy(out_dw, grad_dw, out_sems.at[2]).start()
    pltpu.make_async_copy(out_down, grad_down.at[0], out_sems.at[0]).wait()
    pltpu.make_async_copy(out_up, grad_up.at[0], out_sems.at[1]).wait()
    pltpu.make_async_copy(out_dw, grad_dw, out_sems.at[2]).wait()


def local_grads(pieces, offsets, maps, flags, parts, images, weights):
    teach_up, teach_dw, teach_down, cand_up, cand_dw, cand_down = weights
    weights = (teach_up, teach_dw.transpose(1, 0, 2), teach_down, cand_up, cand_dw.transpose(1, 0, 2), cand_down)
    channels, hid = teach_up.shape[1:]
    taps = teach_dw.shape[1]
    count = sum(piece.size for piece in pieces) // channels
    cells = count // maps
    side = int(round(cells**0.5))
    rows, constants = dft_matrices(side, taps)
    padded = round_up(hid, LANES)
    own = hid // parts
    spare = max((p * own) % LANES for p in range(parts))
    window = min(round_up(own + spare, LANES), padded)
    tap_rows = round_up(taps, 16)
    dims = (maps, cells, channels, hid, taps, rows, parts, 1.0 / images)
    vmem = pl.BlockSpec(memory_space=pltpu.VMEM)
    anywhere = pl.BlockSpec(memory_space=pl.ANY)
    grad_up, grad_dw, grad_down = pl.pallas_call(
        functools.partial(grads_kernel, dims, offsets),
        out_shape=(
            jax.ShapeDtypeStruct((1, channels, own), F32),
            jax.ShapeDtypeStruct((taps, 1, own), F32),
            jax.ShapeDtypeStruct((1, channels, own), F32),
        ),
        in_specs=[vmem] + [anywhere] * (len(pieces) + 12),
        out_specs=(anywhere, anywhere, anywhere),
        scratch_shapes=[
            pltpu.VMEM((3, channels, hid), BF16),
            pltpu.VMEM(weights[1].shape, F32),
            pltpu.VMEM(weights[4].shape, F32),
            pltpu.VMEM((3, channels, hid), BF16),
            pltpu.VMEM((3, tap_rows, padded), F32),
            pltpu.VMEM((channels, padded), BF16),
            pltpu.VMEM((channels, padded), BF16),
            pltpu.VMEM((count, window), BF16),
            pltpu.VMEM((maps, 2, rows, window), BF16),
            pltpu.VMEM((count, window), BF16),
            pltpu.VMEM((count, window), BF16),
            pltpu.VMEM((channels, own), F32),
            pltpu.VMEM((taps, 1, own), F32),
            pltpu.VMEM((channels, own), F32),
            pltpu.VMEM((count, channels), BF16),
            pltpu.VMEM((count, channels), BF16),
            pltpu.VMEM((count, channels), BF16),
            pltpu.VMEM((channels, count), BF16),
            pltpu.VMEM((count, channels), BF16),
            pltpu.VMEM((channels, count), BF16),
            pltpu.VMEM((channels, count), F32),
            pltpu.VMEM((channels, window), F32),
            pltpu.VMEM((tap_rows, window), F32),
            pltpu.SemaphoreType.DMA((3, 3)),
            pltpu.SemaphoreType.DMA((len(pieces) + len(constants),)),
            pltpu.SemaphoreType.DMA((3,)),
            *[pltpu.VMEM(array.shape, BF16) for array in (*pieces, *constants)],
        ],
        compiler_params=pltpu.CompilerParams(vmem_limit_bytes=60 * 2**20),
        cost_estimate=pl.CostEstimate(
            flops=20 * count * channels * hid, bytes_accessed=12 * channels * hid, transcendentals=6 * count * hid
        ),
    )(flags, *pieces, *constants, *weights)
    return grad_up, grad_dw.transpose(1, 0, 2), grad_down


def exchange(block, masks, devices, flags):
    offset = [0]
    for mask in masks:
        distances = [d for d in range(1, devices) if d & ~mask == 0]
        parts = [block] + [
            lax.ppermute(block, ("cand", "img"), [(source, source ^ d) for source in range(devices)])
            for d in distances
        ]
        pieces = [[o ^ d for o in offset] for d in [0] + distances]
        offset = sum(pieces, [])
        if mask != masks[-1]:
            block = jnp.concatenate(parts, axis=0)
        if mask == masks[0]:
            block, flags = lax.optimization_barrier((block, flags))
            flags = jnp.concatenate(flags).reshape(1, 3)
        elif mask == masks[1]:
            block, flags = lax.optimization_barrier((block, flags))
    return parts, pieces, flags


def body(
    first_maps,
    layer_of,
    expand_half,
    radius,
    teach_up,
    teach_dw,
    teach_down,
    cand_up,
    cand_dw,
    cand_down,
):
    parts = lax.axis_size("img")
    cands = lax.axis_size("cand")
    devices = parts * cands
    batch, own_cells, channels = first_maps.shape
    images = parts * batch
    weights = (teach_up, teach_dw, teach_down, cand_up, cand_dw, cand_down)
    flags = (layer_of, expand_half, radius)
    scalars = (jnp.concatenate(flags).reshape(1, 3), parts, images, weights)
    if batch == 1 and images == 2 and own_cells % 16 == 0 and devices & (devices - 1) == 0:
        core = parts * (cands > 1)
        near = (parts - 1) | (2 * core)
        masks = [(devices - 1) & ~near & ~core, near, core]
        pieces, offsets, flags = exchange(first_maps.astype(BF16), masks, devices, flags)
        return local_grads(pieces, offsets, images, flags, *scalars[1:])
    whole = lax.all_gather(first_maps.astype(BF16), ("img", "cand")).reshape(parts, cands, batch, own_cells, channels)
    whole = whole.transpose(0, 2, 1, 3, 4).reshape(images, -1, channels)
    group = 2 if images % 2 == 0 else 1
    total = None
    for first in range(0, images, group):
        pieces = [whole[first : first + group].reshape(-1, channels)]
        grads = local_grads(pieces, [None], group, *scalars)
        total = grads if total is None else tuple(a + b for a, b in zip(total, grads))
    return total


def solution(mesh):
    placed = (
        P("img", "cand", None),
        P("cand"),
        P("cand"),
        P("cand"),
        P(),
        P(),
        P(),
        P("cand", None, None),
        P("cand", None, None),
        P("cand", None, None),
    )
    return jax.shard_map(
        body,
        mesh=mesh,
        in_specs=placed,
        out_specs=(P("cand", None, "img"), P("cand", None, "img"), P("cand", None, "img")),
        check_vma=False,
    )
```

```python
import functools
import itertools

import jax
import jax.numpy as jnp
import ml_dtypes
import numpy as np
from jax import lax
from jax.experimental import pallas as pl
from jax.experimental.pallas import tpu as pltpu
from jax.sharding import PartitionSpec as P

F32 = jnp.float32
BF16 = jnp.bfloat16
LANES = 128
UNIT = 1024
BACK_UNIT = 1152
DEPTH = 3
STAGGER = 2


def round_up(value, step):
    return -(-value // step) * step


def dft_matrices(side, taps):
    width = int(round(taps**0.5))
    reach = width // 2
    period = side + reach
    kept = []
    for u in range(period):
        for v in range(period):
            if (u, v) <= ((-u) % period, (-v) % period):
                kept.append((u, v))
    freqs = np.array(kept)
    count = len(kept)
    rows = round_up(count, 8)
    mirrored = ((-freqs) % period == freqs).all(axis=1)
    weight = np.where(mirrored, 1.0, 2.0) / period**2
    cell = np.stack(np.meshgrid(np.arange(side), np.arange(side), indexing="ij"), -1).reshape(-1, 2)
    half = len(cell) // 2
    cell = np.concatenate([cell[:half], cell[half:][::-1]]) - (side - 1) / 2
    tap = np.stack(np.meshgrid(np.arange(width), np.arange(width), indexing="ij"), -1).reshape(-1, 2) - reach
    cell_angle = 2 * np.pi * (freqs @ cell.T) / period
    tap_angle = 2 * np.pi * ((freqs @ tap.T) % period) / period
    tap_rows = round_up(taps, 16)

    analysis = np.zeros((2 * rows, side * side))
    analysis[:count] = np.cos(cell_angle)
    analysis[rows : rows + count] = -np.sin(cell_angle)
    even = np.zeros((half, rows))
    even[:, :count] = (weight[:, None] * np.cos(cell_angle)).T[:half]
    odd = np.zeros((half, rows))
    odd[:, :count] = -(weight[:, None] * np.sin(cell_angle)).T[:half]
    spectrum = np.zeros((2 * rows, tap_rows))
    spectrum[:count, :taps] = np.cos(tap_angle)
    spectrum[rows : rows + count, :taps] = np.sin(tap_angle)
    gather_re, gather_im = np.zeros((tap_rows, rows)), np.zeros((tap_rows, rows))
    gather_re[:taps, :count] = (weight[:, None] * np.cos(tap_angle)).T
    gather_im[:taps, :count] = -(weight[:, None] * np.sin(tap_angle)).T

    coarse = spectrum.astype(ml_dtypes.bfloat16).astype(np.float64)
    spectrum = np.concatenate([coarse, coarse, spectrum - coarse], axis=1)
    matrices = (analysis, even, odd, spectrum, gather_re, gather_im)
    return rows, [jnp.asarray(m.astype(ml_dtypes.bfloat16)) for m in matrices]


def dot(a, b):
    return jnp.dot(a, b, preferred_element_type=F32)


def dot_nt(a, b):
    return lax.dot_general(a, b, (((1,), (1,)), ((), ())), preferred_element_type=F32)


def interleave(units):
    waiting, running = list(units), []
    turn = 0
    while waiting or running:
        if waiting and len(running) < DEPTH and turn % STAGGER == 0:
            running.append(waiting.pop(0))
        turn += 1
        for unit in list(running):
            try:
                next(unit)
            except StopIteration:
                running.remove(unit)


def grads_kernel(
    dims,
    offsets,
    *refs,
):
    pieces = len(offsets)
    flags, refs = refs[0], refs[1:]
    layer, half_units, radius = flags[:, 0:1], flags[:, 1:2], flags[:, 2:3]
    count = pieces + 6
    in_hbm, refs, in_vmem = refs[:count], refs[count:-count], refs[-count:]
    x_refs, constants = in_vmem[:pieces], in_vmem[pieces:]
    (
    teach_up,
    teach_dw,
    teach_down,
    cand_up,
    cand_dw,
    cand_down,
    grad_up,
    grad_dw,
    grad_down,
    up_buf,
    dw_buf,
    cand_dw_buf,
    down_buf,
    dw_pad,
    up_pad,
    down_pad,
    act,
    spec,
    slope_e,
    slope_k,
    out_up,
    out_dw,
    out_down,
    x_first,
    x_next,
    x_now,
    x_turned,
    err_now,
    err_turned,
    target,
    wide_up,
    wide_dw,
    sems,
    in_sems,
    out_sems,
    ) = refs
    maps, cells, channels, hid, taps, rows, parts, scale = dims
    padded = round_up(hid, LANES)
    own = hid // parts
    window = wide_up.shape[1]

    def copies(slot):
        if slot < 2:
            sources = (teach_up.at[slot], teach_dw, teach_down.at[slot])
            targets = (up_buf.at[slot], dw_buf, down_buf.at[slot])
        else:
            sources = (cand_up.at[0], cand_dw, cand_down.at[0])
            targets = (up_buf.at[slot], cand_dw_buf, down_buf.at[slot])
        if slot == 1:
            sources, targets = sources[::2], targets[::2]
        return [
            pltpu.make_async_copy(src, dst, sems.at[slot, n])
            for n, (src, dst) in enumerate(zip(sources, targets))
        ]

    staged = [
        pltpu.make_async_copy(src, dst, in_sems.at[n]) for n, (src, dst) in enumerate(zip(in_hbm, in_vmem))
    ]
    first_copies = copies(0)
    for copy in [first_copies[1], *staged, first_copies[0], first_copies[2]]:
        copy.start()

    dw_pad[...] = jnp.zeros_like(dw_pad)

    half_cells = cells // 2
    bases = [min(p * own // LANES * LANES, padded - window) for p in range(parts)]
    part = lax.axis_index("img")
    place = lax.axis_index("cand") * parts + part
    start = part * own
    base = jnp.minimum(start // LANES * LANES, padded - window)

    def split(both):
        return both[:rows].astype(BF16), both[rows:].astype(BF16)

    def synthesis(re, im):
        same, other = dot(even, re), dot(odd, im)
        return jnp.concatenate([same + other, same - other], axis=0)

    def tap_spectrum(slot, cols):
        weights = dw_pad[slot, :, cols]
        high = weights.astype(BF16)
        low = (weights - high.astype(F32)).astype(BF16)
        return split(dot(spectrum, jnp.concatenate([high, low, high], axis=0)))

    def load(slot, mask_taps):
        if slot != 1:
            copies(slot)[1].wait()
        weights = cand_dw_buf[:, 0] if slot == 2 else dw_buf[:, slot]
        if mask_taps:
            side = int(round(taps**0.5))
            index = lax.broadcasted_iota(jnp.int32, weights.shape, 0)
            row = sum((index >= side * n).astype(jnp.int32) for n in range(1, side))
            ring = jnp.maximum(jnp.abs(row - side // 2), jnp.abs(index - side * row - side // 2))
            unit = lax.broadcasted_iota(jnp.int32, weights.shape, 1)
            keep = (ring <= radius) & (unit < half_units * (hid // 2))
            weights = jnp.where(keep, weights, 0.0)
        dw_pad[slot, :taps, :hid] = weights

    def forward(slot, lhs, up, down, cols, save, results, copy=None):
        keep = save is not None
        pre = dot(lhs[...], up[:, cols])
        yield
        half = 0.5 * pre
        bend = jnp.tanh(half)
        more = 1.0 + bend
        wide = half * more
        units = wide.astype(BF16)
        if keep:
            slope_e[:, save] = (more + wide - wide * bend).astype(BF16)
        yield
        tap_re, tap_im = tap_spectrum(slot, cols)
        acts = []
        for m in range(maps):
            here = slice(m * cells, (m + 1) * cells)
            both = dot(analysis, units[here])
            yield
            re, im = split(both)
            if keep:
                spec[m, 0, :, save], spec[m, 1, :, save] = re, im
            mixed_re, mixed_im = re * tap_re - im * tap_im, re * tap_im + im * tap_re
            yield
            mixed = synthesis(mixed_re, mixed_im)
            yield
            half_k = 0.5 * mixed
            bend_k = jnp.tanh(half_k)
            more_k = 1.0 + bend_k
            wide_k = half_k * more_k
            acts.append(wide_k.astype(BF16))
            if keep:
                act[here, save] = acts[-1]
                slope_k[here, save] = (more_k + wide_k - wide_k * bend_k).astype(BF16)
        yield
        if copy is not None:
            copy.wait()
        results.append(dot_nt(down[:, cols], jnp.concatenate(acts, axis=0)))

    def teacher(slot, lhs, results, copy=None):
        bounds = list(range(0, max(hid - UNIT // 2, 1), UNIT)) + [hid]
        return [
            forward(slot, lhs, up_buf.at[slot], down_buf.at[slot], slice(lo, hi), None, results, copy if lo == 0 else None)
            for lo, hi in zip(bounds, bounds[1:])
        ]

    def aligned(at, width):
        return pl.ds(pl.multiple_of(at, LANES), width)

    def candidate(lhs, results):
        units = []
        for at in range(0, window, BACK_UNIT):
            width = min(BACK_UNIT, window - at)
            cols = aligned(base + at, width)
            units.append(forward(2, lhs, up_pad, down_pad, cols, slice(at, at + width), results))
        step = max(w for w in (LANES, 2 * LANES, UNIT) if all(b % w == 0 for b in bases))
        for at in range(0, padded - window, step):
            cols = aligned(jnp.where(at < base, at, at + window), min(step, padded - window - at))
            units.append(forward(2, lhs, up_pad, down_pad, cols, None, results))
        return units

    load(0, False)
    for copy in staged:
        copy.wait()
    analysis, even, odd, spectrum, gather_re, gather_im = (ref[...] for ref in constants)
    whole_turn = (
        lax.broadcasted_iota(jnp.int32, (half_cells, half_cells), 0)
        + lax.broadcasted_iota(jnp.int32, (half_cells, half_cells), 1)
    ) == half_cells - 1
    turn_half = whole_turn.astype(F32).astype(BF16)
    for x_ref, offset in zip(x_refs, offsets):
        if offset is None:
            x_first[...] = x_ref[...]
            continue
        block = x_ref.shape[1]
        for n, distance in enumerate(offset):
            source = place ^ distance
            source = (source & (parts - 1)) * (cells // block) + (source >> (parts.bit_length() - 1))
            at = pl.multiple_of(source * block, block)
            x_first[pl.ds(at, block), :] = x_ref[n]
    for m in range(maps):
        second = slice(m * cells + half_cells, (m + 1) * cells)
        x_first[second] = dot(turn_half, x_first[second]).astype(BF16)
    first_copies[0].wait()
    for copy in copies(2) + copies(1):
        copy.start()
    first = []
    interleave(teacher(0, x_first, first, first_copies[2]))
    branch = sum(first)
    x_next[...] = (x_first[...].astype(F32) + jnp.transpose(branch)).astype(BF16)
    x_now[...] = jnp.where(layer == 0, x_first[...], x_next[...])
    target[...] = branch
    load(2, True)
    load(1, False)
    for copy in copies(2)[::2] + copies(1):
        copy.wait()
    for pad, buf in ((up_pad, up_buf), (down_pad, down_buf)):
        pad[:, hid // LANES * LANES :] = jnp.zeros((channels, padded - hid // LANES * LANES), BF16)
        pad[:, :hid] = buf[2]
    second, third = [], []
    units = [teacher(1, x_next, second), candidate(x_now, third)]
    interleave([unit for pair in itertools.zip_longest(*units) for unit in pair if unit is not None])
    err = (sum(third) - jnp.where(layer == 0, target[...], sum(second))) * scale
    err_now[...] = jnp.transpose(0.5 * err).astype(BF16)
    err_turned[...] = err.astype(BF16)
    x_turned[...] = jnp.transpose(0.5 * x_now[...].astype(F32)).astype(BF16)

    offset = start - base
    shifts = sorted({p * own - at for p, at in enumerate(bases)})

    def leave(wide, out, n, grad):
        for shift in shifts:
            @pl.when(offset == shift)
            def _():
                out[...] = wide[:, shift : shift + own]
        pltpu.make_async_copy(out, grad.at[0], out_sems.at[n]).start()

    wide_up[...] = dot(err_turned[...], act[...])
    leave(wide_up, out_down, 0, grad_down)

    def back(at, width):
        cols = aligned(base + at, width)
        here = slice(at, at + width)
        grad_act = dot(err_now[...], down_pad[:, cols])
        yield
        grad_k = grad_act.astype(BF16) * slope_k[:, here]
        yield
        tap_re, tap_im = tap_spectrum(2, cols)
        sum_re, sum_im = [], []
        grad_pre = []
        for m in range(maps):
            rows_here = slice(m * cells, (m + 1) * cells)
            both = dot(analysis, grad_k[rows_here])
            yield
            re, im = split(both)
            e_re, e_im = spec[m, 0, :, here], spec[m, 1, :, here]
            sum_re.append(re * e_re + im * e_im)
            sum_im.append(re * e_im - im * e_re)
            mixed_re, mixed_im = re * tap_re + im * tap_im, im * tap_re - re * tap_im
            yield
            grad_e = synthesis(mixed_re, mixed_im)
            yield
            grad_pre.append(grad_e.astype(BF16) * slope_e[rows_here, here])
        yield
        wide_up[:, here] = dot(x_turned[...], jnp.concatenate(grad_pre, axis=0))
        wide_dw[:, here] = dot(gather_re, sum(sum_re[1:], sum_re[0])) + dot(gather_im, sum(sum_im[1:], sum_im[0]))

    interleave([back(at, min(BACK_UNIT, window - at)) for at in range(0, window, BACK_UNIT)])

    leave(wide_up, out_up, 1, grad_up)
    for shift in shifts:
        @pl.when(offset == shift)
        def _():
            own_dw = wide_dw[:taps, shift : shift + own]
            side = int(round(taps**0.5))
            index = lax.broadcasted_iota(jnp.int32, own_dw.shape, 0)
            row = sum((index >= side * n).astype(jnp.int32) for n in range(1, side))
            ring = jnp.maximum(jnp.abs(row - side // 2), jnp.abs(index - side * row - side // 2))
            unit = lax.broadcasted_iota(jnp.int32, own_dw.shape, 1) + start
            keep = (ring <= radius) & (unit < half_units * (hid // 2))
            out_dw[:, 0] = jnp.where(keep, own_dw, 0.0)
    pltpu.make_async_copy(out_dw, grad_dw, out_sems.at[2]).start()
    pltpu.make_async_copy(out_down, grad_down.at[0], out_sems.at[0]).wait()
    pltpu.make_async_copy(out_up, grad_up.at[0], out_sems.at[1]).wait()
    pltpu.make_async_copy(out_dw, grad_dw, out_sems.at[2]).wait()


def local_grads(pieces, offsets, maps, flags, parts, images, weights):
    teach_up, teach_dw, teach_down, cand_up, cand_dw, cand_down = weights
    weights = (teach_up, teach_dw.transpose(1, 0, 2), teach_down, cand_up, cand_dw.transpose(1, 0, 2), cand_down)
    channels, hid = teach_up.shape[1:]
    taps = teach_dw.shape[1]
    count = sum(piece.size for piece in pieces) // channels
    cells = count // maps
    side = int(round(cells**0.5))
    rows, constants = dft_matrices(side, taps)
    padded = round_up(hid, LANES)
    own = hid // parts
    spare = max((p * own) % LANES for p in range(parts))
    window = min(round_up(own + spare, LANES), padded)
    tap_rows = round_up(taps, 16)
    dims = (maps, cells, channels, hid, taps, rows, parts, 1.0 / images)
    vmem = pl.BlockSpec(memory_space=pltpu.VMEM)
    anywhere = pl.BlockSpec(memory_space=pl.ANY)
    grad_up, grad_dw, grad_down = pl.pallas_call(
        functools.partial(grads_kernel, dims, offsets),
        out_shape=(
            jax.ShapeDtypeStruct((1, channels, own), F32),
            jax.ShapeDtypeStruct((taps, 1, own), F32),
            jax.ShapeDtypeStruct((1, channels, own), F32),
        ),
        in_specs=[vmem] + [anywhere] * (len(pieces) + 12),
        out_specs=(anywhere, anywhere, anywhere),
        scratch_shapes=[
            pltpu.VMEM((3, channels, hid), BF16),
            pltpu.VMEM(weights[1].shape, F32),
            pltpu.VMEM(weights[4].shape, F32),
            pltpu.VMEM((3, channels, hid), BF16),
            pltpu.VMEM((3, tap_rows, padded), F32),
            pltpu.VMEM((channels, padded), BF16),
            pltpu.VMEM((channels, padded), BF16),
            pltpu.VMEM((count, window), BF16),
            pltpu.VMEM((maps, 2, rows, window), BF16),
            pltpu.VMEM((count, window), BF16),
            pltpu.VMEM((count, window), BF16),
            pltpu.VMEM((channels, own), F32),
            pltpu.VMEM((taps, 1, own), F32),
            pltpu.VMEM((channels, own), F32),
            pltpu.VMEM((count, channels), BF16),
            pltpu.VMEM((count, channels), BF16),
            pltpu.VMEM((count, channels), BF16),
            pltpu.VMEM((channels, count), BF16),
            pltpu.VMEM((count, channels), BF16),
            pltpu.VMEM((channels, count), BF16),
            pltpu.VMEM((channels, count), F32),
            pltpu.VMEM((channels, window), F32),
            pltpu.VMEM((tap_rows, window), F32),
            pltpu.SemaphoreType.DMA((3, 3)),
            pltpu.SemaphoreType.DMA((len(pieces) + len(constants),)),
            pltpu.SemaphoreType.DMA((3,)),
            *[pltpu.VMEM(array.shape, BF16) for array in (*pieces, *constants)],
        ],
        compiler_params=pltpu.CompilerParams(vmem_limit_bytes=60 * 2**20),
        cost_estimate=pl.CostEstimate(
            flops=20 * count * channels * hid, bytes_accessed=12 * channels * hid, transcendentals=6 * count * hid
        ),
    )(flags, *pieces, *constants, *weights)
    return grad_up, grad_dw.transpose(1, 0, 2), grad_down


def exchange(block, masks, devices, flags):
    offset = [0]
    for mask in masks:
        distances = [d for d in range(1, devices) if d & ~mask == 0]
        parts = [block] + [
            lax.ppermute(block, ("cand", "img"), [(source, source ^ d) for source in range(devices)])
            for d in distances
        ]
        pieces = [[o ^ d for o in offset] for d in [0] + distances]
        offset = sum(pieces, [])
        if mask != masks[-1]:
            block = jnp.concatenate(parts, axis=0)
        if mask == masks[0]:
            block, flags = lax.optimization_barrier((block, flags))
            flags = jnp.concatenate(flags).reshape(1, 3)
        elif mask == masks[1]:
            block, flags = lax.optimization_barrier((block, flags))
    return parts, pieces, flags


def body(
    first_maps,
    layer_of,
    expand_half,
    radius,
    teach_up,
    teach_dw,
    teach_down,
    cand_up,
    cand_dw,
    cand_down,
):
    parts = lax.axis_size("img")
    cands = lax.axis_size("cand")
    devices = parts * cands
    batch, own_cells, channels = first_maps.shape
    images = parts * batch
    weights = (teach_up, teach_dw, teach_down, cand_up, cand_dw, cand_down)
    flags = (layer_of, expand_half, radius)
    scalars = (jnp.concatenate(flags).reshape(1, 3), parts, images, weights)
    if batch == 1 and images == 2 and own_cells % 16 == 0 and devices & (devices - 1) == 0:
        core = parts * (cands > 1)
        near = (parts - 1) | (2 * core)
        masks = [(devices - 1) & ~near & ~core, near, core]
        pieces, offsets, flags = exchange(first_maps.astype(BF16), masks, devices, flags)
        return local_grads(pieces, offsets, images, flags, *scalars[1:])
    whole = lax.all_gather(first_maps.astype(BF16), ("img", "cand")).reshape(parts, cands, batch, own_cells, channels)
    whole = whole.transpose(0, 2, 1, 3, 4).reshape(images, -1, channels)
    group = 2 if images % 2 == 0 else 1
    total = None
    for first in range(0, images, group):
        pieces = [whole[first : first + group].reshape(-1, channels)]
        grads = local_grads(pieces, [None], group, *scalars)
        total = grads if total is None else tuple(a + b for a, b in zip(total, grads))
    return total


def solution(mesh):
    placed = (
        P("img", "cand", None),
        P("cand"),
        P("cand"),
        P("cand"),
        P(),
        P(),
        P(),
        P("cand", None, None),
        P("cand", None, None),
        P("cand", None, None),
    )
    return jax.shard_map(
        body,
        mesh=mesh,
        in_specs=placed,
        out_specs=(P("cand", None, "img"), P("cand", None, "img"), P("cand", None, "img")),
        check_vma=False,
    )
```
